32 devices in a mesh: dp: 4 (over y, core), seq: 8 (over z, x).
Axes of the slice: x: 2, y: 2, z: 4, core: 2. Of those that a mesh axis runs over, the one named last changes fastest.
Arguments:
- stream_in: float32 [4, 1024, 1536], P('dp', 'seq'), may hold values from -6 to 6
- doc_starts: int32 [4, 4], P('dp'), may hold values from 0 to 1023, as said below
- norm_mix: float32 [2, 1536], P(None, ('dp', 'seq')), may hold values from 0.5 to 1.5
- in_proj: float32 [2, 1536, 4608], P(None, ('dp', 'seq')), may hold values from -0.15625 to 0.15625
- conv_taps: float32 [2, 1536, 3], P(None, ('dp', 'seq')), may hold values from -3.5 to 3.5
- out_proj: float32 [2, 1536, 1536], P(None, ('dp', 'seq')), may hold values from -0.15625 to 0.15625
- norm_ffn: float32 [2, 1536], P(None, ('dp', 'seq')), may hold values from 0.5 to 1.5
- w_gate: float32 [2, 1536, 4608], P(None, ('dp', 'seq')), may hold values from -0.15625 to 0.15625
- w_up: float32 [2, 1536, 4608], P(None, ('dp', 'seq')), may hold values from -0.15625 to 0.15625
- w_down: float32 [2, 4608, 1536], P(None, ('dp', 'seq')), may hold values from -0.125 to 0.125
- grad_out: float32 [4, 1024, 1536], P('dp', 'seq'), may hold values from -6 to 6
Outputs:
- stream_out: float32 [4, 1024, 1536], P('dp', 'seq')
- grad_in: float32 [4, 1024, 1536], P('dp', 'seq')
- grad_norm_mix: float32 [2, 1536], P(None, ('dp', 'seq'))
- grad_in_proj: float32 [2, 1536, 4608], P(None, ('dp', 'seq'))
- grad_conv_taps: float32 [2, 1536, 3], P(None, ('dp', 'seq'))
- grad_out_proj: float32 [2, 1536, 1536], P(None, ('dp', 'seq'))
- grad_norm_ffn: float32 [2, 1536], P(None, ('dp', 'seq'))
- grad_gate: float32 [2, 1536, 4608], P(None, ('dp', 'seq'))
- grad_up: float32 [2, 1536, 4608], P(None, ('dp', 'seq'))
- grad_down: float32 [2, 4608, 1536], P(None, ('dp', 'seq'))
The draws below stay inside these ranges and needn't reach their ends.
Inputs may be any that keep to these rules, and one draw needn't show every extreme that they name: `doc_starts`: in each row the starts rise strictly and the first is 0; every other start lies in positions 1 to 63 or in the last 64 positions of the row.
All inputs are finite; a program needn't handle non-finite values.
Results may differ from the reference program's by a relative error of at most 0.017.
The reference program's roundings to bfloat16 on the way count: a program that leaves them out, or rounds other values in their place, can miss the bound.
Values may be sent and summed in bfloat16 or wider, within the bound.
A program may use at most 704 MiB of HBM per device.

```python
import jax
import jax.numpy as jnp
from jax import lax

D = 1536
FF = 4608
LAYERS = 2
NDOC = 4
TOK_DEV = 128
ROWS = 4
LENGTH = 1024


def draw_doc_starts(key, part):
    key = jax.random.fold_in(key, 11)
    half_dev = TOK_DEV // 2

    def one_row(row_key):
        first_key, second_key, third_key = jax.random.split(row_key, 3)
        early = jnp.sort(jax.random.permutation(first_key, half_dev - 1)[:NDOC - 1] + 1)
        late = jnp.sort(jax.random.permutation(second_key, half_dev)[:NDOC - 1] + (LENGTH - half_dev))
        chosen = jax.random.randint(third_key, (), 0, NDOC)
        counter = jnp.arange(NDOC, dtype=jnp.int32)
        from_early = early[jnp.clip(counter - 1, 0, NDOC - 2)]
        from_late = late[jnp.clip(counter - chosen - 1, 0, NDOC - 2)]
        picked = jnp.where(counter <= chosen, from_early, from_late)
        return jnp.where(counter == 0, 0, picked).astype(jnp.int32)
    return jax.vmap(one_row)(jax.random.split(key, ROWS))


def strengthened(drawn, stream_key, source, target, parts, factor):
    owner, partner = [(jnp.arange(drawn.shape[axis_at]) // (drawn.shape[axis_at] // parts)).reshape([-1 if axis == axis_at else 1 for axis in range(drawn.ndim)]) for axis_at in (source, target)]
    chosen = jax.random.permutation(stream_key, parts)[partner]
    strong = (owner == chosen) | (owner == (partner + parts // 2) % parts)
    return jnp.where(strong, factor * drawn, drawn)


def block_levels(rng, dims, cuts, smallest, largest):
    gain = 1.0
    for position, blocks in cuts:
        heights = jax.random.uniform(jax.random.fold_in(jax.random.fold_in(rng, 6), position), (blocks,), jnp.float32, smallest / len(cuts), largest / len(cuts))
        gain = gain * jnp.repeat(jnp.exp(heights), dims[position] // blocks).reshape((-1,) + (1,) * (len(dims) - 1 - position))
    return gain


def gaussian(own_key, shape, scale, limit, cuts=(), kind=jnp.bfloat16):
    values = jax.random.normal(own_key, shape, jnp.float32) * scale
    if len(cuts) > 0:
        values = block_levels(own_key, shape, cuts, -0.22, 0.18) * values
    return jnp.clip(values, min=-limit, max=limit).astype(kind)


def noise_with(stream_key, dims, scale, limit, cuts, heavy, held_as=jnp.bfloat16):
    drawn = scale * jax.random.normal(stream_key, dims, jnp.float32)
    if cuts:
        drawn = drawn * block_levels(stream_key, dims, cuts, -0.22, 0.18)
    return jnp.clip(strengthened(drawn, jax.random.fold_in(stream_key, 3), *heavy), -limit, limit).astype(held_as)


def setup_inputs(seed: int = 0) -> dict:
    key_of = jax.random.split(jax.random.key(seed), 12)
    stream_in = noise_with(key_of[0], (ROWS, LENGTH, D), 1.0, 6.0, ((0, 4), (1, 8)), (1, 2, 8, 2.0), jnp.float32)
    doc_starts = draw_doc_starts(jax.random.fold_in(key_of[11], 71), 0)
    norm_mix = jnp.clip(1.0 + 0.1 * jax.random.normal(key_of[2], (LAYERS, D), jnp.float32), 0.5, 1.5)
    in_proj = gaussian(key_of[3], (LAYERS, D, 3 * D), D ** -0.5, 0.15625, ((1, 32),), jnp.float32)
    conv_taps = gaussian(key_of[4], (LAYERS, D, 3), 3 ** -0.5, 3.5, ((1, 32),), jnp.float32)
    out_proj = gaussian(key_of[5], (LAYERS, D, D), D ** -0.5, 0.15625, ((1, 32),), jnp.float32)
    norm_ffn = jnp.clip(1.0 + 0.1 * jax.random.normal(key_of[6], (LAYERS, D), jnp.float32), 0.5, 1.5)
    w_gate = gaussian(key_of[7], (LAYERS, D, FF), D ** -0.5, 0.15625, ((1, 32),), jnp.float32)
    w_up = gaussian(key_of[8], (LAYERS, D, FF), D ** -0.5, 0.15625, ((1, 32),), jnp.float32)
    w_down = gaussian(key_of[9], (LAYERS, FF, D), (FF // 2) ** -0.5, 0.125, ((1, 32),), jnp.float32)
    grad_out = gaussian(key_of[10], (ROWS, LENGTH, D), 1.0, 6.0, ((0, 4), (1, 8)), jnp.float32)
    return {"stream_in": stream_in, "doc_starts": doc_starts, "norm_mix": norm_mix, "in_proj": in_proj, "conv_taps": conv_taps, "out_proj": out_proj, "norm_ffn": norm_ffn, "w_gate": w_gate, "w_up": w_up, "w_down": w_down, "grad_out": grad_out}


@jax.custom_vjp
def low(v):
    return lax.optimization_barrier(v.astype(jnp.bfloat16)).astype(jnp.float32)

@jax.custom_vjp
def low_back(v):
    return v

def low_keep(v):
    return (low(v), None)

def low_pass(kept, grad):
    return (grad,)

def back_keep(v):
    return (v, None)

def back_low(kept, grad):
    return (low(grad),)
low.defvjp(low_keep, low_pass)
low_back.defvjp(back_keep, back_low)
EPSILON = 1e-05

def product(left, right):
    return jnp.dot(left, right, precision=lax.Precision.HIGHEST, preferred_element_type=jnp.float32)

def rms_scale(values):
    return lax.rsqrt(lax.optimization_barrier(jnp.mean(values * values, axis=-1, keepdims=True)) + EPSILON)

def segment_of(starts, places):
    return lax.optimization_barrier(jnp.sum((starts[None, :] <= places[:, None]).astype(jnp.int32), axis=1))

def tap_masks(starts, length):
    places = jnp.arange(length, dtype=jnp.int32)
    own_segment = segment_of(starts, places)
    keep_one = (segment_of(starts, places - 1) == own_segment).astype(jnp.float32)
    keep_two = (segment_of(starts, places - 2) == own_segment).astype(jnp.float32)
    return (keep_one[:, None], keep_two[:, None])

def block_forward(stream, weight_set, keep_one, keep_two):
    gain_mix, in_weight, conv_weight, out_weight, gain_ffn, gate_weight, up_weight, down_weight = weight_set
    length = stream.shape[0]
    features = stream.shape[1]
    normed = low(stream * rms_scale(stream) * gain_mix)
    joint = low_back(product(normed, in_weight))
    b_part = joint[:, :features]
    c_part = joint[:, features:2 * features]
    x_part = joint[:, 2 * features:]
    carried = b_part * x_part
    padded = jnp.concatenate([jnp.zeros((2, features), jnp.float32), carried], axis=0)
    mixed = conv_weight[:, 0] * padded[:length] * keep_two + conv_weight[:, 1] * padded[1:length + 1] * keep_one + conv_weight[:, 2] * carried
    gated = low(c_part * mixed)
    middle = stream + low_back(product(gated, out_weight))
    normed_ffn = low(middle * rms_scale(middle) * gain_ffn)
    gate_value = low_back(product(normed_ffn, gate_weight))
    up_value = low_back(product(normed_ffn, up_weight))
    hidden = low(jax.nn.silu(gate_value) * up_value)
    return middle + low_back(product(hidden, down_weight))

def forward(stream, starts, weights):
    keep_one, keep_two = tap_masks(starts, stream.shape[0])
    for layer_index in range(LAYERS):
        weight_set = tuple((low(weight[layer_index]) for weight in weights))
        stream = block_forward(stream, weight_set, keep_one, keep_two)
    return stream

def reference(stream_in, doc_starts, norm_mix, in_proj, conv_taps, out_proj, norm_ffn, w_gate, w_up, w_down, grad_out):
    weights = (norm_mix, in_proj, conv_taps, out_proj, norm_ffn, w_gate, w_up, w_down)
    zero_totals = tuple((jnp.zeros_like(weight) for weight in weights))

    def per_row(totals, row_items):
        source, starts, cotangent = row_items

        def apply_blocks(stream_value, weight_values):
            return forward(stream_value, starts, weight_values)
        result, pull_back = jax.vjp(apply_blocks, source, weights)
        grad_source, grad_weights = pull_back(cotangent)
        new_totals = tuple((total + grad for total, grad in zip(totals, grad_weights)))
        return (new_totals, (result, grad_source))
    totals, (outputs, grads_input) = lax.scan(per_row, zero_totals, (stream_in, doc_starts, grad_out))
    return (outputs, grads_input, totals[0], totals[1], totals[2], totals[3], totals[4], totals[5], totals[6], totals[7])
```

```python
import jax
import jax.numpy as jnp
from jax import lax
from jax.sharding import Mesh, PartitionSpec as P

EPSILON = 1e-05
TP = ("yl", "core", "xl")
DP = ("yh", "z", "xh")
ROW_AXES = ("yh", "yl", "core")
SEQ_AXES = ("z", "xh", "xl")
OWNERS = ROW_AXES + SEQ_AXES
BF16 = jnp.bfloat16
F32 = jnp.float32


def rms_scale(values):
    return lax.rsqrt(jnp.mean(values * values, axis=-1, keepdims=True) + EPSILON)


def matmul(left, right):
    return jnp.dot(left, right, preferred_element_type=F32)


def inner_rows(left, right):
    return lax.dot_general(left, right, (((0,), (0,)), ((), ())), preferred_element_type=F32)


def outer_cols(left, right):
    return lax.dot_general(left, right, (((1,), (1,)), ((), ())), preferred_element_type=F32)


def sizes_of(axes):
    return tuple(lax.axis_size(axis) for axis in axes)


def split_owners(array, dim):
    owners = sizes_of(OWNERS)
    count = 1
    for size in owners:
        count *= size
    shape = array.shape
    return array.reshape(shape[:dim] + owners + (shape[dim] // count,) + shape[dim + 1 :])


def column_shards(weight, groups):
    rows = weight.shape[0]
    parts = split_owners(weight.reshape(rows, groups, -1), 2)
    parts = parts.transpose(3, 4, 7, 0, 1, 2, 5, 6, 8)
    return parts.reshape(8, rows, -1)


def column_whole(shards, groups):
    rows = shards.shape[1]
    yh, yl, core, z, xh, xl = sizes_of(OWNERS)
    parts = shards.reshape(yl, core, xl, rows, groups, yh, z, xh, -1)
    return parts.transpose(3, 4, 5, 0, 1, 6, 7, 2, 8).reshape(rows, -1)


def gather_columns(shards):
    mine = lax.all_to_all(shards, TP, split_axis=0, concat_axis=0, tiled=True)
    whole = lax.all_gather(mine, DP, axis=0, tiled=False)
    yh, yl, core, z, xh, xl = sizes_of(OWNERS)
    rows, columns = shards.shape[1:]
    whole = whole.reshape(yh, z, xh, yl, core, xl, rows, columns)
    return whole.transpose(0, 3, 4, 1, 2, 5, 6, 7).reshape(-1, columns)


def scatter_columns(total):
    yh, yl, core, z, xh, xl = sizes_of(OWNERS)
    columns = total.shape[1]
    parts = split_owners(total, 0).transpose(0, 3, 4, 1, 2, 5, 6, 7)
    parts = parts.reshape(yh * z * xh, -1, columns)
    mine = lax.psum_scatter(parts, DP, scatter_dimension=0, tiled=False)
    mine = mine.reshape(8, -1, columns)
    return lax.all_to_all(mine, TP, split_axis=0, concat_axis=0, tiled=True)


def gather_tokens(array):
    return lax.all_gather(array, TP, axis=0, tiled=True)


def scatter_tokens(partial):
    return lax.psum_scatter(partial, TP, scatter_dimension=0, tiled=True)


def beside(array, by):
    axes = ("z", "xh")
    count = lax.axis_size("z") * lax.axis_size("xh")
    pairs = [(i, i + by) for i in range(count) if 0 <= i + by < count]
    return lax.ppermute(array, axes, pairs)


def tap_masks(starts, position_count):
    group = lax.axis_index("z") * lax.axis_size("xh") + lax.axis_index("xh")
    places = group * position_count + jnp.arange(position_count, dtype=jnp.int32)

    def segment_of(where):
        return jnp.sum((starts[:, None, :] <= where[None, :, None]).astype(jnp.int32), axis=2)

    own_segment = segment_of(places)
    keep_one = (segment_of(places - 1) == own_segment).astype(F32)[:, :, None]
    keep_two = (segment_of(places - 2) == own_segment).astype(F32)[:, :, None]
    return keep_one, keep_two


def conv_forward(joint, taps, keep_one, keep_two):
    rows, positions, _ = joint.shape
    b_part, c_part, x_part = jnp.split(joint, 3, axis=2)
    carried = b_part * x_part
    previous = beside(carried[:, positions - 2 :], 1)
    padded = jnp.concatenate([previous, carried], axis=1)
    mixed = (
        taps[:, 0] * padded[:, :positions] * keep_two
        + taps[:, 1] * padded[:, 1 : positions + 1] * keep_one
        + taps[:, 2] * carried
    )
    return (c_part * mixed).astype(BF16), mixed, padded


def conv_backward(grad_gated, joint, mixed, padded, taps, keep_one, keep_two):
    rows, positions, width = grad_gated.shape
    b_part, c_part, x_part = jnp.split(joint, 3, axis=2)
    grad_c = grad_gated * mixed
    grad_mixed = grad_gated * c_part
    first_tap = grad_mixed * keep_two
    second_tap = grad_mixed * keep_one
    grad_taps = jnp.stack(
        [
            jnp.sum(first_tap * padded[:, :positions], axis=(0, 1)),
            jnp.sum(second_tap * padded[:, 1 : positions + 1], axis=(0, 1)),
            jnp.sum(grad_mixed * padded[:, 2:], axis=(0, 1)),
        ],
        axis=0,
    )
    one = jnp.zeros((rows, 1, width), F32)
    two = jnp.zeros((rows, 2, width), F32)
    grad_padded = jnp.concatenate([first_tap * taps[:, 0], two], axis=1) + jnp.concatenate(
        [one, second_tap * taps[:, 1], one], axis=1
    )
    returned = beside(grad_padded[:, :2], -1)
    arriving = jnp.concatenate([jnp.zeros((rows, positions - 2, width), F32), returned], axis=1)
    grad_carried = grad_padded[:, 2:] + grad_mixed * taps[:, 2] + arriving
    grad_joint = jnp.concatenate([grad_carried * x_part, grad_c, grad_carried * b_part], axis=2)
    return grad_joint.astype(BF16), grad_taps


def local(stream_in, doc_starts, norm_mix, in_proj, conv_taps, out_proj, norm_ffn, w_gate, w_up, w_down, grad_out):
    batch_rows, token_count, features = stream_in.shape
    layers = norm_mix.shape[0]
    rows, positions = 4 * batch_rows, 2 * token_count
    tokens = rows * positions
    starts = lax.all_gather(doc_starts, ("yl", "core"), axis=0, tiled=True)
    keep_one, keep_two = tap_masks(starts, positions)

    def by_row(array):
        return array.reshape(4, 2, batch_rows, token_count, -1).transpose(0, 2, 1, 3, 4).reshape(rows, positions, -1)

    def by_device(array):
        return array.reshape(4, batch_rows, 2, token_count, -1).transpose(0, 2, 1, 3, 4).reshape(tokens, -1)

    small = jnp.concatenate(
        [norm_mix[:, :, None], norm_ffn[:, :, None], conv_taps], axis=2
    ).astype(BF16)
    gains = lax.all_gather(small[:, :, :2], OWNERS, axis=1, tiled=True).astype(F32)
    taps_all = lax.all_gather(small[:, :, 2:], DP, axis=1, tiled=True).astype(F32)
    weights = []
    for layer in range(layers):
        in_w = gather_columns(column_shards(in_proj[layer].astype(BF16), 3))
        out_w = lax.all_gather(out_proj[layer].astype(BF16), DP, axis=0, tiled=True)
        both = jnp.concatenate(
            [column_shards(w_gate[layer].astype(BF16), 1), column_shards(w_up[layer].astype(BF16), 1)], axis=2
        )
        both_w = gather_columns(both)
        down_w = lax.all_gather(w_down[layer].astype(BF16), DP, axis=0, tiled=True)
        weights.append((gains[layer, :, 0], in_w, taps_all[layer], out_w, gains[layer, :, 1], both_w, down_w))

    stream = stream_in.reshape(-1, features)
    saved = []
    for layer in range(layers):
        gain_mix, in_w, taps, out_w, gain_ffn, both_w, down_w = weights[layer]
        width = down_w.shape[0]
        scale_mix = rms_scale(stream)
        normed = gather_tokens((stream * scale_mix * gain_mix).astype(BF16))
        joint = by_row(matmul(normed, in_w))
        gated, mixed, padded = conv_forward(joint, taps, keep_one, keep_two)
        gated = by_device(gated)
        middle = stream + scatter_tokens(matmul(gated, out_w))
        scale_ffn = rms_scale(middle)
        normed_ffn = gather_tokens((middle * scale_ffn * gain_ffn).astype(BF16))
        gate_up = matmul(normed_ffn, both_w)
        gate, up = gate_up[:, :width], gate_up[:, width:]
        hidden = (jax.nn.silu(gate) * up).astype(BF16)
        result = middle + scatter_tokens(matmul(hidden, down_w))
        saved.append((stream, scale_mix, normed, joint, mixed, padded, gated, middle, scale_ffn, normed_ffn, gate, up, hidden))
        stream = result
    grad_stream = grad_out.reshape(-1, features)
    pieces = [None] * layers
    for layer in reversed(range(layers)):
        gain_mix, in_w, taps, out_w, gain_ffn, both_w, down_w = weights[layer]
        source, scale_mix, normed, joint, mixed, padded, gated, middle, scale_ffn, normed_ffn, gate, up, hidden = saved[layer]
        down_in = gather_tokens(grad_stream.astype(BF16))
        grad_down = lax.psum_scatter(inner_rows(hidden, down_in), DP, scatter_dimension=0, tiled=True)
        grad_hidden = outer_cols(down_in, down_w)
        sigmoid = jax.nn.sigmoid(gate)
        grad_gate_up = jnp.concatenate(
            [grad_hidden * up * sigmoid * (1.0 + gate * (1.0 - sigmoid)), grad_hidden * gate * sigmoid], axis=1
        ).astype(BF16)
        grad_both = scatter_columns(inner_rows(normed_ffn, grad_gate_up))
        width = down_w.shape[0]
        grad_gate = column_whole(grad_both[:, :, :width], 1)
        grad_up = column_whole(grad_both[:, :, width:], 1)
        grad_normed_ffn = scatter_tokens(outer_cols(grad_gate_up, both_w))
        grad_gain_ffn = jnp.sum(grad_normed_ffn * middle * scale_ffn, axis=0)
        scaled = grad_normed_ffn * gain_ffn
        grad_middle = grad_stream + scale_ffn * scaled - middle * scale_ffn**3 * jnp.mean(scaled * middle, axis=-1, keepdims=True)
        mix_in = gather_tokens(grad_middle.astype(BF16))
        grad_out_w = lax.psum_scatter(inner_rows(gated, mix_in), DP, scatter_dimension=0, tiled=True)
        grad_gated = by_row(outer_cols(mix_in, out_w))
        grad_joint, grad_taps = conv_backward(grad_gated, joint, mixed, padded, taps, keep_one, keep_two)
        grad_joint = by_device(grad_joint)
        grad_in_w = column_whole(scatter_columns(inner_rows(normed, grad_joint)), 3)
        grad_normed = scatter_tokens(outer_cols(grad_joint, in_w))
        grad_gain_mix = jnp.sum(grad_normed * source * scale_mix, axis=0)
        scaled = grad_normed * gain_mix
        grad_stream = grad_middle + scale_mix * scaled - source * scale_mix**3 * jnp.mean(scaled * source, axis=-1, keepdims=True)
        pieces[layer] = (grad_gain_mix, grad_in_w, grad_taps, grad_out_w, grad_gain_ffn, grad_gate, grad_up, grad_down)
    gain_grads = jnp.stack([jnp.stack([p[0], p[4]]) for p in pieces])
    gain_grads = lax.psum_scatter(gain_grads, OWNERS, scatter_dimension=2, tiled=True)
    tap_grads = lax.psum_scatter(jnp.stack([p[2] for p in pieces]), DP, scatter_dimension=2, tiled=True)
    return (
        stream.reshape(batch_rows, token_count, features),
        grad_stream.reshape(batch_rows, token_count, features),
        gain_grads[:, 0],
        jnp.stack([p[1] for p in pieces]),
        tap_grads.transpose(0, 2, 1),
        jnp.stack([p[3] for p in pieces]),
        gain_grads[:, 1],
        jnp.stack([p[5] for p in pieces]),
        jnp.stack([p[6] for p in pieces]),
        jnp.stack([p[7] for p in pieces]),
    )


def solution(mesh):
    dp, seq = mesh.shape["dp"], mesh.shape["seq"]
    side = dp // 2
    split = Mesh(mesh.devices.reshape(side // 2, 2, 2, seq // side, side // 2, 2), OWNERS)
    token = P(ROW_AXES, SEQ_AXES, None)
    vector = P(None, OWNERS)
    matrix = P(None, OWNERS, None)
    return jax.shard_map(
        local,
        mesh=split,
        in_specs=(token, P(ROW_AXES, None), vector, matrix, matrix, matrix, vector, matrix, matrix, matrix, token),
        out_specs=(token, token, vector, matrix, matrix, matrix, vector, matrix, matrix, matrix),
        check_vma=False,
    )
```

```python
import functools

import jax
import jax.numpy as jnp
from jax import lax
from jax.experimental import pallas as pl
from jax.experimental.pallas import tpu as pltpu
from jax.sharding import Mesh, PartitionSpec as P

EPSILON = 1e-05
TP = ("zl", "yl", "core")
DP = ("yh", "zh", "x")
ROW_AXES = ("yh", "yl", "core")
SEQ_AXES = ("zh", "zl", "x")
OWNERS = ROW_AXES + SEQ_AXES
BF16 = jnp.bfloat16
F32 = jnp.float32
MESH = pl.DeviceIdType.MESH
HALVES = 2
IN_NAMES = {
    "first": ("stream", "gain"),
    "fwd": ("partial", "stream", "gain"),
    "turn": ("partial", "stream", "grad"),
    "bwd": ("partial", "grad", "stream", "gain"),
    "last": ("partial", "grad", "stream", "gain"),
}
OUT_NAMES = {
    "first": ("whole",),
    "fwd": ("stream_next", "whole"),
    "turn": ("stream_next", "whole"),
    "bwd": ("grad_next", "gain_grad", "whole"),
    "last": ("grad_next", "gain_grad"),
}
COLLECTIVE_ID = {"first": 0, "fwd": 1, "turn": 2, "bwd": 3, "last": 4}


def rms_scale(values):
    return lax.rsqrt(jnp.mean(values * values, axis=-1, keepdims=True) + EPSILON)


def exchange_kernel(kind, *refs):
    names = IN_NAMES[kind] + OUT_NAMES[kind]
    ref = dict(zip(names, refs))
    refs = refs[len(names) :]
    near, sib, yin, yout, zin, zout, mine, local_sem, sums_send, sums_recv, all_send, all_recv = refs
    zl, yl, core = (lax.axis_index(axis) for axis in TP)
    tokens = mine.shape[0]
    half = tokens // HALVES
    to_sibling, to_y, to_z = {"core": 1 - core}, {"yl": 1 - yl}, {"zl": 1 - zl}

    def rank(flip_z, flip_y, flip_core):
        return (1 - zl if flip_z else zl) * 4 + (1 - yl if flip_y else yl) * 2 + (1 - core if flip_core else core)

    def part(h):
        return pl.ds(h * half, half)

    reduces, gathers = kind != "first", kind != "last"
    chips = ((1, 1), (0, 1), (1, 0), (0, 0))
    if reduces:
        near_copies = [
            pltpu.make_async_copy(ref["partial"].at[rank(*chip, 0)], near.at[i], local_sem.at[i])
            for i, chip in enumerate(chips)
        ]
        for copy in near_copies:
            copy.start()
    if kind == "first":
        stream = ref["stream"][...]
        mine[...] = (stream * rms_scale(stream) * ref["gain"][...]).astype(BF16)
    if kind == "turn":
        mine[...] = ref["grad"][...].astype(BF16)

    barrier = pltpu.get_barrier_semaphore()
    for partner in (to_sibling, to_y, to_z):
        pl.semaphore_signal(barrier, inc=1, device_id=partner, device_id_type=MESH)
    pl.semaphore_wait(barrier, 3)

    def sums_copy(index, src, dst, device):
        return pltpu.make_async_remote_copy(
            src_ref=src, dst_ref=dst, send_sem=sums_send.at[index], recv_sem=sums_recv.at[index],
            device_id=device, device_id_type=MESH,
        )

    def gather_copy(index, src, dst, device):
        return pltpu.make_async_remote_copy(
            src_ref=src, dst_ref=dst, send_sem=all_send.at[index], recv_sem=all_recv.at[index],
            device_id=device, device_id_type=MESH,
        )

    waits = []
    own_places = []
    from_z, from_y, from_corner, to_core = [], [], [], []
    if gathers:
        whole = ref["whole"]
        n = HALVES
        own, beside_z, beside_y, corner = (rank(*chip, 0) for chip in ((0, 0), (1, 0), (0, 1), (1, 1)))
        for h in range(HALVES):
            rows = part(h)
            own_places.append(pltpu.make_async_copy(mine.at[rows], whole.at[own, rows], local_sem.at[4 + h]))
            to_core.append(gather_copy(h, mine.at[rows], whole.at[own, rows], to_sibling))
            from_z.append(gather_copy(n + h, mine.at[rows], whole.at[own, rows], to_z))
            from_y.append(gather_copy(2 * n + h, mine.at[rows], whole.at[own, rows], to_y))
        for h in range(HALVES):
            rows = part(h)
            from_corner.append(
                gather_copy(3 * n + h, whole.at[beside_z, rows], whole.at[beside_z, rows], to_y)
            )
        for i, place in enumerate((beside_z, beside_y, corner)):
            for h in range(HALVES):
                rows = part(h)
                to_core.append(gather_copy((4 + i) * n + h, whole.at[place, rows], whole.at[place, rows], to_sibling))

    def send_mine(h):
        from_z[h].start()
        from_y[h].start()
        to_core[h].start()
        own_places[h].start()

    if kind in ("first", "turn"):
        for h in range(HALVES):
            send_mine(h)

    if reduces:
        sib_copies = [
            sums_copy(i, ref["partial"].at[rank(*chip, 1)], sib.at[i], to_sibling) for i, chip in enumerate(chips)
        ]
        for copy in sib_copies:
            copy.start()
        y_copies = [
            [sums_copy(4 + i * HALVES + h, yout.at[i, part(h)], yin.at[i, part(h)], to_y) for h in range(HALVES)]
            for i in range(2)
        ]
        z_copies = [
            sums_copy(4 + 2 * HALVES + h, zout.at[part(h)], zin.at[part(h)], to_z) for h in range(HALVES)
        ]

        def chip_sum(i, h):
            return near[i, part(h)].astype(F32) + sib[i, part(h)].astype(F32)

        for i in range(2):
            near_copies[i].wait()
            sib_copies[i].wait_recv()
            for h in range(HALVES):
                yout[i, part(h)] = chip_sum(i, h).astype(BF16)
                y_copies[i][h].start()
        near_copies[2].wait()
        sib_copies[2].wait_recv()
        for h in range(HALVES):
            y_copies[0][h].wait_recv()
            zout[part(h)] = (chip_sum(2, h) + yin[0, part(h)].astype(F32)).astype(BF16)
            z_copies[h].start()
        near_copies[3].wait()
        sib_copies[3].wait_recv()
        for h in range(HALVES):
            rows = part(h)
            y_copies[1][h].wait_recv()
            z_copies[h].wait_recv()
            total = chip_sum(3, h) + yin[1, rows].astype(F32) + zin[rows].astype(F32)
            stream = ref["stream"][rows]
            if kind in ("fwd", "turn"):
                stream = stream + total
                ref["stream_next"][rows] = stream
            if kind == "fwd":
                mine[rows] = (stream * rms_scale(stream) * ref["gain"][...]).astype(BF16)
                send_mine(h)
            if kind in ("bwd", "last"):
                scale = rms_scale(stream)
                gain_grad = jnp.sum(total * stream * scale, axis=0, keepdims=True)
                ref["gain_grad"][...] = gain_grad if h == 0 else ref["gain_grad"][...] + gain_grad
                scaled = total * ref["gain"][...]
                grad = (
                    ref["grad"][rows]
                    + scale * scaled
                    - stream * (scale * scale * scale) * jnp.mean(scaled * stream, axis=-1, keepdims=True)
                )
                ref["grad_next"][rows] = grad
                if kind == "bwd":
                    mine[rows] = grad.astype(BF16)
                    send_mine(h)
        waits += sib_copies + y_copies[0] + y_copies[1] + z_copies

    if gathers:
        n = HALVES
        for h in range(HALVES):
            from_z[h].wait_recv()
            from_corner[h].start()
            to_core[n + h].start()
        for h in range(HALVES):
            from_y[h].wait_recv()
            to_core[2 * n + h].start()
        for h in range(HALVES):
            from_corner[h].wait_recv()
            to_core[3 * n + h].start()
        for copy in to_core:
            copy.wait_recv()
        waits += from_z + from_y + from_corner + to_core
        for copy in own_places:
            copy.wait()
    for copy in waits:
        copy.wait_send()


def exchange(kind, *operands):
    tokens, features = operands[-2 if kind in ("first", "fwd", "turn") else 1].shape
    shapes = {
        "whole": jax.ShapeDtypeStruct((8, tokens, features), BF16),
        "stream_next": jax.ShapeDtypeStruct((tokens, features), F32),
        "grad_next": jax.ShapeDtypeStruct((tokens, features), F32),
        "gain_grad": jax.ShapeDtypeStruct((1, features), F32),
    }
    anywhere = pl.BlockSpec(memory_space=pl.ANY)
    inside = pl.BlockSpec(memory_space=pltpu.VMEM)
    block = (tokens, features)
    return pl.pallas_call(
        functools.partial(exchange_kernel, kind),
        out_shape=tuple(shapes[name] for name in OUT_NAMES[kind]),
        in_specs=[anywhere if name == "partial" else inside for name in IN_NAMES[kind]],
        out_specs=tuple(anywhere if name == "whole" else inside for name in OUT_NAMES[kind]),
        scratch_shapes=[
            pltpu.VMEM((4,) + block, BF16),
            pltpu.VMEM((4,) + block, BF16),
            pltpu.VMEM((2,) + block, BF16),
            pltpu.VMEM((2,) + block, BF16),
            pltpu.VMEM(block, BF16),
            pltpu.VMEM(block, BF16),
            pltpu.VMEM(block, BF16),
            pltpu.SemaphoreType.DMA((4 + HALVES,)),
            pltpu.SemaphoreType.DMA((4 + 3 * HALVES,)),
            pltpu.SemaphoreType.DMA((4 + 3 * HALVES,)),
            pltpu.SemaphoreType.DMA((7 * HALVES,)),
            pltpu.SemaphoreType.DMA((7 * HALVES,)),
        ],
        compiler_params=pltpu.CompilerParams(
            collective_id=COLLECTIVE_ID[kind], has_side_effects=True, vmem_limit_bytes=40 << 20
        ),
        cost_estimate=pl.CostEstimate(flops=10**7, bytes_accessed=150 * 10**6, transcendentals=0),
        name="exchange_" + kind,
    )(*operands)


def matmul(left, right):
    return jnp.dot(left, right, preferred_element_type=F32)


def inner_rows(left, right):
    return lax.dot_general(left, right, (((0,), (0,)), ((), ())), preferred_element_type=F32)


def outer_cols(left, right):
    return lax.dot_general(left, right, (((1,), (1,)), ((), ())), preferred_element_type=F32)


def sizes_of(axes):
    return tuple(lax.axis_size(axis) for axis in axes)


def split_owners(array, dim):
    owners = sizes_of(OWNERS)
    count = 1
    for size in owners:
        count *= size
    shape = array.shape
    return array.reshape(shape[:dim] + owners + (shape[dim] // count,) + shape[dim + 1 :])


def column_shards(weight, groups):
    rows = weight.shape[0]
    parts = split_owners(weight.reshape(rows, groups, -1), 2)
    return parts.transpose(6, 3, 4, 0, 1, 2, 5, 7, 8).reshape(8, rows, -1)


def column_whole(shards, groups):
    rows = shards.shape[1]
    yh, yl, core, zh, zl, x = sizes_of(OWNERS)
    parts = shards.reshape(zl, yl, core, rows, groups, yh, zh, x, -1)
    return parts.transpose(3, 4, 5, 1, 2, 6, 0, 7, 8).reshape(rows, -1)


def gather_columns(shards):
    mine = lax.all_to_all(shards, TP, split_axis=0, concat_axis=0, tiled=True)
    whole = lax.all_gather(mine, DP, axis=0, tiled=False)
    yh, yl, core, zh, zl, x = sizes_of(OWNERS)
    rows, columns = shards.shape[1:]
    whole = whole.reshape(yh, zh, x, zl, yl, core, rows, columns)
    return whole.transpose(0, 4, 5, 1, 3, 2, 6, 7).reshape(-1, columns)


def scatter_columns(total):
    yh, yl, core, zh, zl, x = sizes_of(OWNERS)
    columns = total.shape[1]
    parts = split_owners(total, 0).transpose(0, 3, 5, 4, 1, 2, 6, 7)
    parts = parts.reshape(yh * zh * x, -1, columns)
    mine = lax.psum_scatter(parts, DP, scatter_dimension=0, tiled=False)
    mine = mine.reshape(8, -1, columns)
    return lax.all_to_all(mine, TP, split_axis=0, concat_axis=0, tiled=True)


def tails_before(tails):
    x_size, zh_size = lax.axis_size("x"), lax.axis_size("zh")
    tails = tails.reshape((2, 4) + tails.shape[1:])
    beside = lax.ppermute(tails, "x", [(i, (i + 1) % x_size) for i in range(x_size)])
    pairs = [(i * x_size + x_size - 1, (i + 1) * x_size) for i in range(zh_size - 1)]
    below = lax.ppermute(tails[1], ("zh", "x"), pairs)
    first = jnp.stack([below, beside[0]])
    return jnp.where(lax.axis_index("x") == 0, first, beside).reshape((8,) + tails.shape[2:])


def heads_after(heads):
    x_size, zh_size = lax.axis_size("x"), lax.axis_size("zh")
    heads = heads.reshape((2, 4) + heads.shape[1:])
    beside = lax.ppermute(heads, "x", [((i + 1) % x_size, i) for i in range(x_size)])
    pairs = [((i + 1) * x_size, i * x_size + x_size - 1) for i in range(zh_size - 1)]
    above = lax.ppermute(heads[0], ("zh", "x"), pairs)
    final = jnp.stack([beside[1], above])
    return jnp.where(lax.axis_index("x") == x_size - 1, final, beside).reshape((8,) + heads.shape[2:])


def tap_masks(starts, token_count):
    zh, x, x_size = lax.axis_index("zh"), lax.axis_index("x"), lax.axis_size("x")
    blocks = (zh * 2 + jnp.arange(2, dtype=jnp.int32)) * x_size + x
    places = blocks[:, None] * token_count + jnp.arange(token_count, dtype=jnp.int32)

    def segment_of(where):
        return jnp.sum((starts[None, :, None, :] <= where[:, None, :, None]).astype(jnp.int32), axis=3)

    own_segment = segment_of(places)
    keep_one = (segment_of(places - 1) == own_segment).astype(F32)
    keep_two = (segment_of(places - 2) == own_segment).astype(F32)
    return keep_one.reshape(8, token_count, 1), keep_two.reshape(8, token_count, 1)


def conv_forward(joint, taps, keep_one, keep_two):
    positions = joint.shape[1]
    b_part, c_part, x_part = jnp.split(joint, 3, axis=2)
    carried = b_part * x_part
    previous = tails_before(carried[:, positions - 2 :])
    padded = jnp.concatenate([previous, carried], axis=1)
    mixed = (
        taps[:, 0] * padded[:, :positions] * keep_two
        + taps[:, 1] * padded[:, 1 : positions + 1] * keep_one
        + taps[:, 2] * carried
    )
    return (c_part * mixed).astype(BF16), mixed, padded


def conv_backward(grad_gated, joint, mixed, padded, taps, keep_one, keep_two):
    rows, positions, width = grad_gated.shape
    b_part, c_part, x_part = jnp.split(joint, 3, axis=2)
    grad_c = grad_gated * mixed
    grad_mixed = grad_gated * c_part
    first_tap = grad_mixed * keep_two
    second_tap = grad_mixed * keep_one
    grad_taps = jnp.stack(
        [
            jnp.sum(first_tap * padded[:, :positions], axis=(0, 1)),
            jnp.sum(second_tap * padded[:, 1 : positions + 1], axis=(0, 1)),
            jnp.sum(grad_mixed * padded[:, 2:], axis=(0, 1)),
        ],
        axis=0,
    )
    one = jnp.zeros((rows, 1, width), F32)
    two = jnp.zeros((rows, 2, width), F32)
    grad_padded = jnp.concatenate([first_tap * taps[:, 0], two], axis=1) + jnp.concatenate(
        [one, second_tap * taps[:, 1], one], axis=1
    )
    returned = heads_after(grad_padded[:, :2])
    arriving = jnp.concatenate([jnp.zeros((rows, positions - 2, width), F32), returned], axis=1)
    grad_carried = grad_padded[:, 2:] + grad_mixed * taps[:, 2] + arriving
    grad_joint = jnp.concatenate([grad_carried * x_part, grad_c, grad_carried * b_part], axis=2)
    return grad_joint.astype(BF16), grad_taps


def local(stream_in, doc_starts, norm_mix, in_proj, conv_taps, out_proj, norm_ffn, w_gate, w_up, w_down, grad_out):
    _, token_count, features = stream_in.shape
    layers = norm_mix.shape[0]
    starts = lax.all_gather(doc_starts, ("yl", "core"), axis=0, tiled=True)
    keep_one, keep_two = tap_masks(starts, token_count)

    def blocks(array):
        return array.reshape(8, token_count, -1)

    def flat(array):
        return array.reshape(8 * token_count, -1)

    small = jnp.concatenate([norm_mix[:, :, None], norm_ffn[:, :, None], conv_taps], axis=2).astype(BF16)
    gains = lax.all_gather(small[:, :, :2], OWNERS, axis=1, tiled=True).astype(F32)
    gains = gains.transpose(0, 2, 1).reshape(layers, 2, 1, features)
    taps_all = lax.all_gather(small[:, :, 2:], DP, axis=1, tiled=True).astype(F32)
    weights = []
    for layer in range(layers):
        in_w = gather_columns(column_shards(in_proj[layer].astype(BF16), 3))
        out_w = lax.all_gather(out_proj[layer].astype(BF16), DP, axis=0, tiled=True)
        both = jnp.concatenate(
            [column_shards(w_gate[layer].astype(BF16), 1), column_shards(w_up[layer].astype(BF16), 1)], axis=2
        )
        both_w = gather_columns(both)
        down_w = lax.all_gather(w_down[layer].astype(BF16), DP, axis=0, tiled=True)
        weights.append((in_w, taps_all[layer], out_w, both_w, down_w))

    stream = stream_in.reshape(-1, features)
    grad_stream = grad_out.reshape(-1, features)
    saved = []
    (normed,) = exchange("first", stream, gains[0, 0])
    for layer in range(layers):
        in_w, taps, out_w, both_w, down_w = weights[layer]
        width = down_w.shape[0]
        normed = flat(normed)
        joint = blocks(matmul(normed, in_w))
        gated, mixed, padded = conv_forward(joint, taps, keep_one, keep_two)
        gated = flat(gated)
        middle, normed_ffn = exchange("fwd", blocks(matmul(gated, out_w).astype(BF16)), stream, gains[layer, 1])
        normed_ffn = flat(normed_ffn)
        gate_up = matmul(normed_ffn, both_w)
        gate, up = gate_up[:, :width], gate_up[:, width:]
        hidden = (jax.nn.silu(gate) * up).astype(BF16)
        saved.append((stream, normed, joint, mixed, padded, gated, middle, normed_ffn, gate, up, hidden))
        partial = blocks(matmul(hidden, down_w).astype(BF16))
        if layer + 1 < layers:
            stream, normed = exchange("fwd", partial, middle, gains[layer + 1, 0])
        else:
            stream, down_in = exchange("turn", partial, middle, grad_stream)
    pieces = [None] * layers
    for layer in reversed(range(layers)):
        in_w, taps, out_w, both_w, down_w = weights[layer]
        width = down_w.shape[0]
        source, normed, joint, mixed, padded, gated, middle, normed_ffn, gate, up, hidden = saved[layer]
        down_in = flat(down_in)
        grad_hidden = outer_cols(down_in, down_w)
        sigmoid = jax.nn.sigmoid(gate)
        grad_gate_up = jnp.concatenate(
            [grad_hidden * up * sigmoid * (1.0 + gate * (1.0 - sigmoid)), grad_hidden * gate * sigmoid], axis=1
        ).astype(BF16)
        partial = blocks(outer_cols(grad_gate_up, both_w).astype(BF16))
        grad_middle, grad_gain_ffn, mix_in = exchange("bwd", partial, grad_stream, middle, gains[layer, 1])
        grad_down = lax.psum_scatter(inner_rows(hidden, down_in).astype(BF16), DP, scatter_dimension=0, tiled=True).astype(F32)
        grad_both = scatter_columns(inner_rows(normed_ffn, grad_gate_up).astype(BF16)).astype(F32)
        grad_gate = column_whole(grad_both[:, :, :width], 1)
        grad_up = column_whole(grad_both[:, :, width:], 1)
        mix_in = flat(mix_in)
        grad_gated = blocks(outer_cols(mix_in, out_w))
        grad_joint, grad_taps = conv_backward(grad_gated, joint, mixed, padded, taps, keep_one, keep_two)
        grad_joint = flat(grad_joint)
        partial = blocks(outer_cols(grad_joint, in_w).astype(BF16))
        if layer > 0:
            grad_stream, grad_gain_mix, down_in = exchange("bwd", partial, grad_middle, source, gains[layer, 0])
        else:
            grad_stream, grad_gain_mix = exchange("last", partial, grad_middle, source, gains[layer, 0])
        grad_out_w = lax.psum_scatter(inner_rows(gated, mix_in).astype(BF16), DP, scatter_dimension=0, tiled=True).astype(F32)
        grad_in_w = column_whole(scatter_columns(inner_rows(normed, grad_joint).astype(BF16)).astype(F32), 3)
        pieces[layer] = (grad_gain_mix, grad_in_w, grad_taps, grad_out_w, grad_gain_ffn, grad_gate, grad_up, grad_down)
    gain_grads = jnp.stack([jnp.concatenate([p[0], p[4]]) for p in pieces])
    gain_grads = lax.psum_scatter(gain_grads, OWNERS, scatter_dimension=2, tiled=True)
    tap_grads = lax.psum_scatter(jnp.stack([p[2] for p in pieces]), DP, scatter_dimension=2, tiled=True)
    return (
        stream[None],
        grad_stream[None],
        gain_grads[:, 0],
        jnp.stack([p[1] for p in pieces]),
        tap_grads.transpose(0, 2, 1),
        jnp.stack([p[3] for p in pieces]),
        gain_grads[:, 1],
        jnp.stack([p[5] for p in pieces]),
        jnp.stack([p[6] for p in pieces]),
        jnp.stack([p[7] for p in pieces]),
    )


def solution(mesh):
    dp, seq = mesh.shape["dp"], mesh.shape["seq"]
    side = dp // 2
    split = Mesh(mesh.devices.reshape(side // 2, 2, 2, seq // side // 2, 2, side), OWNERS)
    token = P(ROW_AXES, SEQ_AXES, None)
    vector = P(None, OWNERS)
    matrix = P(None, OWNERS, None)
    return jax.shard_map(
        local,
        mesh=split,
        in_specs=(token, P(ROW_AXES, None), vector, matrix, matrix, matrix, vector, matrix, matrix, matrix, token),
        out_specs=(token, token, vector, matrix, matrix, matrix, vector, matrix, matrix, matrix),
        check_vma=False,
    )
```

```python
import functools
import itertools

import jax
import jax.numpy as jnp
from jax import lax
from jax.experimental import pallas as pl
from jax.experimental.pallas import tpu as pltpu
from jax.sharding import Mesh, PartitionSpec as P

EPSILON = 1e-05
TP = ("zl", "yl", "core")
DP = ("yh", "zh", "x")
ROW_AXES = ("yh", "yl", "core")
SEQ_AXES = ("zh", "zl", "x")
OWNERS = ROW_AXES + SEQ_AXES
BF16 = jnp.bfloat16
F32 = jnp.float32
MESH = pl.DeviceIdType.MESH
HALVES = 2
IN_NAMES = {
    "first": ("stream", "gain"),
    "fwd": ("partial", "stream", "gain"),
    "turn": ("partial", "stream", "grad"),
    "bwd": ("partial", "grad", "stream", "gain"),
    "last": ("partial", "grad", "stream", "gain"),
}
OUT_NAMES = {
    "first": ("whole",),
    "fwd": ("stream_next", "whole"),
    "turn": ("stream_next", "whole"),
    "bwd": ("grad_next", "gain_grad", "whole"),
    "last": ("grad_next", "gain_grad"),
}
COLLECTIVE_ID = {
    "first": 0, "fwd_ffn": 1, "fwd_conv": 2, "turn": 3, "bwd_ffn": 4, "bwd_conv": 5, "last": 6, "prepare": 7, "collect": 8,
}
FLIPS = ((1, 1, 1), (1, 1, 0), (1, 0, 1), (1, 0, 0), (0, 1, 1), (0, 1, 0), (0, 0, 1))
OTHERS = tuple(itertools.product((0, 1), repeat=5))[1:]
OTHER_AXES = ("yl", "core", "zh", "zl", "x")
SEMAPHORES = 64
LANES = 128


def rms_scale(values):
    return lax.rsqrt(jnp.mean(values * values, axis=-1, keepdims=True) + EPSILON)


class Place:
    def __init__(self, send, recv, local):
        self.zl, self.yl, self.core = (lax.axis_index(axis) for axis in TP)
        self.zh, self.x = lax.axis_index("zh"), lax.axis_index("x")
        self.send, self.recv, self.local = send, recv, local
        self.remote_count = self.local_count = 0
        self.sent = []

    def rank(self, flip_z, flip_y, flip_core):
        return self.flipped("zl", flip_z) * 4 + self.flipped("yl", flip_y) * 2 + self.flipped("core", flip_core)

    def flipped(self, axis, flip):
        return 1 - getattr(self, axis) if flip else getattr(self, axis)

    def member(self, flips):
        return {axis: 1 - getattr(self, axis) for axis, flip in zip(TP, flips) if flip}

    def beside(self, axis):
        return {axis: 1 - getattr(self, axis)}

    def owner(self, flips=(0,) * 5):
        index = 0
        for axis, flip in zip(OTHER_AXES, flips):
            index = index * 2 + self.flipped(axis, flip)
        return index

    def push(self, src, dst, device):
        index = self.remote_count
        self.remote_count += 1
        copy = pltpu.make_async_remote_copy(
            src_ref=src, dst_ref=dst, send_sem=self.send.at[index], recv_sem=self.recv.at[index],
            device_id=device, device_id_type=MESH,
        )
        self.sent.append(copy)
        return copy

    def copy(self, src, dst):
        index = self.local_count
        self.local_count += 1
        return pltpu.make_async_copy(src, dst, self.local.at[index])


def pieces_of(groups, width, group, low, high):
    main = width // LANES * LANES
    rest = width - main
    ranges = []
    if low < main:
        ranges.append((group * main + low, group * main + min(high, main)))
    if high > main:
        start = groups * main + group * rest - main
        ranges.append((start + max(low, main), start + high))
    return ranges


def shards_from(weights, out):
    width = weights[0].shape[1] // 8
    block = width // 4
    main = width // LANES * LANES
    rest = width - main
    for group, weight in enumerate(weights):
        for member in range(8):
            zl, others = member // 4, member % 4
            starts = [((others * 2 + zh) * 4 + zl * 2 + x) * block for zh in range(2) for x in range(2)]
            values = jnp.concatenate([weight[:, start : start + block] for start in starts], axis=1).astype(BF16)
            out[member, :, group * main : (group + 1) * main] = values[:, :main]
            if rest:
                low = len(weights) * main + group * rest
                out[member, :, low : low + rest] = values[:, main:]


def shards_to(shards, outs):
    groups, width = len(outs), shards.shape[2] // len(outs)
    block = width // 4
    for group, out in enumerate(outs):
        for others in range(4):
            for zh in range(2):
                values = []
                for zl in range(2):
                    for x in range(2):
                        low = (zh * 2 + x) * block
                        for start, end in pieces_of(groups, width, group, low, low + block):
                            values.append(shards[zl * 4 + others, :, start:end].astype(F32))
                start = (others * 2 + zh) * 4 * block
                out[:, start : start + 4 * block] = jnp.concatenate(values, axis=1)


def prepare_kernel(layers, small, in_proj, gate, up, out_proj, down, *refs):
    refs = list(refs)
    spread, *refs = refs
    outs, (send, recv, local) = refs[:-3], refs[-3:]
    place = Place(send, recv, local)
    barrier = pltpu.get_barrier_semaphore()
    for flips in OTHERS:
        device = {axis: place.flipped(axis, 1) for axis, flip in zip(OTHER_AXES, flips) if flip}
        pl.semaphore_signal(barrier, inc=1, device_id=device, device_id_type=MESH)
    pl.semaphore_wait(barrier, len(OTHERS))
    kept = place.copy(small, spread.at[place.owner()])
    kept.start()
    copies = []
    for flips in OTHERS:
        device = {axis: place.flipped(axis, 1) for axis, flip in zip(OTHER_AXES, flips) if flip}
        copies.append(place.push(small, spread.at[place.owner()], device))
        copies[-1].start()
    width = in_proj.shape[2] // 3
    for layer in range(layers):
        in_out, both_out, out_out, down_out = outs[4 * layer : 4 * layer + 4]
        shards_from([in_proj.at[layer, :, i * width : (i + 1) * width] for i in range(3)], in_out)
        shards_from([gate.at[layer], up.at[layer]], both_out)
        out_out[...] = out_proj[layer].astype(BF16)
        down_out[...] = down[layer].astype(BF16)
    kept.wait()
    for copy in copies:
        copy.wait()


def prepare(small, in_proj, gate, up, out_proj, down):
    layers, rows, columns = in_proj.shape
    width = gate.shape[2]
    shapes = []
    for _ in range(layers):
        shapes += [
            (8, rows, columns // 8), (8, rows, width // 4), out_proj.shape[1:], down.shape[1:],
        ]
    inside = pl.BlockSpec(memory_space=pltpu.VMEM)
    return pl.pallas_call(
        functools.partial(prepare_kernel, layers),
        out_shape=[jax.ShapeDtypeStruct((32,) + small.shape, F32)]
        + [jax.ShapeDtypeStruct(shape, BF16) for shape in shapes],
        in_specs=[inside] * 6,
        out_specs=[inside] * (1 + len(shapes)),
        scratch_shapes=[pltpu.SemaphoreType.DMA((SEMAPHORES,))] * 3,
        compiler_params=pltpu.CompilerParams(
            collective_id=COLLECTIVE_ID["prepare"], has_side_effects=True, vmem_limit_bytes=48 << 20
        ),
        name="prepare",
    )(small, in_proj, gate, up, out_proj, down)


def collect_kernel(slabs, out, landed, send, recv, local):
    place = Place(send, recv, local)
    barrier = pltpu.get_barrier_semaphore()
    for flips in OTHERS:
        device = {axis: place.flipped(axis, 1) for axis, flip in zip(OTHER_AXES, flips) if flip}
        pl.semaphore_signal(barrier, inc=1, device_id=device, device_id_type=MESH)
    pl.semaphore_wait(barrier, len(OTHERS))
    copies = []
    for i, flips in enumerate(OTHERS):
        device = {axis: place.flipped(axis, 1) for axis, flip in zip(OTHER_AXES, flips) if flip}
        copies.append(place.push(slabs.at[place.owner(flips)], landed.at[i], device))
        copies[-1].start()
    for copy in copies:
        copy.wait()
    out[...] = slabs[place.owner()] + jnp.sum(landed[...], axis=0)


def collect(slabs):
    inside = pl.BlockSpec(memory_space=pltpu.VMEM)
    return pl.pallas_call(
        collect_kernel,
        out_shape=jax.ShapeDtypeStruct(slabs.shape[1:], F32),
        in_specs=[inside],
        out_specs=inside,
        scratch_shapes=[pltpu.VMEM((len(OTHERS),) + slabs.shape[1:], F32)] + [pltpu.SemaphoreType.DMA((SEMAPHORES,))] * 3,
        compiler_params=pltpu.CompilerParams(collective_id=COLLECTIVE_ID["collect"], has_side_effects=True),
        name="collect",
    )(slabs)


class Gather:
    def __init__(self, place, mine, whole):
        self.columns = len(whole.shape) == 6
        self.chunks = whole.shape[0] if self.columns else 1
        self.mine, self.whole, self.place = mine, whole, place
        own, other = place.zh, 1 - place.zh
        self.along_z = [place.push(self.of_mine(c), self.at(c, own), place.beside("zh")) for c in range(self.chunks)]
        self.along_x = [place.push(self.of_mine(c), self.at(c, own), place.beside("x")) for c in range(self.chunks)]
        self.onward = [place.push(self.at(c, other), self.at(c, other), place.beside("x")) for c in range(self.chunks)]
        self.kept = [place.copy(self.of_mine(c), self.at(c, own)) for c in range(self.chunks)]

    def of_mine(self, c):
        return self.mine.at[c] if self.columns else self.mine

    def at(self, c, zh):
        return self.whole.at[c, zh, :, self.place.x] if self.columns else self.whole.at[zh, self.place.x]

    def start(self):
        for copies in (self.along_z, self.along_x, self.kept):
            for copy in copies:
                copy.start()

    def steps(self):
        def step(c):
            self.along_z[c].wait_recv()
            self.onward[c].start()
        return [functools.partial(step, c) for c in range(self.chunks)]

    def finish(self):
        for c in range(self.chunks):
            self.along_x[c].wait_recv()
            self.onward[c].wait_recv()
            self.kept[c].wait()


class Reduce:
    def __init__(self, place, total, outs, scratch):
        self.columns = len(total.shape) == 6
        self.place, self.total, self.outs = place, total, outs
        self.own, self.xin, self.zout, self.zin = scratch[:4]
        self.final, self.landed = scratch[4:] if self.columns else (None, None)
        self.chunks = 4 if self.columns else 1
        x, beside = place.x, place.beside
        pick = self.pick
        self.along_x = [place.push(pick(j, 1 - x), self.xin.at[j], beside("x")) for j in range(self.chunks)]
        self.kept = [place.copy(pick(j, x), self.own.at[j]) for j in range(self.chunks)]
        self.along_z = [place.push(self.zout.at[j], self.zin.at[j], beside("zh")) for j in range(self.chunks)]
        if self.columns:
            mine = place.rank(0, 0, 0)
            self.back = [
                [
                    place.push(self.final.at[j, fz], self.landed.at[mine], place.member((fz,) + self.flips(j)))
                    if (fz,) + self.flips(j) != (0, 0, 0)
                    else place.copy(self.final.at[j, fz], self.landed.at[mine])
                    for fz in (1, 0)
                ]
                for j in range(4)
            ]

    def flips(self, j):
        return ((1, 1), (1, 0), (0, 1), (0, 0))[j]

    def pick(self, j, x):
        if not self.columns:
            return self.total.at[:, x]
        flip_y, flip_core = self.flips(j)
        return self.total.at[self.place.flipped("yl", flip_y) * 2 + self.place.flipped("core", flip_core), :, :, x]

    def start(self):
        for j in range(self.chunks):
            self.along_x[j].start()
            self.kept[j].start()

    def steps(self):
        def first(j):
            self.kept[j].wait()
            self.along_x[j].wait_recv()
            there = 1 - self.place.zh
            self.zout[j] = (self.own[j, there].astype(F32) + self.xin[j, there].astype(F32)).astype(BF16)
            self.along_z[j].start()

        def second(j):
            self.along_z[j].wait_recv()
            here = self.place.zh
            total = self.own[j, here].astype(F32) + self.xin[j, here].astype(F32) + self.zin[j].astype(F32)
            if not self.columns:
                self.outs[0][...] = total
                return
            zl = self.place.zl
            for i, fz in enumerate((1, 0)):
                row = 1 - zl if fz else zl
                self.final[j, fz] = (
                    self.own[j, here, row].astype(F32) + self.xin[j, here, row].astype(F32) + self.zin[j, row].astype(F32)
                ).astype(BF16)
                self.back[j][i].start()

        steps = [functools.partial(first, 0)]
        for j in range(1, self.chunks):
            steps += [functools.partial(first, j), functools.partial(second, j - 1)]
        return steps + [functools.partial(second, self.chunks - 1)]

    def finish(self):
        if self.columns:
            for copies in self.back:
                for copy in copies:
                    if copy is self.back[3][1]:
                        copy.wait()
                    else:
                        copy.wait_recv()
            shards_to(self.landed, self.outs)


def exchange_kernel(kind, plan, *refs):
    reduces, gathers = kind != "first", kind != "last"
    refs = list(refs)

    def take(count):
        taken = refs[:count]
        del refs[:count]
        return taken

    ref = dict(zip(IN_NAMES[kind], take(len(IN_NAMES[kind]))))
    shard_refs, mine_refs, total_refs = (take(plan[name]) for name in ("shards", "mine", "totals"))
    ref.update(zip(OUT_NAMES[kind], take(len(OUT_NAMES[kind]))))
    shard_outs, whole_outs = (take(plan[name]) for name in ("shards", "wholes"))
    total_outs = [take(count) for count in plan["groups"]]
    near, sib, yin, yout, zin, zout, mine, send, recv, local = take(10)
    place = Place(send, recv, local)
    tokens = mine.shape[0]
    half = tokens // HALVES
    to_sibling, to_y, to_z = (place.beside(axis) for axis in ("core", "yl", "zl"))
    rank, push = place.rank, place.push

    def part(h):
        return pl.ds(h * half, half)

    chips = ((1, 1), (0, 1), (1, 0), (0, 0))
    if reduces:
        near_copies = [place.copy(ref["partial"].at[rank(*chip, 0)], near.at[i]) for i, chip in enumerate(chips)]
        for copy in near_copies:
            copy.start()
    if kind == "first":
        stream = ref["stream"][...]
        mine[...] = (stream * rms_scale(stream) * ref["gain"][...]).astype(BF16)
    if kind == "turn":
        mine[...] = ref["grad"][...].astype(BF16)

    partners = [place.member(flips) for flips in FLIPS] if shard_refs or total_refs else [to_sibling, to_y, to_z]
    if whole_outs or total_refs:
        partners += [place.beside("zh"), place.beside("x")]
    barrier = pltpu.get_barrier_semaphore()
    for partner in partners:
        pl.semaphore_signal(barrier, inc=1, device_id=partner, device_id_type=MESH)
    pl.semaphore_wait(barrier, len(partners))

    scattered = []
    for shards, out in zip(shard_refs, shard_outs):
        here = out.at[place.yl * 2 + place.core, place.zl]
        scattered.append(
            [push(shards.at[rank(*flips)], here, place.member(flips)) for flips in FLIPS]
            + [place.copy(shards.at[rank(0, 0, 0)], here)]
        )
    gather_list = [Gather(place, own, whole) for own, whole in zip(shard_outs[:1] + mine_refs, whole_outs)]
    reduce_list = []
    for total, out in zip(total_refs, total_outs):
        reduce_list.append(Reduce(place, total, out, take(6 if len(total.shape) == 6 else 4)))
    steps = []

    def do_steps(count):
        for step in steps[:count]:
            step()
        del steps[:count]

    for item in reduce_list:
        item.start()
        steps += item.steps()
    for item in gather_list[1:] if scattered else gather_list:
        item.start()
    for copy in scattered[0] if scattered else ():
        copy.start()

    if gathers:
        whole = ref["whole"]
        own, beside_z, beside_y, corner = (rank(*chip, 0) for chip in ((0, 0), (1, 0), (0, 1), (1, 1)))
        halves = [part(h) for h in range(HALVES)]

        def sends(src, at, device):
            return [push(src.at[at, rows] if src is whole else src.at[rows], whole.at[at, rows], device) for rows in halves]

        own_places = [place.copy(mine.at[rows], whole.at[own, rows]) for rows in halves]
        own_to_core = sends(mine, own, to_sibling)
        from_z, from_y = sends(mine, own, to_z), sends(mine, own, to_y)
        from_corner = sends(whole, beside_z, to_y)
        z_to_core, y_to_core, corner_to_core = (sends(whole, at, to_sibling) for at in (beside_z, beside_y, corner))

    def send_mine(h):
        for copies in (from_z, from_y, own_to_core, own_places):
            copies[h].start()

    if kind in ("first", "turn"):
        for h in range(HALVES):
            send_mine(h)
    for copies in scattered[1:]:
        for copy in copies:
            copy.start()
    if scattered:
        for copy in scattered[0][:-1]:
            copy.wait_recv()
        scattered[0][-1].wait()
        gather_list[0].start()
    for item in gather_list:
        steps += item.steps()
    step_count = len(steps)

    if reduces:
        sib_copies = [push(ref["partial"].at[rank(*chip, 1)], sib.at[i], to_sibling) for i, chip in enumerate(chips)]
        for copy in sib_copies:
            copy.start()
        y_copies = [[push(yout.at[i, part(h)], yin.at[i, part(h)], to_y) for h in range(HALVES)] for i in range(2)]
        z_copies = [push(zout.at[part(h)], zin.at[part(h)], to_z) for h in range(HALVES)]

        def chip_sum(i, h):
            return near[i, part(h)].astype(F32) + sib[i, part(h)].astype(F32)

        for i in range(2):
            near_copies[i].wait()
            sib_copies[i].wait_recv()
            for h in range(HALVES):
                yout[i, part(h)] = chip_sum(i, h).astype(BF16)
                y_copies[i][h].start()
        near_copies[2].wait()
        sib_copies[2].wait_recv()
        for h in range(HALVES):
            y_copies[0][h].wait_recv()
            zout[part(h)] = (chip_sum(2, h) + yin[0, part(h)].astype(F32)).astype(BF16)
            z_copies[h].start()
        do_steps(step_count // 4)
        near_copies[3].wait()
        sib_copies[3].wait_recv()
        for h in range(HALVES):
            rows = part(h)
            y_copies[1][h].wait_recv()
            z_copies[h].wait_recv()
            total = chip_sum(3, h) + yin[1, rows].astype(F32) + zin[rows].astype(F32)
            stream = ref["stream"][rows]
            if kind in ("fwd", "turn"):
                stream = stream + total
                ref["stream_next"][rows] = stream
            if kind == "fwd":
                mine[rows] = (stream * rms_scale(stream) * ref["gain"][...]).astype(BF16)
                send_mine(h)
            if kind in ("bwd", "last"):
                scale = rms_scale(stream)
                gain_grad = jnp.sum(total * stream * scale, axis=0, keepdims=True)
                ref["gain_grad"][...] = gain_grad if h == 0 else ref["gain_grad"][...] + gain_grad
                scaled = total * ref["gain"][...]
                grad = (
                    ref["grad"][rows]
                    + scale * scaled
                    - stream * (scale * scale * scale) * jnp.mean(scaled * stream, axis=-1, keepdims=True)
                )
                ref["grad_next"][rows] = grad
                if kind == "bwd":
                    mine[rows] = grad.astype(BF16)
                    send_mine(h)
        do_steps(step_count // 4)

    if gathers:
        for h in range(HALVES):
            from_z[h].wait_recv()
            from_corner[h].start()
            z_to_core[h].start()
        do_steps(step_count // 4)
        for h in range(HALVES):
            from_y[h].wait_recv()
            y_to_core[h].start()
        for h in range(HALVES):
            from_corner[h].wait_recv()
            corner_to_core[h].start()
        for copy in own_places:
            copy.wait()
    do_steps(step_count)
    if gathers:
        for copy in own_to_core + z_to_core + y_to_core + corner_to_core:
            copy.wait_recv()
    for copies in scattered[1:]:
        for copy in copies[:-1]:
            copy.wait_recv()
        copies[-1].wait()
    for item in gather_list + reduce_list:
        item.finish()
    for copy in place.sent:
        copy.wait_send()


def exchange(kind, operands, use="", shards=(), mine=(), totals=(), groups=()):
    tokens, features = operands[IN_NAMES[kind].index("stream")].shape
    shapes = {
        "whole": ((8, tokens, features), BF16),
        "stream_next": ((tokens, features), F32),
        "grad_next": ((tokens, features), F32),
        "gain_grad": ((1, features), F32),
    }
    anywhere = pl.BlockSpec(memory_space=pl.ANY)
    inside = pl.BlockSpec(memory_space=pltpu.VMEM)
    block = (tokens, features)
    outs = [shapes[name] + (anywhere if name == "whole" else inside,) for name in OUT_NAMES[kind]]
    outs += [((4, 2) + array.shape[1:], BF16, anywhere) for array in shards]
    for array in [jax.ShapeDtypeStruct((4, 2) + array.shape[1:], BF16) for array in shards[:1]] + list(mine):
        if len(array.shape) == 4:
            outs.append(((4, 2, 2, 2) + array.shape[2:], BF16, anywhere))
        else:
            outs.append(((2, 2) + array.shape, BF16, anywhere))
    scratch = [
        pltpu.VMEM((4,) + block, BF16),
        pltpu.VMEM((4,) + block, BF16),
        pltpu.VMEM((2,) + block, BF16),
        pltpu.VMEM((2,) + block, BF16),
        pltpu.VMEM(block, BF16),
        pltpu.VMEM(block, BF16),
        pltpu.VMEM(block, BF16),
        pltpu.SemaphoreType.DMA((SEMAPHORES,)),
        pltpu.SemaphoreType.DMA((SEMAPHORES,)),
        pltpu.SemaphoreType.DMA((SEMAPHORES,)),
    ]
    for array, count in zip(totals, groups):
        if array.ndim == 6:
            rows = array.shape[4:]
            outs += [((rows[0], rows[1] // count * 8), F32, inside)] * count
            quarter = (4, 2) + rows
            scratch += [pltpu.VMEM((4, 2, 2) + rows, BF16)] * 2 + [pltpu.VMEM(quarter, BF16)] * 3
            scratch.append(pltpu.VMEM((8,) + rows, BF16))
        else:
            rows = array.shape[2:]
            outs.append((rows, F32, inside))
            scratch += [pltpu.VMEM((1, 2) + rows, BF16)] * 2 + [pltpu.VMEM((1,) + rows, BF16)] * 2
    plan = {
        "shards": len(shards), "mine": len(mine), "totals": len(totals), "wholes": len(shards[:1]) + len(mine),
        "groups": groups,
    }
    name = kind + use
    return pl.pallas_call(
        functools.partial(exchange_kernel, kind, plan),
        out_shape=tuple(jax.ShapeDtypeStruct(shape, dtype) for shape, dtype, _ in outs),
        in_specs=[anywhere if name == "partial" else inside for name in IN_NAMES[kind]]
        + [anywhere] * (len(shards) + len(mine) + len(totals)),
        out_specs=tuple(spec for _, _, spec in outs),
        scratch_shapes=scratch,
        compiler_params=pltpu.CompilerParams(
            collective_id=COLLECTIVE_ID[name], has_side_effects=True, vmem_limit_bytes=48 << 20
        ),
        cost_estimate=pl.CostEstimate(flops=10**7, bytes_accessed=150 * 10**6, transcendentals=0),
        name="exchange_" + name,
    )(*operands, *shards, *mine, *totals)


def matmul(left, right):
    return jnp.dot(left, right, preferred_element_type=F32)


def inner_rows(left, right):
    return lax.dot_general(left, right, (((0,), (0,)), ((), ())), preferred_element_type=F32)


def outer_cols(left, right):
    return lax.dot_general(left, right, (((1,), (1,)), ((), ())), preferred_element_type=F32)


def sizes_of(axes):
    return tuple(lax.axis_size(axis) for axis in axes)


def split_owners(array, dim):
    owners = sizes_of(OWNERS)
    count = 1
    for size in owners:
        count *= size
    shape = array.shape
    return array.reshape(shape[:dim] + owners + (shape[dim] // count,) + shape[dim + 1 :])


def column_shards(weights):
    rows = weights[0].shape[0]
    mains, rests = [], []
    for weight in weights:
        parts = split_owners(weight, 1).transpose(5, 2, 3, 0, 1, 4, 6, 7).reshape(8, rows, -1)
        main = parts.shape[2] // LANES * LANES
        mains.append(parts[:, :, :main])
        rests.append(parts[:, :, main:])
    return jnp.concatenate(mains + rests, axis=2)


def column_groups(values, groups):
    width = values.shape[-1] // groups
    return [
        jnp.concatenate([values[..., a:b] for a, b in pieces_of(groups, width, group, 0, width)], axis=-1)
        for group in range(groups)
    ]


def group_columns(groups):
    main = groups[0].shape[-1] // LANES * LANES
    return jnp.concatenate([g[..., :main] for g in groups] + [g[..., main:] for g in groups], axis=-1)


def column_whole(shards, groups):
    rows = shards.shape[1]
    yh, yl, core, zh, zl, x = sizes_of(OWNERS)
    return [
        part.reshape(zl, yl, core, rows, yh, zh, x, -1).transpose(3, 4, 1, 2, 5, 0, 6, 7).reshape(rows, -1)
        for part in column_groups(shards, groups)
    ]


def gather_columns(shards):
    mine = lax.all_to_all(shards, TP, split_axis=0, concat_axis=0, tiled=True)
    whole = lax.all_gather(mine, DP, axis=0, tiled=False)
    yh, yl, core, zh, zl, x = sizes_of(OWNERS)
    rows, columns = shards.shape[1:]
    whole = whole.reshape(yh, zh, x, zl, yl, core, rows, columns)
    return whole.transpose(0, 4, 5, 1, 3, 2, 6, 7).reshape(-1, columns)


def scatter_columns(total):
    yh, yl, core, zh, zl, x = sizes_of(OWNERS)
    columns = total.shape[1]
    parts = split_owners(total, 0).transpose(0, 3, 5, 4, 1, 2, 6, 7)
    parts = parts.reshape(yh * zh * x, -1, columns)
    mine = lax.psum_scatter(parts, DP, scatter_dimension=0, tiled=False)
    mine = mine.reshape(8, -1, columns)
    return lax.all_to_all(mine, TP, split_axis=0, concat_axis=0, tiled=True)


def tails_before(tails):
    x_size, zh_size = lax.axis_size("x"), lax.axis_size("zh")
    tails = tails.reshape((2, 4) + tails.shape[1:])
    beside = lax.ppermute(tails, "x", [(i, (i + 1) % x_size) for i in range(x_size)])
    pairs = [(i * x_size + x_size - 1, (i + 1) * x_size) for i in range(zh_size - 1)]
    below = lax.ppermute(tails[1], ("zh", "x"), pairs)
    first = jnp.stack([below, beside[0]])
    return jnp.where(lax.axis_index("x") == 0, first, beside).reshape((8,) + tails.shape[2:])


def heads_after(heads):
    x_size, zh_size = lax.axis_size("x"), lax.axis_size("zh")
    heads = heads.reshape((2, 4) + heads.shape[1:])
    beside = lax.ppermute(heads, "x", [((i + 1) % x_size, i) for i in range(x_size)])
    pairs = [((i + 1) * x_size, i * x_size + x_size - 1) for i in range(zh_size - 1)]
    above = lax.ppermute(heads[0], ("zh", "x"), pairs)
    final = jnp.stack([beside[1], above])
    return jnp.where(lax.axis_index("x") == x_size - 1, final, beside).reshape((8,) + heads.shape[2:])


def tap_masks(starts, token_count):
    zh, x, x_size = lax.axis_index("zh"), lax.axis_index("x"), lax.axis_size("x")
    blocks = (zh * 2 + jnp.arange(2, dtype=jnp.int32)) * x_size + x
    places = blocks[:, None] * token_count + jnp.arange(token_count, dtype=jnp.int32)

    def segment_of(where):
        return jnp.sum((starts[None, :, None, :] <= where[:, None, :, None]).astype(jnp.int32), axis=3)

    own_segment = segment_of(places)
    keep_one = (segment_of(places - 1) == own_segment).astype(F32)
    keep_two = (segment_of(places - 2) == own_segment).astype(F32)
    return keep_one.reshape(8, token_count, 1), keep_two.reshape(8, token_count, 1)


def conv_forward(joint, taps, keep_one, keep_two):
    positions = joint.shape[1]
    b_part, c_part, x_part = column_groups(joint, 3)
    carried = b_part * x_part
    previous = tails_before(carried[:, positions - 2 :])
    padded = jnp.concatenate([previous, carried], axis=1)
    mixed = (
        taps[:, 0] * padded[:, :positions] * keep_two
        + taps[:, 1] * padded[:, 1 : positions + 1] * keep_one
        + taps[:, 2] * carried
    )
    return (c_part * mixed).astype(BF16), mixed, padded


def conv_backward(grad_gated, joint, mixed, padded, taps, keep_one, keep_two):
    rows, positions, width = grad_gated.shape
    b_part, c_part, x_part = column_groups(joint, 3)
    grad_c = grad_gated * mixed
    grad_mixed = grad_gated * c_part
    first_tap = grad_mixed * keep_two
    second_tap = grad_mixed * keep_one
    grad_taps = jnp.stack(
        [
            jnp.sum(first_tap * padded[:, :positions], axis=(0, 1)),
            jnp.sum(second_tap * padded[:, 1 : positions + 1], axis=(0, 1)),
            jnp.sum(grad_mixed * padded[:, 2:], axis=(0, 1)),
        ],
        axis=0,
    )
    one = jnp.zeros((rows, 1, width), F32)
    two = jnp.zeros((rows, 2, width), F32)
    grad_padded = jnp.concatenate([first_tap * taps[:, 0], two], axis=1) + jnp.concatenate(
        [one, second_tap * taps[:, 1], one], axis=1
    )
    returned = heads_after(grad_padded[:, :2])
    arriving = jnp.concatenate([jnp.zeros((rows, positions - 2, width), F32), returned], axis=1)
    grad_carried = grad_padded[:, 2:] + grad_mixed * taps[:, 2] + arriving
    return group_columns([grad_carried * x_part, grad_c, grad_carried * b_part]).astype(BF16), grad_taps


def local(stream_in, doc_starts, norm_mix, in_proj, conv_taps, out_proj, norm_ffn, w_gate, w_up, w_down, grad_out):
    _, token_count, features = stream_in.shape
    layers = norm_mix.shape[0]
    def blocks(array):
        return array.reshape(8, token_count, -1)

    def flat(array):
        return array.reshape(8 * token_count, -1)

    own_kernels = sizes_of(DP) == (1, 2, 2)
    stream = stream_in.reshape(-1, features)
    grad_stream = grad_out.reshape(-1, features)
    small = jnp.concatenate([norm_mix[:, None], norm_ffn[:, None], conv_taps.transpose(0, 2, 1)], axis=1)
    small = small.astype(BF16).astype(F32)
    owned = small.shape[2]
    in_w, both_w, out_w, down_w = ([None] * layers for _ in range(4))
    if own_kernels:
        packed = jnp.zeros((16, LANES), F32).at[: 5 * layers, :owned].set(small.reshape(-1, owned))
        packed = packed.at[15, : doc_starts.shape[1]].set(doc_starts[0].astype(F32))
        spread, *results = prepare(packed, in_proj, w_gate, w_up, out_proj, w_down)
        shards, out_own, down_own = [], [], []
        for layer in range(layers):
            shards += results[4 * layer : 4 * layer + 2]
            out_own.append(results[4 * layer + 2])
            down_own.append(results[4 * layer + 3])
        params = spread[:, : 5 * layers, :owned].transpose(1, 0, 2)
        gains = params.reshape(layers, 5, 1, -1)[:, :2]
        params = params.reshape(layers, 5, 4, 2, 2, 2, owned)[:, 2:]
        others = lax.axis_index("yl") * 2 + lax.axis_index("core")
        params = lax.dynamic_index_in_dim(params, others, 2, False)
        taps_all = lax.dynamic_index_in_dim(params, lax.axis_index("zl"), 3, False)
        taps_all = taps_all.reshape(layers, 3, -1).transpose(0, 2, 1)
        starts = spread.reshape(4, 8, 16, LANES)[:, 0, 15, : doc_starts.shape[1]].astype(jnp.int32)
        normed, *results = exchange("first", (stream, gains[0, 0]), shards=shards, mine=(out_own[0], down_own[0]))
        mine, results = results[: len(shards)], results[len(shards) :]
        in_w[0], out_w[0], down_w[0] = results
    else:
        starts = lax.all_gather(doc_starts, ("yl", "core"), axis=0, tiled=True)
        small = small.astype(BF16)
        gains = lax.all_gather(small[:, :2], OWNERS, axis=2, tiled=True).astype(F32)[:, :, None]
        taps_all = lax.all_gather(small[:, 2:], DP, axis=2, tiled=True).astype(F32).transpose(0, 2, 1)
        (normed,) = exchange("first", (stream, gains[0, 0]))
        for layer in range(layers):
            in_w[layer] = gather_columns(column_shards(jnp.split(in_proj[layer].astype(BF16), 3, axis=1)))
            both_w[layer] = gather_columns(column_shards([w_gate[layer].astype(BF16), w_up[layer].astype(BF16)]))
            out_w[layer] = lax.all_gather(out_proj[layer].astype(BF16), DP, axis=0, tiled=True)
            down_w[layer] = lax.all_gather(w_down[layer].astype(BF16), DP, axis=0, tiled=True)
    keep_one, keep_two = tap_masks(starts, token_count)

    def rows_of(weight):
        return weight.reshape(-1, weight.shape[-1])

    saved = []
    for layer in range(layers):
        taps = taps_all[layer]
        normed = flat(normed)
        joint = blocks(matmul(normed, rows_of(in_w[layer])))
        gated, mixed, padded = conv_forward(joint, taps, keep_one, keep_two)
        gated = flat(gated)
        partial = blocks(matmul(gated, rows_of(out_w[layer])).astype(BF16))
        moved = (mine[2 * layer + 1],) if own_kernels else ()
        middle, normed_ffn, *results = exchange("fwd", (partial, stream, gains[layer, 1]), "_ffn", mine=moved)
        if own_kernels:
            (both_w[layer],) = results
        normed_ffn = flat(normed_ffn)
        gate_up = matmul(normed_ffn, rows_of(both_w[layer]))
        gate, up = column_groups(gate_up, 2)
        hidden = (jax.nn.silu(gate) * up).astype(BF16)
        saved.append((stream, normed, joint, mixed, padded, gated, middle, normed_ffn, gate, up, hidden))
        partial = blocks(matmul(hidden, rows_of(down_w[layer])).astype(BF16))
        if layer + 1 < layers:
            moved = (mine[2 * layer + 2], out_own[layer + 1], down_own[layer + 1]) if own_kernels else ()
            stream, normed, *results = exchange("fwd", (partial, middle, gains[layer + 1, 0]), "_conv", mine=moved)
            if own_kernels:
                in_w[layer + 1], out_w[layer + 1], down_w[layer + 1] = results
        else:
            stream, down_in = exchange("turn", (partial, middle, grad_stream))

    def by_owner(grad):
        return grad.astype(BF16).reshape(4, 2, 2, 2, -1, grad.shape[1])

    def by_part(grad):
        return grad.astype(BF16).reshape(2, 2, -1, grad.shape[1])

    pieces = [None] * layers
    for layer in reversed(range(layers)):
        source, normed, joint, mixed, padded, gated, middle, normed_ffn, gate, up, hidden = saved[layer]
        taps = taps_all[layer]
        down_in = flat(down_in)
        grad_hidden = outer_cols(down_in, rows_of(down_w[layer]))
        sigmoid = jax.nn.sigmoid(gate)
        grad_gate_up = group_columns(
            [grad_hidden * up * sigmoid * (1.0 + gate * (1.0 - sigmoid)), grad_hidden * gate * sigmoid]
        ).astype(BF16)
        partial = blocks(outer_cols(grad_gate_up, rows_of(both_w[layer])).astype(BF16))
        grad_down = inner_rows(hidden, down_in)
        grad_both = inner_rows(normed_ffn, grad_gate_up)
        totals = (by_owner(grad_both),) if own_kernels else ()
        grad_middle, grad_gain_ffn, mix_in, *results = exchange(
            "bwd", (partial, grad_stream, middle, gains[layer, 1]), "_ffn", totals=totals, groups=(2,)[: len(totals)]
        )
        if own_kernels:
            grad_gate, grad_up = results
        else:
            grad_gate, grad_up = column_whole(scatter_columns(grad_both.astype(BF16)).astype(F32), 2)
        mix_in = flat(mix_in)
        grad_gated = blocks(outer_cols(mix_in, rows_of(out_w[layer])))
        grad_joint, grad_taps = conv_backward(grad_gated, joint, mixed, padded, taps, keep_one, keep_two)
        grad_joint = flat(grad_joint)
        partial = blocks(outer_cols(grad_joint, rows_of(in_w[layer])).astype(BF16))
        grad_out_w, grad_in_w = inner_rows(gated, mix_in), inner_rows(normed, grad_joint)
        totals = (by_owner(grad_in_w), by_part(grad_out_w), by_part(grad_down)) if own_kernels else ()
        operands, groups = (partial, grad_middle, source, gains[layer, 0]), (3, 1, 1)[: len(totals)]
        if layer > 0:
            grad_stream, grad_gain_mix, down_in, *results = exchange("bwd", operands, "_conv", totals=totals, groups=groups)
        else:
            grad_stream, grad_gain_mix, *results = exchange("last", operands, totals=totals, groups=groups)
        if own_kernels:
            *grad_in_w, grad_out_w, grad_down = results
        else:
            grad_in_w = column_whole(scatter_columns(grad_in_w.astype(BF16)).astype(F32), 3)
            grad_out_w, grad_down = (
                lax.psum_scatter(grad.astype(BF16), DP, scatter_dimension=0, tiled=True).astype(F32)
                for grad in (grad_out_w, grad_down)
            )
        grad_in_w = jnp.concatenate(grad_in_w, axis=1)
        pieces[layer] = (grad_gain_mix, grad_in_w, grad_taps, grad_out_w, grad_gain_ffn, grad_gate, grad_up, grad_down)
    gain_grads = jnp.stack([jnp.concatenate([p[0], p[4]]) for p in pieces])
    tap_grads = jnp.stack([p[2] for p in pieces])
    if own_kernels:
        slabs = gain_grads.reshape(2 * layers, 32, owned).transpose(1, 0, 2)
        lanes = ((0, 0), (0, 0), (0, LANES - owned))
        taps = tap_grads.reshape(3 * layers, 2, 1, 2, owned).transpose(1, 2, 3, 0, 4)
        taps = jnp.pad(taps, ((0, 0), (0, 0), (0, 0), (0, 0), (0, LANES - owned)))
        same = (jnp.arange(4) == others)[:, None, None, None, None, None]
        same = same & (jnp.arange(2) == lax.axis_index("zl"))[None, None, :, None, None, None]
        taps = jnp.where(same, taps[None], 0.0).reshape(32, 3 * layers, LANES)
        rows = 16 - 5 * layers
        slabs = jnp.concatenate([jnp.pad(slabs, lanes), taps, jnp.zeros((32, rows, LANES), F32)], axis=1)
        sums = collect(slabs)[:, :owned]
        gain_grads = sums[: 2 * layers].reshape(layers, 2, owned)
        tap_grads = sums[2 * layers : 5 * layers].reshape(layers, 3, owned)
    else:
        gain_grads = lax.psum_scatter(gain_grads, OWNERS, scatter_dimension=2, tiled=True)
        tap_grads = lax.psum_scatter(tap_grads, DP, scatter_dimension=2, tiled=True)
    return (
        stream[None],
        grad_stream[None],
        gain_grads[:, 0],
        jnp.stack([p[1] for p in pieces]),
        tap_grads.transpose(0, 2, 1),
        jnp.stack([p[3] for p in pieces]),
        gain_grads[:, 1],
        jnp.stack([p[5] for p in pieces]),
        jnp.stack([p[6] for p in pieces]),
        jnp.stack([p[7] for p in pieces]),
    )


def solution(mesh):
    dp, seq = mesh.shape["dp"], mesh.shape["seq"]
    side = dp // 2
    split = Mesh(mesh.devices.reshape(side // 2, 2, 2, seq // side // 2, 2, side), OWNERS)
    token = P(ROW_AXES, SEQ_AXES, None)
    vector = P(None, OWNERS)
    matrix = P(None, OWNERS, None)
    return jax.shard_map(
        local,
        mesh=split,
        in_specs=(token, P(ROW_AXES, None), vector, matrix, matrix, matrix, vector, matrix, matrix, matrix, token),
        out_specs=(token, token, vector, matrix, matrix, matrix, vector, matrix, matrix, matrix),
        check_vma=False,
    )
```

```python
import functools
import itertools

import jax
import jax.numpy as jnp
from jax import lax
from jax.experimental import pallas as pl
from jax.experimental.pallas import tpu as pltpu
from jax.sharding import Mesh, PartitionSpec as P

EPSILON = 1e-05
TP = ("zl", "yl", "core")
DP = ("yh", "zh", "x")
ROW_AXES = ("yh", "yl", "core")
SEQ_AXES = ("zh", "zl", "x")
OWNERS = ROW_AXES + SEQ_AXES
BF16 = jnp.bfloat16
F32 = jnp.float32
MESH = pl.DeviceIdType.MESH
HALVES = 2
OWN_IN = {
    "conv": ("mine", "stream", "gain", "taps", "keep"),
    "ffn": ("mine", "stream", "gain"),
    "conv_back": ("mine", "grad", "stream", "gain", "taps", "keep"),
    "ffn_back": ("mine", "grad", "stream", "gain"),
}
GROUP_IN = {
    "conv": ("in_w", "out_w"),
    "ffn": ("both_w", "down_w"),
    "conv_back": ("in_w", "out_w", "whole", "joint", "carried", "mixed", "gated"),
    "ffn_back": ("both_w", "down_w", "whole", "gate_up", "hidden"),
}
OWN_OUT = {
    "conv": ("stream_next", "next"),
    "ffn": ("stream_next", "next"),
    "conv_back": ("grad_next", "gain_grad", "next", "grad_taps"),
    "ffn_back": ("grad_next", "gain_grad", "next"),
}
GROUP_OUT = {
    "conv": ("whole", "joint", "carried", "mixed", "gated"),
    "ffn": ("whole", "gate_up", "hidden"),
    "conv_back": ("grad_in_w", "grad_out_w"),
    "ffn_back": ("grad_both_w", "grad_down_w"),
}
COLLECTIVE_ID = {
    name: i
    for i, name in enumerate(
        ("prepare", "finish", "conv", "ffn", "ffn_moving", "conv_back", "ffn_back", "ffn_back_moving")
    )
}
FLIPS = ((1, 1, 1), (1, 1, 0), (1, 0, 1), (1, 0, 0), (0, 1, 1), (0, 1, 0), (0, 0, 1))
OTHERS = tuple(itertools.product((0, 1), repeat=5))[1:]
OTHER_AXES = ("yl", "core", "zh", "zl", "x")
SEMAPHORES = 112
LANES = 128
TILE = 256
HALO = 8


def rms_scale(values):
    return lax.rsqrt(jnp.mean(values * values, axis=-1, keepdims=True) + EPSILON)


class Place:
    def __init__(self, send, recv, local):
        self.zl, self.yl, self.core = (lax.axis_index(axis) for axis in TP)
        self.zh, self.x = lax.axis_index("zh"), lax.axis_index("x")
        self.send, self.recv, self.local = send, recv, local
        self.remote_count = self.local_count = 0
        self.sent = []

    def rank(self, flip_z, flip_y, flip_core):
        return self.flipped("zl", flip_z) * 4 + self.flipped("yl", flip_y) * 2 + self.flipped("core", flip_core)

    def flipped(self, axis, flip):
        return 1 - getattr(self, axis) if flip else getattr(self, axis)

    def member(self, flips):
        return {axis: 1 - getattr(self, axis) for axis, flip in zip(TP, flips) if flip}

    def beside(self, axis):
        return {axis: 1 - getattr(self, axis)}

    def owner(self, flips=(0,) * 5):
        index = 0
        for axis, flip in zip(OTHER_AXES, flips):
            index = index * 2 + self.flipped(axis, flip)
        return index

    def push(self, src, dst, device, kept=True):
        index = self.remote_count
        self.remote_count += 1
        copy = pltpu.make_async_remote_copy(
            src_ref=src, dst_ref=dst, send_sem=self.send.at[index], recv_sem=self.recv.at[index],
            device_id=device, device_id_type=MESH,
        )
        if kept:
            self.sent.append(copy)
        return copy

    def copy(self, src, dst):
        index = self.local_count
        self.local_count += 1
        return pltpu.make_async_copy(src, dst, self.local.at[index])


def pieces_of(groups, width, group, low, high):
    main = width // LANES * LANES
    rest = width - main
    ranges = []
    if low < main:
        ranges.append((group * main + low, group * main + min(high, main)))
    if high > main:
        start = groups * main + group * rest - main
        ranges.append((start + max(low, main), start + high))
    return ranges


def shards_from(weights, out):
    width = weights[0].shape[1] // 8
    block = width // 4
    main = width // LANES * LANES
    rest = width - main
    for group, weight in enumerate(weights):
        for member in range(8):
            zl, others = member // 4, member % 4
            starts = [((others * 2 + zh) * 4 + zl * 2 + x) * block for zh in range(2) for x in range(2)]
            values = jnp.concatenate([weight[:, start : start + block] for start in starts], axis=1).astype(BF16)
            out[member, :, group * main : (group + 1) * main] = values[:, :main]
            if rest:
                low = len(weights) * main + group * rest
                out[member, :, low : low + rest] = values[:, main:]
    pad = out.shape[2] - len(weights) * width
    if pad:
        out[:, :, len(weights) * width :] = jnp.zeros((8, out.shape[1], pad), BF16)


def shards_to(shards, outs):
    groups, width = len(outs), outs[0].shape[1] // 8
    block = width // 4
    for group, out in enumerate(outs):
        for others in range(4):
            for zh in range(2):
                values = []
                for zl in range(2):
                    for x in range(2):
                        low = (zh * 2 + x) * block
                        for start, end in pieces_of(groups, width, group, low, low + block):
                            values.append(shards[zl * 4 + others, :, start:end].astype(F32))
                start = (others * 2 + zh) * 4 * block
                out[:, start : start + 4 * block] = jnp.concatenate(values, axis=1)


def every_other(place):
    return [
        ({axis: place.flipped(axis, 1) for axis, flip in zip(OTHER_AXES, flips) if flip}, flips) for flips in OTHERS
    ]


def prepare_kernel(layers, small, in_proj, gate, up, out_proj, down, *refs):
    refs = list(refs)

    def take(count):
        taken = refs[:count]
        del refs[:count]
        return taken

    (spread,), mine, rounded, wholes = take(1), take(2 * layers), take(2 * layers), take(3)
    shards, (send, recv, local) = take(2 * layers), take(3)
    place = Place(send, recv, local)
    barrier = pltpu.get_barrier_semaphore()
    for device, _ in every_other(place):
        pl.semaphore_signal(barrier, inc=1, device_id=device, device_id_type=MESH)
    width = in_proj.shape[2] // 3

    def cut(layer, which):
        if which == 0:
            shards_from([in_proj.at[layer, :, i * width : (i + 1) * width] for i in range(3)], shards[2 * layer])
        else:
            shards_from([gate.at[layer], up.at[layer]], shards[2 * layer + 1])

    def scatter(index):
        here = mine[index].at[place.yl * 2 + place.core, place.zl]
        copies = [place.push(shards[index].at[place.rank(*flips)], here, place.member(flips)) for flips in FLIPS]
        copies.append(place.copy(shards[index].at[place.rank(0, 0, 0)], here))
        for copy in copies:
            copy.start()
        return copies

    def landed(copies):
        for copy in copies[:-1]:
            copy.wait_recv()
        copies[-1].wait()

    cut(0, 0)
    for layer in range(layers):
        rounded[2 * layer][...] = out_proj[layer].astype(BF16)
        rounded[2 * layer + 1][...] = down[layer].astype(BF16)
    pl.semaphore_wait(barrier, len(OTHERS))
    kept = place.copy(small, spread.at[place.owner()])
    kept.start()
    spreads = [place.push(small, spread.at[place.owner()], device) for device, _ in every_other(place)]
    first = scatter(0)
    for copy in spreads:
        copy.start()
    gathers = [Gather(place, own, whole) for own, whole in zip([mine[0]] + list(rounded[:2]), wholes)]
    for gather in gathers[1:]:
        gather.start()
    cut(0, 1)
    landed(first)
    gathers[0].start()
    others = [scatter(1)]
    for layer in range(1, layers):
        for which in range(2):
            cut(layer, which)
            others.append(scatter(2 * layer + which))
    for gather in gathers[1:] + gathers[:1]:
        for step in gather.steps():
            step()
    for copies in others:
        landed(copies)
    kept.wait()
    for copy in spreads:
        copy.wait_recv()
    for gather in gathers:
        gather.finish()
    for copy in place.sent:
        copy.wait_send()


def whole_shape(mine):
    return (4, 2, 2, 2) + mine[2:] if len(mine) == 4 else (2, 2) + mine


def prepare(small, in_proj, gate, up, out_proj, down):
    layers, rows, columns = in_proj.shape
    widths = (-(-columns // 8 // LANES) * LANES, gate.shape[2] // 4)
    inside = pl.BlockSpec(memory_space=pltpu.VMEM)
    anywhere = pl.BlockSpec(memory_space=pl.ANY)
    mine = [(4, 2, rows, width) for _ in range(layers) for width in widths]
    rounded = [array.shape[1:] for _ in range(layers) for array in (out_proj, down)]
    wholes = [whole_shape(shape) for shape in [mine[0]] + rounded[:2]]
    outs = pl.pallas_call(
        functools.partial(prepare_kernel, layers),
        out_shape=[jax.ShapeDtypeStruct((32,) + small.shape, F32)]
        + [jax.ShapeDtypeStruct(shape, BF16) for shape in mine + rounded + wholes],
        in_specs=[inside] * 6,
        out_specs=[anywhere] * (1 + len(mine)) + [inside] * len(rounded) + [anywhere] * 3,
        scratch_shapes=[pltpu.VMEM((8, rows, width), BF16) for _ in range(layers) for width in widths]
        + [pltpu.SemaphoreType.DMA((SEMAPHORES,))] * 3,
        compiler_params=pltpu.CompilerParams(
            collective_id=COLLECTIVE_ID["prepare"], has_side_effects=True, vmem_limit_bytes=48 << 20
        ),
        name="prepare",
    )(small, in_proj, gate, up, out_proj, down)
    spread, outs = outs[0], outs[1:]
    return spread, outs[: len(mine)], outs[len(mine) : -3], outs[-3:]


def finish_kernel(counts, slabs, *refs):
    refs = list(refs)

    def take(count):
        taken = refs[:count]
        del refs[:count]
        return taken

    totals = take(len(counts))
    (out,) = take(1)
    outs = [take(count) for count in counts]
    (landed,) = take(1)
    scratch = [take(6 if len(total.shape) == 6 else 4) for total in totals]
    place = Place(*take(3))
    barrier = pltpu.get_barrier_semaphore()
    for device, _ in every_other(place):
        pl.semaphore_signal(barrier, inc=1, device_id=device, device_id_type=MESH)
    pl.semaphore_wait(barrier, len(OTHERS))
    reduces = [Reduce(place, *group) for group in zip(totals, outs, scratch)]
    for item in reduces:
        item.start()
    copies = []
    for i, (device, flips) in enumerate(every_other(place)):
        copies.append(place.push(slabs.at[place.owner(flips)], landed.at[i], device))
        copies[-1].start()
    for step in interleaved([item.steps() for item in reduces]):
        step()
    for copy in copies:
        copy.wait_recv()
    out[...] = slabs[place.owner()] + jnp.sum(landed[...], axis=0)
    for item in reduces:
        item.finish()
    for copy in place.sent:
        copy.wait_send()


def finish(slabs, totals, groups):
    inside = pl.BlockSpec(memory_space=pltpu.VMEM)
    anywhere = pl.BlockSpec(memory_space=pl.ANY)
    outs, scratch = reduce_shapes(totals, groups)
    return pl.pallas_call(
        functools.partial(finish_kernel, groups),
        out_shape=[jax.ShapeDtypeStruct(slabs.shape[1:], F32)] + outs,
        in_specs=[inside] + [anywhere] * len(totals),
        out_specs=[inside] * (1 + len(outs)),
        scratch_shapes=[pltpu.VMEM((len(OTHERS),) + slabs.shape[1:], F32)]
        + scratch
        + [pltpu.SemaphoreType.DMA((SEMAPHORES,))] * 3,
        compiler_params=pltpu.CompilerParams(
            collective_id=COLLECTIVE_ID["finish"], has_side_effects=True, vmem_limit_bytes=48 << 20
        ),
        name="finish",
    )(slabs, *totals)


def interleaved(lists):
    keyed = [((i + 1) / len(items), n, item) for n, items in enumerate(lists) for i, item in enumerate(items)]
    return [item for _, _, item in sorted(keyed, key=lambda entry: entry[:2])]


def reduce_shapes(totals, groups):
    outs, scratch = [], []
    for array, count in zip(totals, groups):
        if array.ndim == 6:
            rows = array.shape[4:]
            width = rows[1] // LANES * LANES if count == 2 else rows[1] - LANES // 2
            outs += [jax.ShapeDtypeStruct((rows[0], width // count * 8), F32)] * count
            quarter = (4, 2) + rows
            scratch += [pltpu.VMEM((4, 2, 2) + rows, BF16)] * 2 + [pltpu.VMEM(quarter, BF16)] * 3
            scratch.append(pltpu.VMEM((8,) + rows, BF16))
        else:
            rows = array.shape[2:]
            outs.append(jax.ShapeDtypeStruct(rows, F32))
            scratch += [pltpu.VMEM((1, 2) + rows, BF16)] * 2 + [pltpu.VMEM((1,) + rows, BF16)] * 2
    return outs, scratch


class Gather:
    def __init__(self, place, mine, whole):
        self.columns = len(whole.shape) == 6
        self.chunks = whole.shape[0] if self.columns else 1
        self.mine, self.whole, self.place = mine, whole, place
        own, other = place.zh, 1 - place.zh
        self.along_z = [place.push(self.of_mine(c), self.at(c, own), place.beside("zh")) for c in range(self.chunks)]
        self.along_x = [place.push(self.of_mine(c), self.at(c, own), place.beside("x")) for c in range(self.chunks)]
        self.onward = [place.push(self.at(c, other), self.at(c, other), place.beside("x")) for c in range(self.chunks)]
        self.kept = [place.copy(self.of_mine(c), self.at(c, own)) for c in range(self.chunks)]

    def of_mine(self, c):
        return self.mine.at[c] if self.columns else self.mine

    def at(self, c, zh):
        return self.whole.at[c, zh, :, self.place.x] if self.columns else self.whole.at[zh, self.place.x]

    def start(self):
        for copies in (self.along_z, self.along_x, self.kept):
            for copy in copies:
                copy.start()

    def steps(self):
        def step(c):
            self.along_z[c].wait_recv()
            self.onward[c].start()
        return [functools.partial(step, c) for c in range(self.chunks)]

    def finish(self):
        for c in range(self.chunks):
            self.along_x[c].wait_recv()
            self.onward[c].wait_recv()
            self.kept[c].wait()


class Reduce:
    def __init__(self, place, total, outs, scratch):
        self.columns = len(total.shape) == 6
        self.place, self.total, self.outs = place, total, outs
        self.own, self.xin, self.zout, self.zin = scratch[:4]
        self.final, self.landed = scratch[4:] if self.columns else (None, None)
        self.chunks = 4 if self.columns else 1
        x, beside = place.x, place.beside
        pick = self.pick
        self.along_x = [place.push(pick(j, 1 - x), self.xin.at[j], beside("x")) for j in range(self.chunks)]
        self.kept = [place.copy(pick(j, x), self.own.at[j]) for j in range(self.chunks)]
        self.along_z = [place.push(self.zout.at[j], self.zin.at[j], beside("zh")) for j in range(self.chunks)]
        if self.columns:
            mine = place.rank(0, 0, 0)
            self.back = [
                [
                    place.push(self.final.at[j, fz], self.landed.at[mine], place.member((fz,) + self.flips(j)))
                    if (fz,) + self.flips(j) != (0, 0, 0)
                    else place.copy(self.final.at[j, fz], self.landed.at[mine])
                    for fz in (1, 0)
                ]
                for j in range(4)
            ]

    def flips(self, j):
        return ((1, 1), (1, 0), (0, 1), (0, 0))[j]

    def pick(self, j, x):
        if not self.columns:
            return self.total.at[:, x]
        flip_y, flip_core = self.flips(j)
        return self.total.at[self.place.flipped("yl", flip_y) * 2 + self.place.flipped("core", flip_core), :, :, x]

    def start(self):
        for j in range(self.chunks):
            self.along_x[j].start()
            self.kept[j].start()

    def steps(self):
        def first(j):
            self.kept[j].wait()
            self.along_x[j].wait_recv()
            there = 1 - self.place.zh
            self.zout[j] = (self.own[j, there].astype(F32) + self.xin[j, there].astype(F32)).astype(BF16)
            self.along_z[j].start()

        def second(j):
            self.along_z[j].wait_recv()
            here = self.place.zh
            total = self.own[j, here].astype(F32) + self.xin[j, here].astype(F32) + self.zin[j].astype(F32)
            if not self.columns:
                self.outs[0][...] = total
                return
            zl = self.place.zl
            for i, fz in enumerate((1, 0)):
                row = 1 - zl if fz else zl
                self.final[j, fz] = (
                    self.own[j, here, row].astype(F32) + self.xin[j, here, row].astype(F32) + self.zin[j, row].astype(F32)
                ).astype(BF16)
                self.back[j][i].start()

        steps = [functools.partial(first, 0)]
        for j in range(1, self.chunks):
            steps += [functools.partial(first, j), functools.partial(second, j - 1)]
        return steps + [functools.partial(second, self.chunks - 1)]

    def finish(self):
        if self.columns:
            for copies in self.back:
                for copy in copies:
                    if copy is self.back[3][1]:
                        copy.wait()
                    else:
                        copy.wait_recv()
            shards_to(self.landed, self.outs)


def loop(count, body):
    def step(i, carry):
        body(i)
        return carry

    lax.fori_loop(0, count, step, 0)


def tile(i, width=TILE):
    return pl.ds(pl.multiple_of(i * width, width), width)


def dot(left, right):
    return jnp.dot(left, right, preferred_element_type=F32)


def dot_cols(left, right):
    return lax.dot_general(left, right, (((1,), (1,)), ((), ())), preferred_element_type=F32)


def dot_rows(left, right):
    return lax.dot_general(left, right, (((0,), (0,)), ((), ())), preferred_element_type=F32)


def swap_half(values):
    return pltpu.roll(values, LANES // 2, 1)


class Halo:
    def __init__(self, place, buffer, edge, halo, forward):
        x, zh, count = place.x, place.zh, lax.axis_size("x")
        first, final = x == 0, x == count - 1
        low, high = pl.ds(0, 4), pl.ds(4, 4)
        lead = len(buffer.shape) - 3
        lead = (slice(None),) * lead

        def at(blocks, rows):
            return buffer.at[lead + (blocks, rows)]

        every = pl.ds(0, 8)
        step = lax.rem(x + 1, count) if forward else lax.rem(x + count - 1, count)
        if forward:
            within, turn, beyond = jnp.logical_not(final), final, jnp.logical_and(final, zh == 0)
            into, turned, entered = jnp.logical_not(first), first, jnp.logical_and(first, zh == 1)
            sent, landing = low, high
        else:
            within, turn, beyond = jnp.logical_not(first), first, jnp.logical_and(first, zh == 1)
            into, turned, entered = jnp.logical_not(final), final, jnp.logical_and(final, zh == 0)
            sent, landing = high, low
        copies = [
            place.push(at(every, edge), at(every, halo), {"x": step}, False),
            place.push(at(sent, edge), at(landing, halo), {"x": step}, False),
            place.push(at(landing, edge), at(sent, halo), {"x": step, "zh": 1 - zh}, False),
        ]
        self.sends = list(zip((within, turn, beyond), copies))
        self.lands = list(zip((into, turned, entered), copies))
        self.unreached = jnp.logical_and(turned, jnp.logical_not(entered))
        self.open_end = lead + (sent, halo)
        self.buffer = buffer

    def start(self):
        for condition, copy in self.sends:
            pl.when(condition)(copy.start)

        @pl.when(self.unreached)
        def _():
            shape = self.buffer.at[self.open_end].shape
            self.buffer[self.open_end] = jnp.zeros(shape, self.buffer.dtype)

    def wait_recv(self):
        for condition, copy in self.lands:
            pl.when(condition)(copy.wait_recv)

    def wait_send(self):
        for condition, copy in self.sends:
            pl.when(condition)(copy.wait_send)


def phase_kernel(kind, plan, *refs):
    back = kind in ("ffn_back", "conv_back")
    conv = kind in ("conv", "conv_back")
    refs = list(refs)

    def take(count):
        taken = refs[:count]
        del refs[:count]
        return taken

    ref = dict(zip(OWN_IN[kind], take(len(OWN_IN[kind]))))
    loads = dict(zip(GROUP_IN[kind], take(len(GROUP_IN[kind]))))
    mine_refs, total_refs = take(plan["mine"]), take(len(plan["groups"]))
    ref.update(zip(OWN_OUT[kind], take(len(OWN_OUT[kind]))))
    saves = dict(zip(GROUP_OUT[kind], take(len(GROUP_OUT[kind]))))
    whole_outs = take(plan["mine"])
    total_outs = [take(count) for count in plan["groups"]]
    buffer = dict(zip(plan["buffers"], take(len(plan["buffers"]))))
    whole, part, sib, yin, yout, zin, zout = take(7)
    scratch = [take(6 if len(total.shape) == 6 else 4) for total in total_refs]
    place = Place(*take(3))
    rank, push = place.rank, place.push
    mine = ref["mine"]
    tokens, features = mine.shape
    half = tokens // HALVES
    halves = [pl.ds(h * half, half) for h in range(HALVES)]
    to_sibling, to_y, to_z = (place.beside(axis) for axis in ("core", "yl", "zl"))
    chips = ((0, 0), (1, 0), (0, 1), (1, 1))
    own, beside_z, beside_y, corner = (rank(*chip, 0) for chip in chips)

    loading = {}
    for name, source in loads.items():
        target = buffer[name]
        if target.shape != source.shape:
            target[source.shape[0] :] = jnp.zeros((target.shape[0] - source.shape[0],) + target.shape[1:], BF16)
            target = target.at[: source.shape[0]]
        loading[name] = place.copy(source, target)
        loading[name].start()
    saving = []

    def save(name, source):
        saving.append(place.copy(source, saves[name]))
        saving[-1].start()

    def loaded(*names):
        for name in names:
            loading[name].wait()

    barrier = pltpu.get_barrier_semaphore()
    partners = [to_sibling, to_y, to_z]
    if whole_outs or total_refs:
        partners += [place.beside("zh"), place.beside("x")]
    if any(len(total.shape) == 6 for total in total_refs):
        partners += [place.member(flips) for flips in FLIPS if sum(flips) > 1]
    x, zh, x_size = place.x, place.zh, lax.axis_size("x")
    expected = len(partners)
    if conv:
        partners += [{"x": lax.rem(x + 1, x_size)}, {"x": lax.rem(x + x_size - 1, x_size)}]
        at_turn = jnp.logical_or(
            jnp.logical_and(x == x_size - 1, zh == 0), jnp.logical_and(x == 0, zh == 1)
        )
        across = {"x": jnp.where(x == 0, x_size - 1, 0), "zh": 1 - zh}

        @pl.when(at_turn)
        def _():
            pl.semaphore_signal(barrier, inc=1, device_id=across, device_id_type=MESH)

        expected = len(partners) + jnp.where(at_turn, 1, 0)
    for partner in partners:
        pl.semaphore_signal(barrier, inc=1, device_id=partner, device_id_type=MESH)
    pl.semaphore_wait(barrier, expected)

    def sends(src, at, device):
        return [push(src.at[at, rows] if src is whole else src.at[rows], whole.at[at, rows], device) for rows in halves]

    from_z, from_y, own_to_core = sends(mine, own, to_z), sends(mine, own, to_y), sends(mine, own, to_sibling)
    from_corner = sends(whole, beside_z, to_y)
    z_to_core, y_to_core, corner_to_core = (sends(whole, at, to_sibling) for at in (beside_z, beside_y, corner))
    own_place = place.copy(mine, whole.at[own])
    own_place.start()
    for h in range(HALVES):
        for copies in (from_z, from_y, own_to_core):
            copies[h].start()

    gather_list = [Gather(place, *group) for group in zip(mine_refs, whole_outs)]
    reduce_list = [Reduce(place, *group) for group in zip(total_refs, total_outs, scratch)]
    for item in gather_list + reduce_list:
        item.start()
    steps = interleaved([item.steps() for item in gather_list + reduce_list])
    done = [0, len(steps)]

    def steps_until(share):
        while done[0] < int(share * done[1]):
            steps[done[0]]()
            done[0] += 1

    def landed(copies):
        for copy in copies:
            copy.wait_recv()

    def pair(chip):
        return pl.ds(rank(*chip, 0) - place.core, 2)

    def rows_of(values):
        return values.reshape(2 * tokens, values.shape[-1])

    def blocks_of(values):
        return values.reshape(2, tokens, values.shape[-1])

    def conv_first(chip):
        at = pair(chip)

        def columns(j):
            buffer["joint"][at, :, tile(j)] = blocks_of(dot(rows_of(whole[at]), buffer["in_w"][:, tile(j)]))

        loop(2, columns)
        low = 2 * TILE
        buffer["joint"][at, :, low:] = blocks_of(dot(rows_of(whole[at]), buffer["in_w"][:, low:]))
        joint = buffer["joint"]
        here = pl.ds(HALO, tokens)
        buffer["carried"][at, here, :LANES] = joint[at, :, :LANES] * joint[at, :, 2 * LANES : 3 * LANES]
        buffer["carried"][at, here, LANES:] = joint[at, :, 3 * LANES : 4 * LANES] * joint[at, :, 4 * LANES :]

    def conv_second(chip, j):
        at = pair(chip)
        return dot(rows_of(buffer["gated"][at]), buffer["out_w"][:, tile(j)])

    def c_columns(b, lane):
        if lane == 0:
            return buffer["joint"][b, :, LANES : 2 * LANES]
        return swap_half(buffer["joint"][b, :, 3 * LANES : 4 * LANES])

    def conv_between():
        carried = buffer["carried"]
        halo = Halo(place, carried, pl.ds(tokens, HALO), pl.ds(0, HALO), True)
        halo.start()
        save("joint", buffer["joint"])
        save("whole", whole)
        halo.wait_recv()
        taps = ref["taps"]

        def block(b):
            keep_one, keep_two = ref["keep"][0, b], ref["keep"][1, b]
            for lane in (0, LANES):
                lanes = slice(lane, lane + LANES)
                mixed = (
                    taps[0:1, lanes] * carried[b, HALO - 2 : HALO - 2 + tokens, lanes] * keep_two
                    + taps[1:2, lanes] * carried[b, HALO - 1 : HALO - 1 + tokens, lanes] * keep_one
                    + taps[2:3, lanes] * carried[b, HALO : HALO + tokens, lanes]
                )
                buffer["mixed"][b, :, lanes] = mixed
                buffer["gated"][b, :, lanes] = (c_columns(b, lane) * mixed).astype(BF16)

        loop(8, block)
        halo.wait_send()
        for name in ("carried", "mixed", "gated"):
            save(name, buffer[name])

    def ffn_first(chip):
        at = pair(chip)
        main = buffer["gate_up"].shape[2] // (2 * LANES) * LANES

        def columns(j):
            gate = dot(rows_of(whole[at]), buffer["both_w"][:, tile(j)])
            up = dot(rows_of(whole[at]), buffer["both_w"][:, pl.ds(pl.multiple_of(main + j * TILE, TILE), TILE)])
            buffer["gate_up"][at, :, tile(j)] = blocks_of(gate)
            buffer["gate_up"][at, :, pl.ds(pl.multiple_of(main + j * TILE, TILE), TILE)] = blocks_of(up)
            buffer["hidden"][at, :, tile(j)] = blocks_of((gate * jax.nn.sigmoid(gate) * up).astype(BF16))

        loop(main // TILE, columns)
        both = dot(rows_of(whole[at]), buffer["both_w"][:, 2 * main :])
        buffer["gate_up"][at, :, 2 * main :] = blocks_of(both)
        lane = lax.broadcasted_iota(jnp.int32, both.shape, 1)
        hidden = jnp.where(lane < LANES // 2, both * jax.nn.sigmoid(both) * swap_half(both), 0.0)
        buffer["hidden"][at, :, main:] = blocks_of(hidden.astype(BF16))

    def ffn_second(chip, j):
        return dot(rows_of(buffer["hidden"][pair(chip)]), buffer["down_w"][:, tile(j)])

    def ffn_back_first(chip):
        at = pair(chip)
        main = buffer["gate_up"].shape[2] // (2 * LANES) * LANES

        def grads(grad_hidden, gate, up):
            sigmoid = jax.nn.sigmoid(gate)
            return grad_hidden * up * sigmoid * (1.0 + gate * (1.0 - sigmoid)), grad_hidden * gate * sigmoid

        def columns(j):
            ups = pl.ds(pl.multiple_of(main + j * TILE, TILE), TILE)
            grad_hidden = dot_cols(rows_of(whole[at]), buffer["down_w"][tile(j), :])
            gate, up = (rows_of(buffer["gate_up"][at, :, lanes]) for lanes in (tile(j), ups))
            grad_gate, grad_up = grads(grad_hidden, gate, up)
            buffer["grad_gate_up"][at, :, tile(j)] = blocks_of(grad_gate.astype(BF16))
            buffer["grad_gate_up"][at, :, ups] = blocks_of(grad_up.astype(BF16))

        loop(main // TILE, columns)
        grad_hidden = dot_cols(rows_of(whole[at]), buffer["down_w"][main:, :])
        both = rows_of(buffer["gate_up"][at, :, 2 * main :])
        grad_gate, grad_up = grads(grad_hidden, both, swap_half(both))
        buffer["grad_gate_up"][at, :, 2 * main :] = blocks_of((grad_gate + swap_half(grad_up)).astype(BF16))

    def ffn_back_second(chip, j):
        return dot_cols(rows_of(buffer["grad_gate_up"][pair(chip)]), buffer["both_w"][tile(j), :])

    def all_rows(values):
        return values.reshape(8 * tokens, values.shape[-1])

    def ffn_back_grads():
        def both_rows(j):
            left = all_rows(buffer["whole"][:, :, tile(j)])
            buffer["grad_both_w"][tile(j), :] = dot_rows(left, all_rows(buffer["grad_gate_up"][...])).astype(BF16)

        def down_rows(j):
            left = all_rows(buffer["hidden"][:, :, tile(j, LANES)])
            buffer["grad_down_w"][tile(j, LANES), :] = dot_rows(left, all_rows(whole[...])).astype(BF16)

        loop(features // TILE, both_rows)
        save("grad_both_w", buffer["grad_both_w"])
        loop(buffer["grad_down_w"].shape[0] // LANES, down_rows)
        save("grad_down_w", buffer["grad_down_w"].at[: saves["grad_down_w"].shape[0]])

    def conv_back_first(chip):
        at = pair(chip)
        buffer["grad_gated"][at] = blocks_of(dot_cols(rows_of(whole[at]), buffer["out_w"][...]))

    def conv_back_between():
        edges, carried, joint = buffer["edges"], buffer["carried"], buffer["joint"]
        taps = ref["taps"]
        grad_taps = ref["grad_taps"]
        grad_taps[...] = jnp.zeros_like(grad_taps)

        def block(b):
            keep_one, keep_two = ref["keep"][0, b], ref["keep"][1, b]
            for lane in (0, LANES):
                lanes = slice(lane, lane + LANES)
                grad_mixed = buffer["grad_gated"][b, :, lanes] * c_columns(b, lane)
                first_tap, second_tap = grad_mixed * keep_two, grad_mixed * keep_one
                edges[0, b, :tokens, lanes] = second_tap * taps[1:2, lanes]
                edges[1, b, :tokens, lanes] = first_tap * taps[0:1, lanes]
                buffer["grad_carried"][b, :, lanes] = grad_mixed * taps[2:3, lanes]
                for row, grad, back_by in ((0, first_tap, 2), (1, second_tap, 1), (2, grad_mixed, 0)):
                    tap_in = carried[b, HALO - back_by : HALO - back_by + tokens, lanes]
                    grad_taps[row : row + 1, lanes] += jnp.sum(grad * tap_in, axis=0, keepdims=True)

        loop(8, block)
        halo = Halo(place, edges, pl.ds(0, HALO), pl.ds(tokens, HALO), False)
        halo.start()
        halo.wait_recv()
        grad_joint = buffer["grad_joint"]

        def block_after(b):
            for lane in (0, LANES):
                lanes = slice(lane, lane + LANES)
                grad_carried = (
                    buffer["grad_carried"][b, :, lanes]
                    + edges[0, b, 1 : 1 + tokens, lanes]
                    + edges[1, b, 2 : 2 + tokens, lanes]
                )
                grad_c = buffer["grad_gated"][b, :, lanes] * buffer["mixed"][b, :, lanes]
                if lane == 0:
                    grad_joint[b, :, :LANES] = (grad_carried * joint[b, :, 2 * LANES : 3 * LANES]).astype(BF16)
                    grad_joint[b, :, LANES : 2 * LANES] = grad_c.astype(BF16)
                    grad_joint[b, :, 2 * LANES : 3 * LANES] = (grad_carried * joint[b, :, :LANES]).astype(BF16)
                else:
                    grad_b = grad_carried * joint[b, :, 4 * LANES :]
                    grad_joint[b, :, 3 * LANES : 4 * LANES] = (grad_b + swap_half(grad_c)).astype(BF16)
                    grad_joint[b, :, 4 * LANES :] = (grad_carried * joint[b, :, 3 * LANES : 4 * LANES]).astype(BF16)

        loop(8, block_after)
        halo.wait_send()

    def conv_back_second(chip, j):
        return dot_cols(rows_of(buffer["grad_joint"][pair(chip)]), buffer["in_w"][tile(j), :])

    def conv_back_grads():
        def in_rows(j):
            left = all_rows(buffer["whole"][:, :, tile(j)])
            buffer["grad_in_w"][tile(j), :] = dot_rows(left, all_rows(buffer["grad_joint"][...])).astype(BF16)

        def out_rows(j):
            left = all_rows(buffer["gated"][:, :, tile(j, LANES)])
            buffer["grad_out_w"][tile(j, LANES), :] = dot_rows(left, all_rows(whole[...])).astype(BF16)

        loop(features // TILE, in_rows)
        save("grad_in_w", buffer["grad_in_w"])
        loop(buffer["grad_out_w"].shape[0] // LANES, out_rows)
        save("grad_out_w", buffer["grad_out_w"].at[: saves["grad_out_w"].shape[0]])

    first = {"conv": conv_first, "ffn": ffn_first, "conv_back": conv_back_first, "ffn_back": ffn_back_first}[kind]
    second = {"conv": conv_second, "ffn": ffn_second, "conv_back": conv_back_second, "ffn_back": ffn_back_second}[kind]
    weight_names = ("in_w", "out_w") if conv else ("both_w", "down_w")

    own_place.wait()
    landed(own_to_core)
    loaded(*weight_names)
    if kind == "ffn_back":
        loaded("gate_up")
    first(chips[0])
    for h in range(HALVES):
        from_z[h].wait_recv()
        from_corner[h].start()
        z_to_core[h].start()
    for h in range(HALVES):
        from_y[h].wait_recv()
        y_to_core[h].start()
    landed(z_to_core)
    first(chips[1])
    landed(y_to_core)
    first(chips[2])
    steps_until(0.25)
    for h in range(HALVES):
        from_corner[h].wait_recv()
        corner_to_core[h].start()
    landed(corner_to_core)
    first(chips[3])
    if kind == "conv":
        conv_between()
    if kind == "conv_back":
        loaded("joint", "carried", "mixed")
        conv_back_between()
    if kind == "ffn":
        save("whole", whole)
        save("gate_up", buffer["gate_up"])
        save("hidden", buffer["hidden"])

    order = (chips[3], chips[2], chips[1], chips[0])
    sib_copies = [push(part.at[i, 1 - place.core], sib.at[i], to_sibling) for i in range(4)]
    y_copies = [[push(yout.at[i, rows], yin.at[i, rows], to_y) for rows in halves] for i in range(2)]
    z_copies = [push(zout.at[rows], zin.at[rows], to_z) for rows in halves]

    def multiply(i):
        def columns(j):
            part[i, :, :, tile(j)] = blocks_of(second(order[i], j).astype(BF16))

        loop(features // TILE, columns)
        sib_copies[i].start()

    def chip_sum(i, rows):
        return part[i, place.core, rows].astype(F32) + sib[i, rows].astype(F32)

    def to_y_side(i):
        sib_copies[i].wait_recv()
        for h, rows in enumerate(halves):
            yout[i, rows] = chip_sum(i, rows).astype(BF16)
            y_copies[i][h].start()

    multiply(0)
    multiply(1)
    to_y_side(0)
    multiply(2)
    to_y_side(1)
    multiply(3)
    steps_until(0.5)
    sib_copies[2].wait_recv()
    for h, rows in enumerate(halves):
        y_copies[0][h].wait_recv()
        zout[rows] = (chip_sum(2, rows) + yin[0, rows].astype(F32)).astype(BF16)
        z_copies[h].start()
    if kind == "ffn_back":
        loaded("whole", "hidden")
        ffn_back_grads()
    if kind == "conv_back":
        loaded("whole", "gated")
        conv_back_grads()
    steps_until(0.75)
    sib_copies[3].wait_recv()
    for h, rows in enumerate(halves):
        y_copies[1][h].wait_recv()
        z_copies[h].wait_recv()
        total = chip_sum(3, rows) + yin[1, rows].astype(F32) + zin[rows].astype(F32)
        stream = ref["stream"][rows]
        if not back:
            stream = stream + total
            ref["stream_next"][rows] = stream
            ref["next"][rows] = (stream * rms_scale(stream) * ref["gain"][...]).astype(BF16)
        else:
            scale = rms_scale(stream)
            gain_grad = jnp.sum(total * stream * scale, axis=0, keepdims=True)
            ref["gain_grad"][...] = gain_grad if h == 0 else ref["gain_grad"][...] + gain_grad
            scaled = total * ref["gain"][...]
            grad = (
                ref["grad"][rows]
                + scale * scaled
                - stream * (scale * scale * scale) * jnp.mean(scaled * stream, axis=-1, keepdims=True)
            )
            ref["grad_next"][rows] = grad
            ref["next"][rows] = grad.astype(BF16)
    steps_until(1)
    for item in gather_list + reduce_list:
        item.finish()
    for copy in saving:
        copy.wait()
    for copy in place.sent:
        copy.wait_send()


def phase(kind, own_in, group_in, use="", mine=(), totals=(), groups=()):
    tokens, features = own_in[0].shape
    inside = pl.BlockSpec(memory_space=pltpu.VMEM)
    anywhere = pl.BlockSpec(memory_space=pl.ANY)
    conv = kind in ("conv", "conv_back")
    names = dict(zip(GROUP_IN[kind], group_in))
    wide, tall = (names["in_w"], names["out_w"]) if conv else (names["both_w"], names["down_w"])
    columns, rows = wide.shape[1], tall.shape[0]
    rows_padded = -(-rows // LANES) * LANES
    block = (tokens, features)
    forms = {
        "in_w": (wide.shape, BF16),
        "both_w": (wide.shape, BF16),
        "out_w": ((rows_padded, features), BF16),
        "down_w": ((rows_padded, features), BF16),
        "whole": ((8,) + block, BF16),
        "joint": ((8, tokens, columns), F32),
        "gate_up": ((8, tokens, columns), F32),
        "carried": ((8, tokens + HALO, rows_padded), F32),
        "mixed": ((8, tokens, rows_padded), F32),
        "gated": ((8, tokens, rows_padded), BF16),
        "hidden": ((8, tokens, rows_padded), BF16),
        "stream_next": (block, F32),
        "grad_next": (block, F32),
        "next": (block, BF16),
        "gain_grad": ((1, features), F32),
        "grad_taps": ((HALO, rows_padded), F32),
        "grad_in_w": (wide.shape, BF16),
        "grad_both_w": (wide.shape, BF16),
        "grad_out_w": ((rows_padded, features), BF16),
        "grad_down_w": ((rows_padded, features), BF16),
        "grad_gated": ((8, tokens, rows_padded), F32),
        "grad_carried": ((8, tokens, rows_padded), F32),
        "edges": ((2, 8, tokens + HALO, rows_padded), F32),
        "grad_joint": ((8, tokens, columns), BF16),
        "grad_gate_up": ((8, tokens, columns), BF16),
    }
    buffers = {
        "conv": ("in_w", "out_w", "joint", "carried", "mixed", "gated"),
        "ffn": ("both_w", "down_w", "gate_up", "hidden"),
        "conv_back": GROUP_IN[kind] + ("grad_gated", "grad_carried", "edges", "grad_joint", "grad_in_w", "grad_out_w"),
        "ffn_back": GROUP_IN[kind] + ("grad_gate_up", "grad_both_w", "grad_down_w"),
    }[kind]
    reduced, reduce_scratch = reduce_shapes(totals, groups)
    outs = [(jax.ShapeDtypeStruct(*forms[name]), inside) for name in OWN_OUT[kind]]
    for name in GROUP_OUT[kind]:
        shape, dtype = forms[name]
        if name in ("grad_out_w", "grad_down_w"):
            shape = tall.shape
        outs.append((jax.ShapeDtypeStruct(shape, dtype), anywhere))
    outs += [(jax.ShapeDtypeStruct(whole_shape(array.shape), BF16), anywhere) for array in mine]
    outs += [(shape, inside) for shape in reduced]
    plan = {"mine": len(mine), "groups": groups, "buffers": buffers}
    name = kind + use
    return pl.pallas_call(
        functools.partial(phase_kernel, kind, plan),
        out_shape=[shape for shape, _ in outs],
        in_specs=[inside] * len(own_in) + [anywhere] * (len(group_in) + len(mine) + len(totals)),
        out_specs=[spec for _, spec in outs],
        scratch_shapes=[pltpu.VMEM(*forms[buffer]) for buffer in buffers]
        + [pltpu.VMEM((8,) + block, BF16), pltpu.VMEM((4, 2) + block, BF16), pltpu.VMEM((4,) + block, BF16)]
        + [pltpu.VMEM((2,) + block, BF16)] * 2
        + [pltpu.VMEM(block, BF16)] * 2
        + reduce_scratch
        + [pltpu.SemaphoreType.DMA((SEMAPHORES,))] * 3,
        compiler_params=pltpu.CompilerParams(
            collective_id=COLLECTIVE_ID[name], has_side_effects=True, vmem_limit_bytes=60 << 20
        ),
        name=name,
    )(*own_in, *group_in, *mine, *totals)


def sizes_of(axes):
    return tuple(lax.axis_size(axis) for axis in axes)


def split_owners(array, dim):
    owners = sizes_of(OWNERS)
    count = 1
    for size in owners:
        count *= size
    shape = array.shape
    return array.reshape(shape[:dim] + owners + (shape[dim] // count,) + shape[dim + 1 :])


def column_shards(weights):
    rows = weights[0].shape[0]
    mains, rests = [], []
    for weight in weights:
        parts = split_owners(weight, 1).transpose(5, 2, 3, 0, 1, 4, 6, 7).reshape(8, rows, -1)
        main = parts.shape[2] // LANES * LANES
        mains.append(parts[:, :, :main])
        rests.append(parts[:, :, main:])
    shards = jnp.concatenate(mains + rests, axis=2)
    return jnp.pad(shards, ((0, 0), (0, 0), (0, -shards.shape[2] % LANES)))


def column_whole(shards, groups, width):
    rows = shards.shape[1]
    yh, yl, core, zh, zl, x = sizes_of(OWNERS)
    wholes = []
    for group in range(groups):
        part = jnp.concatenate(
            [shards[..., a:b] for a, b in pieces_of(groups, width, group, 0, width)], axis=-1
        ).reshape(zl, yl, core, rows, yh, zh, x, -1)
        wholes.append(part.transpose(3, 4, 1, 2, 5, 0, 6, 7).reshape(rows, -1))
    return wholes


def gather_columns(shards):
    mine = lax.all_to_all(shards, TP, split_axis=0, concat_axis=0, tiled=True)
    whole = lax.all_gather(mine, DP, axis=0, tiled=False)
    yh, yl, core, zh, zl, x = sizes_of(OWNERS)
    rows, columns = shards.shape[1:]
    whole = whole.reshape(yh, zh, x, zl, yl, core, rows, columns)
    return whole.transpose(0, 4, 5, 1, 3, 2, 6, 7).reshape(-1, columns)


def scatter_columns(total):
    yh, yl, core, zh, zl, x = sizes_of(OWNERS)
    columns = total.shape[1]
    parts = split_owners(total, 0).transpose(0, 3, 5, 4, 1, 2, 6, 7)
    parts = parts.reshape(yh * zh * x, -1, columns)
    mine = lax.psum_scatter(parts, DP, scatter_dimension=0, tiled=False)
    mine = mine.reshape(8, -1, columns)
    return lax.all_to_all(mine, TP, split_axis=0, concat_axis=0, tiled=True)


def tap_masks(starts, token_count):
    zh, x, x_size = lax.axis_index("zh"), lax.axis_index("x"), lax.axis_size("x")
    blocks = (zh * 2 + jnp.arange(2, dtype=jnp.int32)) * x_size + x
    places = blocks[:, None] * token_count + jnp.arange(token_count, dtype=jnp.int32)

    def segment_of(where):
        return jnp.sum((starts[None, :, None, :] <= where[:, None, :, None]).astype(jnp.int32), axis=3)

    own_segment = segment_of(places)
    keep_one = (segment_of(places - 1) == own_segment).astype(F32)
    keep_two = (segment_of(places - 2) == own_segment).astype(F32)
    return keep_one.reshape(8, token_count, 1), keep_two.reshape(8, token_count, 1)


def local(stream_in, doc_starts, norm_mix, in_proj, conv_taps, out_proj, norm_ffn, w_gate, w_up, w_down, grad_out):
    _, token_count, features = stream_in.shape
    layers = norm_mix.shape[0]
    own_kernels = sizes_of(DP) == (1, 2, 2)
    stream = stream_in.reshape(-1, features)
    grad_stream = grad_out.reshape(-1, features)
    small = jnp.concatenate([norm_mix[:, None], norm_ffn[:, None], conv_taps.transpose(0, 2, 1)], axis=1)
    small = small.astype(BF16).astype(F32)
    owned = small.shape[2]
    in_w, both_w, out_w, down_w = ([None] * layers for _ in range(4))

    def rows_of(weight):
        return weight.reshape(-1, weight.shape[-1])

    if own_kernels:
        packed = jnp.zeros((16, LANES), F32).at[: 5 * layers, :owned].set(small.reshape(-1, owned))
        packed = packed.at[15, : doc_starts.shape[1]].set(doc_starts[0].astype(F32))
        spread, mine, rounded, wholes = prepare(packed, in_proj, w_gate, w_up, out_proj, w_down)
        in_w[0], out_w[0], down_w[0] = (rows_of(whole) for whole in wholes)
        params = spread[:, : 5 * layers, :owned].transpose(1, 0, 2)
        gains = params.reshape(layers, 5, 1, -1)[:, :2]
        params = params.reshape(layers, 5, 4, 2, 2, 2, owned)[:, 2:]
        others = lax.axis_index("yl") * 2 + lax.axis_index("core")
        params = lax.dynamic_index_in_dim(params, others, 2, False)
        taps_all = lax.dynamic_index_in_dim(params, lax.axis_index("zl"), 3, False).reshape(layers, 3, -1)
        starts = spread.reshape(4, 8, 16, LANES)[:, 0, 15, : doc_starts.shape[1]].astype(jnp.int32)
    else:
        starts = lax.all_gather(doc_starts, ("yl", "core"), axis=0, tiled=True)
        small = small.astype(BF16)
        gains = lax.all_gather(small[:, :2], OWNERS, axis=2, tiled=True).astype(F32)[:, :, None]
        taps_all = lax.all_gather(small[:, 2:], DP, axis=2, tiled=True).astype(F32)
        for layer in range(layers):
            in_w[layer] = gather_columns(column_shards(jnp.split(in_proj[layer].astype(BF16), 3, axis=1)))
            both_w[layer] = gather_columns(column_shards([w_gate[layer].astype(BF16), w_up[layer].astype(BF16)]))
            out_w[layer] = lax.all_gather(out_proj[layer].astype(BF16), DP, axis=0, tiled=True)
            down_w[layer] = lax.all_gather(w_down[layer].astype(BF16), DP, axis=0, tiled=True)
    channels = taps_all.shape[2]
    taps_all = jnp.pad(taps_all, ((0, 0), (0, HALO - 3), (0, -channels % LANES)))
    keep = jnp.stack(tap_masks(starts, token_count))

    saved = []
    normed = (stream * rms_scale(stream) * gains[0, 0]).astype(BF16)
    for layer in range(layers):
        moved = (mine[2 * layer + 1],) if own_kernels else ()
        middle, normed, *kept, = phase(
            "conv", (normed, stream, gains[layer, 1], taps_all[layer], keep), (in_w[layer], out_w[layer]), mine=moved
        )
        if own_kernels:
            both_w[layer] = rows_of(kept.pop())
        if layer + 1 < layers and own_kernels:
            moved, use = (mine[2 * layer + 2], rounded[2 * layer + 2], rounded[2 * layer + 3]), "_moving"
        else:
            moved, use = (), ""
        gain = gains[min(layer + 1, layers - 1), 0]
        after, normed, *kept_ffn = phase("ffn", (normed, middle, gain), (both_w[layer], down_w[layer]), use, mine=moved)
        if moved:
            in_w[layer + 1], out_w[layer + 1], down_w[layer + 1] = (rows_of(whole) for whole in kept_ffn[3:])
        saved.append((stream, middle, kept, kept_ffn[:3]))
        stream = after

    def by_owner(grad):
        return grad.reshape(4, 2, 2, 2, -1, grad.shape[1])

    def by_part(grad):
        return grad.reshape(2, 2, -1, grad.shape[1])

    pieces = [None] * layers
    waiting, groups = (), ()
    sums = [[] for _ in range(layers)]
    rounded_grad = grad_stream.astype(BF16)
    for layer in reversed(range(layers)):
        source, middle, kept, kept_ffn = saved[layer]
        grad_middle, grad_gain_ffn, rounded_grad, grad_both, grad_down, *results = phase(
            "ffn_back", (rounded_grad, grad_stream, middle, gains[layer, 1]), (both_w[layer], down_w[layer], *kept_ffn),
            "_moving" if waiting else "", totals=waiting, groups=groups,
        )
        if waiting:
            sums[layer + 1] += results
        waiting, groups = ((by_owner(grad_both),), (2,)) if own_kernels else ((), ())
        grad_stream, grad_gain_mix, rounded_grad, grad_taps, grad_in, grad_out, *results = phase(
            "conv_back", (rounded_grad, grad_middle, source, gains[layer, 0], taps_all[layer], keep),
            (in_w[layer], out_w[layer], *kept), totals=waiting, groups=groups,
        )
        if own_kernels:
            sums[layer] += results
            waiting, groups = (by_owner(grad_in), by_part(grad_out), by_part(grad_down)), (3, 1, 1)
        else:
            sums[layer] = column_whole(scatter_columns(grad_both).astype(F32), 2, down_w[layer].shape[0])
            sums[layer] += column_whole(scatter_columns(grad_in).astype(F32), 3, out_w[layer].shape[0])
            sums[layer] += [
                lax.psum_scatter(grad, DP, scatter_dimension=0, tiled=True).astype(F32) for grad in (grad_out, grad_down)
            ]
        pieces[layer] = (grad_gain_mix, grad_gain_ffn, grad_taps[:3, :channels])
    gain_grads = jnp.stack([jnp.concatenate(p[:2]) for p in pieces])
    tap_grads = jnp.stack([p[2] for p in pieces])
    if own_kernels:
        slabs = gain_grads.reshape(2 * layers, 32, owned).transpose(1, 0, 2)
        slabs = jnp.pad(slabs, ((0, 0), (0, 0), (0, LANES - owned)))
        taps = tap_grads.reshape(3 * layers, 2, 1, 2, owned).transpose(1, 2, 3, 0, 4)
        taps = jnp.pad(taps, ((0, 0), (0, 0), (0, 0), (0, 0), (0, LANES - owned)))
        same = (jnp.arange(4) == others)[:, None, None, None, None, None]
        same = same & (jnp.arange(2) == lax.axis_index("zl"))[None, None, :, None, None, None]
        taps = jnp.where(same, taps[None], 0.0).reshape(32, 3 * layers, LANES)
        slabs = jnp.concatenate([slabs, taps, jnp.zeros((32, 16 - 5 * layers, LANES), F32)], axis=1)
        small_sums, *results = finish(slabs, waiting, groups)
        sums[0] += results
        small_sums = small_sums[:, :owned]
        gain_grads = small_sums[: 2 * layers].reshape(layers, 2, owned)
        tap_grads = small_sums[2 * layers : 5 * layers].reshape(layers, 3, owned)
    else:
        gain_grads = lax.psum_scatter(gain_grads, OWNERS, scatter_dimension=2, tiled=True)
        gain_grads = gain_grads.reshape(layers, 2, -1)
        tap_grads = lax.psum_scatter(tap_grads, DP, scatter_dimension=2, tiled=True)
    return (
        stream[None],
        grad_stream[None],
        gain_grads[:, 0],
        jnp.stack([jnp.concatenate(s[2:5], axis=1) for s in sums]),
        tap_grads.transpose(0, 2, 1),
        jnp.stack([s[5] for s in sums]),
        gain_grads[:, 1],
        jnp.stack([s[0] for s in sums]),
        jnp.stack([s[1] for s in sums]),
        jnp.stack([s[6] for s in sums]),
    )


def solution(mesh):
    dp, seq = mesh.shape["dp"], mesh.shape["seq"]
    side = dp // 2
    split = Mesh(mesh.devices.reshape(side // 2, 2, 2, seq // side // 2, 2, side), OWNERS)
    token = P(ROW_AXES, SEQ_AXES, None)
    vector = P(None, OWNERS)
    matrix = P(None, OWNERS, None)
    return jax.shard_map(
        local,
        mesh=split,
        in_specs=(token, P(ROW_AXES, None), vector, matrix, matrix, matrix, vector, matrix, matrix, matrix, token),
        out_specs=(token, token, vector, matrix, matrix, matrix, vector, matrix, matrix, matrix),
        check_vma=False,
    )
```

```python
import functools
import itertools

import jax
import jax.numpy as jnp
from jax import lax
from jax.experimental import pallas as pl
from jax.experimental.pallas import tpu as pltpu
from jax.sharding import Mesh, PartitionSpec as P

EPSILON = 1e-05
TP = ("zl", "yl", "core")
DP = ("yh", "zh", "x")
ROW_AXES = ("yh", "yl", "core")
SEQ_AXES = ("zh", "zl", "x")
OWNERS = ROW_AXES + SEQ_AXES
BF16 = jnp.bfloat16
F32 = jnp.float32
MESH = pl.DeviceIdType.MESH
HALVES = 2
COLLECTIVE_ID = {"prepare": 0, "forward": 1, "backward": 2}
FLIPS = ((1, 1, 1), (1, 1, 0), (1, 0, 1), (1, 0, 0), (0, 1, 1), (0, 1, 0), (0, 0, 1))
OTHERS = tuple(itertools.product((0, 1), repeat=5))[1:]
OTHER_AXES = ("yl", "core", "zh", "zl", "x")
SEMAPHORES = 288
FLYING = 2
LANES = 128
TILE = 256
HALO = 8


def rms_scale(values):
    return lax.rsqrt(jnp.mean(values * values, axis=-1, keepdims=True) + EPSILON)


class Place:
    def __init__(self, send, recv, local):
        self.zl, self.yl, self.core = (lax.axis_index(axis) for axis in TP)
        self.zh, self.x = lax.axis_index("zh"), lax.axis_index("x")
        self.send, self.recv, self.local = send, recv, local
        self.remote_count = self.local_count = 0
        self.sent = []

    def rank(self, flip_z, flip_y, flip_core):
        return self.flipped("zl", flip_z) * 4 + self.flipped("yl", flip_y) * 2 + self.flipped("core", flip_core)

    def flipped(self, axis, flip):
        return 1 - getattr(self, axis) if flip else getattr(self, axis)

    def member(self, flips):
        return {axis: 1 - getattr(self, axis) for axis, flip in zip(TP, flips) if flip}

    def beside(self, axis):
        return {axis: 1 - getattr(self, axis)}

    def owner(self, flips=(0,) * 5):
        index = 0
        for axis, flip in zip(OTHER_AXES, flips):
            index = index * 2 + self.flipped(axis, flip)
        return index

    def push(self, src, dst, device, kept=True):
        index = self.remote_count
        self.remote_count += 1
        assert index < SEMAPHORES
        copy = pltpu.make_async_remote_copy(
            src_ref=src, dst_ref=dst, send_sem=self.send.at[index], recv_sem=self.recv.at[index],
            device_id=device, device_id_type=MESH,
        )
        if kept:
            self.sent.append(copy)
        return copy

    def copy(self, src, dst):
        index = self.local_count
        self.local_count += 1
        return pltpu.make_async_copy(src, dst, self.local.at[index])


def pieces_of(groups, width, group, low, high):
    main = width // LANES * LANES
    rest = width - main
    ranges = []
    if low < main:
        ranges.append((group * main + low, group * main + min(high, main)))
    if high > main:
        start = groups * main + group * rest - main
        ranges.append((start + max(low, main), start + high))
    return ranges


def shards_from(weights, out):
    width = weights[0].shape[1] // 8
    block = width // 4
    main = width // LANES * LANES
    rest = width - main
    for group, weight in enumerate(weights):
        for member in range(8):
            zl, others = member // 4, member % 4
            starts = [((others * 2 + zh) * 4 + zl * 2 + x) * block for zh in range(2) for x in range(2)]
            values = jnp.concatenate([weight[:, start : start + block] for start in starts], axis=1).astype(BF16)
            out[member, :, group * main : (group + 1) * main] = values[:, :main]
            if rest:
                low = len(weights) * main + group * rest
                out[member, :, low : low + rest] = values[:, main:]
    pad = out.shape[2] - len(weights) * width
    if pad:
        out[:, :, len(weights) * width :] = jnp.zeros((8, out.shape[1], pad), BF16)


def shards_to(shards, outs):
    groups, width = len(outs), outs[0].shape[1] // 8
    block = width // 4
    for group, out in enumerate(outs):
        for others in range(4):
            for zh in range(2):
                values = []
                for zl in range(2):
                    for x in range(2):
                        low = (zh * 2 + x) * block
                        for start, end in pieces_of(groups, width, group, low, low + block):
                            values.append(shards[zl * 4 + others, :, start:end].astype(F32))
                start = (others * 2 + zh) * 4 * block
                out[:, start : start + 4 * block] = jnp.concatenate(values, axis=1)


def every_other(place):
    return [
        ({axis: place.flipped(axis, 1) for axis, flip in zip(OTHER_AXES, flips) if flip}, flips) for flips in OTHERS
    ]


def prepare_kernel(layers, small, in_proj, gate, up, out_proj, down, *refs):
    refs = list(refs)

    def take(count):
        taken = refs[:count]
        del refs[:count]
        return taken

    (spread,), mine, rounded, wholes = take(1), take(2 * layers), take(2 * layers), take(2)
    shards, (send, recv, local) = take(2 * layers), take(3)
    place = Place(send, recv, local)
    barrier = pltpu.get_barrier_semaphore()
    for device, _ in every_other(place):
        pl.semaphore_signal(barrier, inc=1, device_id=device, device_id_type=MESH)
    width = in_proj.shape[2] // 3

    def cut(layer, which):
        if which == 0:
            shards_from([in_proj.at[layer, :, i * width : (i + 1) * width] for i in range(3)], shards[2 * layer])
        else:
            shards_from([gate.at[layer], up.at[layer]], shards[2 * layer + 1])

    def scatter(index):
        here = mine[index].at[place.yl * 2 + place.core, place.zl]
        copies = [place.push(shards[index].at[place.rank(*flips)], here, place.member(flips)) for flips in FLIPS]
        copies.append(place.copy(shards[index].at[place.rank(0, 0, 0)], here))
        for copy in copies:
            copy.start()
        return copies

    def landed(copies):
        for copy in copies[:-1]:
            copy.wait_recv()
        copies[-1].wait()

    cut(0, 0)
    for layer in range(layers):
        rounded[2 * layer][...] = out_proj[layer].astype(BF16)
        rounded[2 * layer + 1][...] = down[layer].astype(BF16)
    pl.semaphore_wait(barrier, len(OTHERS))
    kept = place.copy(small, spread.at[place.owner()])
    kept.start()
    spreads = [place.push(small, spread.at[place.owner()], device) for device, _ in every_other(place)]
    first = scatter(0)
    for copy in spreads:
        copy.start()
    gathers = [Gather(place, own, whole) for own, whole in zip((mine[0], rounded[0]), wholes)]
    for gather in gathers[1:]:
        for launch, _ in gather.pairs():
            launch()
    cut(0, 1)
    landed(first)
    for launch, _ in gathers[0].pairs():
        launch()
    others = [scatter(1)]
    for layer in range(1, layers):
        for which in range(2):
            cut(layer, which)
            others.append(scatter(2 * layer + which))
    for gather in gathers[1:] + gathers[:1]:
        for _, land in gather.pairs():
            land()
    for copies in others:
        landed(copies)
    kept.wait()
    for copy in spreads:
        copy.wait_recv()
    for gather in gathers:
        gather.finish()
    for copy in place.sent:
        copy.wait_send()


def whole_shape(mine):
    return (4, 2, 2, 2) + mine[2:] if len(mine) == 4 else (2, 2) + mine


def prepare(small, in_proj, gate, up, out_proj, down):
    layers, rows, columns = in_proj.shape
    widths = (-(-columns // 8 // LANES) * LANES, gate.shape[2] // 4)
    inside = pl.BlockSpec(memory_space=pltpu.VMEM)
    anywhere = pl.BlockSpec(memory_space=pl.ANY)
    mine = [(4, 2, rows, width) for _ in range(layers) for width in widths]
    rounded = [array.shape[1:] for _ in range(layers) for array in (out_proj, down)]
    wholes = [whole_shape(shape) for shape in (mine[0], rounded[0])]
    outs = pl.pallas_call(
        functools.partial(prepare_kernel, layers),
        out_shape=[jax.ShapeDtypeStruct((32,) + small.shape, F32)]
        + [jax.ShapeDtypeStruct(shape, BF16) for shape in mine + rounded + wholes],
        in_specs=[inside] * 6,
        out_specs=[anywhere] * (1 + len(mine)) + [inside] * len(rounded) + [anywhere] * 2,
        scratch_shapes=[pltpu.VMEM((8, rows, width), BF16) for _ in range(layers) for width in widths]
        + [pltpu.SemaphoreType.DMA((SEMAPHORES,))] * 3,
        compiler_params=pltpu.CompilerParams(
            collective_id=COLLECTIVE_ID["prepare"], has_side_effects=True, vmem_limit_bytes=48 << 20
        ),
        name="prepare",
    )(small, in_proj, gate, up, out_proj, down)
    spread, outs = outs[0], outs[1:]
    return spread, outs[: len(mine)], outs[len(mine) : -2], outs[-2:]


class Gather:
    def __init__(self, place, mine, whole):
        x, own, other = place.x, place.zh, 1 - place.zh
        if len(whole.shape) == 6:
            parts = [
                (mine.at[c, zl], whole.at[c, own, zl, x], whole.at[c, other, zl, x])
                for c in range(4)
                for zl in range(2)
            ]
        else:
            count = whole.shape[2]
            size = 48 if count % 48 == 0 else count
            parts = [
                (mine.at[rows], whole.at[own, x, rows], whole.at[other, x, rows])
                for rows in (pl.ds(low, size) for low in range(0, count, size))
            ]
        self.along_z = [place.push(src, here, place.beside("zh")) for src, here, _ in parts]
        self.along_x = [place.push(src, here, place.beside("x")) for src, here, _ in parts]
        self.onward = [place.push(there, there, place.beside("x")) for _, _, there in parts]
        self.kept = [place.copy(src, here) for src, here, _ in parts]

    def pairs(self):
        def launch(c):
            self.along_z[c].start()
            self.along_x[c].start()
            self.kept[c].start()

        def land(c):
            self.along_z[c].wait_recv()
            self.onward[c].start()

        return [(functools.partial(launch, c), functools.partial(land, c)) for c in range(len(self.kept))]

    def finish(self):
        for c in range(len(self.kept)):
            self.along_x[c].wait_recv()
            self.onward[c].wait_recv()
            self.kept[c].wait()


class Reduce:
    def __init__(self, place, total, landing, deliver):
        self.columns = len(total.shape) == 6
        self.place, self.total, self.deliver = place, total, deliver
        self.xin, self.zout, self.zin, self.final = landing[:4]
        self.landed = landing[4] if self.columns else None
        x, zh, beside = place.x, place.zh, place.beside
        self.flips = FLIPS + ((0, 0, 0),)
        self.chunks = self.zin.shape[0]
        self.along_x = [
            [
                place.push(self.part(j, to_zh, 1 - x), self.xin.at[j, i], beside("x"), False)
                for i, to_zh in enumerate((1 - zh, zh))
            ]
            for j in range(self.chunks)
        ]
        self.along_z = [place.push(self.zout.at[j], self.zin.at[j], beside("zh"), False) for j in range(self.chunks)]
        if self.columns:
            here = self.landed.at[place.rank(0, 0, 0)]
            self.back = [place.push(self.final.at[j], here, place.member(flips), False) for j, flips in enumerate(FLIPS)]
            self.back.append(place.copy(self.final.at[7], here))

    def part(self, j, zh, x):
        if self.columns:
            flip_z, flip_y, flip_core = self.flips[j]
            place = self.place
            chunk = place.flipped("yl", flip_y) * 2 + place.flipped("core", flip_core)
            return self.total.at[chunk, zh, place.flipped("zl", flip_z), x]
        count = self.zin.shape[1]
        low = ((zh * 2 + x) * self.chunks + j) * count
        return self.total.at[pl.ds(pl.multiple_of(low, 16), count)]

    def start(self):
        for copies in self.along_x:
            for copy in copies:
                copy.start()

    def pairs(self):
        x, zh = self.place.x, self.place.zh

        def launch(j):
            for copy in self.along_x[j]:
                copy.wait_recv()
            self.zout[j] = (self.part(j, 1 - zh, x)[...].astype(F32) + self.xin[j, 0].astype(F32)).astype(BF16)
            self.along_z[j].start()

        def land(j):
            self.along_z[j].wait_recv()
            total = self.part(j, zh, x)[...].astype(F32) + self.xin[j, 1].astype(F32) + self.zin[j].astype(F32)
            if self.columns:
                self.final[j] = total.astype(BF16)
                self.back[j].start()
            else:
                count = self.zin.shape[1]
                self.final[j * count : (j + 1) * count] = total

        return [(functools.partial(launch, j), functools.partial(land, j)) for j in range(self.chunks)]

    def finish(self):
        if self.columns:
            for copy in self.back[:-1]:
                copy.wait_recv()
            self.back[-1].wait()
        sent = [copy for copies in self.along_x for copy in copies] + self.along_z
        for copy in sent + (self.back[:-1] if self.columns else []):
            copy.wait_send()
        self.deliver(self.landed if self.columns else self.final)


def landing_shapes(total):
    if len(total) == 6:
        rows = total[4:]
        return [((8, 2) + rows, BF16)] + [((8,) + rows, BF16)] * 4
    count = total[0] // 4
    size = 48 if count % 48 == 0 else count
    rows = (size,) + total[1:]
    chunks = (count // size,)
    return [(chunks + (2,) + rows, BF16), (chunks + rows, BF16), (chunks + rows, BF16), ((count,) + total[1:], F32)]


def loop(count, body):
    def step(i, carry):
        body(i)
        return carry

    lax.fori_loop(0, count, step, 0)


def tile(i, width=TILE):
    return pl.ds(pl.multiple_of(i * width, width), width)


def dot(left, right):
    return jnp.dot(left, right, preferred_element_type=F32)


def dot_cols(left, right):
    return lax.dot_general(left, right, (((1,), (1,)), ((), ())), preferred_element_type=F32)


def dot_rows(left, right):
    return lax.dot_general(left, right, (((0,), (0,)), ((), ())), preferred_element_type=F32)


def swap_half(values):
    return pltpu.roll(values, LANES // 2, 1)


class Halo:
    def __init__(self, place, buffer, edge, landing, forward):
        x, zh, count = place.x, place.zh, lax.axis_size("x")
        first, final = x == 0, x == count - 1
        low, high, every = pl.ds(0, 4), pl.ds(4, 4), pl.ds(0, 8)
        lead = (slice(None),) * (len(buffer.shape) - 3)
        step = lax.rem(x + 1, count) if forward else lax.rem(x + count - 1, count)
        if forward:
            within, turn, beyond = jnp.logical_not(final), final, jnp.logical_and(final, zh == 0)
            into, turned, entered = jnp.logical_not(first), first, jnp.logical_and(first, zh == 1)
            sent, landed = low, high
        else:
            within, turn, beyond = jnp.logical_not(first), first, jnp.logical_and(first, zh == 1)
            into, turned, entered = jnp.logical_not(final), final, jnp.logical_and(final, zh == 0)
            sent, landed = high, low

        def push(src, dst, device):
            return place.push(buffer.at[lead + (src, edge)], landing.at[lead + (dst,)], device, False)

        copies = [
            push(every, every, {"x": step}),
            push(sent, landed, {"x": step}),
            push(landed, sent, {"x": step, "zh": 1 - zh}),
        ]
        self.sends = list(zip((within, turn, beyond), copies))
        self.lands = list(zip((into, turned, entered), copies))
        self.unreached = jnp.logical_and(turned, jnp.logical_not(entered))
        self.landing, self.open_end = landing, lead + (sent,)

    def start(self):
        for condition, copy in self.sends:
            pl.when(condition)(copy.start)

        @pl.when(self.unreached)
        def _():
            shape = self.landing.at[self.open_end].shape
            self.landing[self.open_end] = jnp.zeros(shape, self.landing.dtype)

    def wait_recv(self):
        for condition, copy in self.lands:
            pl.when(condition)(copy.wait_recv)

    def wait_send(self):
        for condition, copy in self.sends:
            pl.when(condition)(copy.wait_send)


SAVED = ("conv_whole", "joint", "carried", "mixed", "gated", "ffn_whole", "gate_up", "hidden")
WEIGHTS = ("in_w", "out_w", "both_w", "down_w")


def forms_of(tokens, features, wide, tall, layers):
    channels, units = (-(-rows // LANES) * LANES for rows in tall)
    block = (tokens, features)
    return {
        "in_w": ((features, wide[0]), BF16),
        "both_w": ((features, wide[1]), BF16),
        "out_w": ((tall[0], features), BF16),
        "down_w": ((tall[1], features), BF16),
        "conv_whole": ((8,) + block, BF16),
        "ffn_whole": ((8,) + block, BF16),
        "joint": ((8, tokens, wide[0]), F32),
        "gate_up": ((8, tokens, wide[1]), F32),
        "carried": ((8, tokens + HALO, channels), F32),
        "mixed": ((8, tokens, channels), F32),
        "gated": ((8, tokens, channels), BF16),
        "hidden": ((8, tokens, units), BF16),
        "tall_w": ((units, features), BF16),
        "grad_rows": ((8, tokens, wide[1]), BF16),
        "grad_gated": ((8, tokens, channels), F32),
        "edges": ((2, 8, tokens + HALO, channels), F32),
        "heads": ((layers, 2, 8, HALO, channels), F32),
        "tails": ((layers, 8, HALO, channels), F32),
        "stream": (block, F32),
        "next": (block, BF16),
        "whole": ((2, 8) + block, BF16),
        "part": ((4, 2) + block, BF16),
        "sib": ((4,) + block, BF16),
        "yin": ((2,) + block, BF16),
        "yout": ((2,) + block, BF16),
        "zin": (block, BF16),
        "zout": (block, BF16),
        "grad_in_w": ((4, 2, 2, 2, features // 32, wide[0]), BF16),
        "grad_both_w": ((4, 2, 2, 2, features // 32, wide[1]), BF16),
        "grad_out_w": ((channels, features), BF16),
        "grad_down_w": ((units, features), BF16),
    }


class Pass:
    def __init__(self, place, buffers):
        self.place, self.buffers = place, buffers
        self.tokens, self.features = buffers["zin"].shape
        half = self.tokens // HALVES
        self.halves = [pl.ds(h * half, half) for h in range(HALVES)]
        self.chips = ((0, 0), (1, 0), (0, 1), (1, 1))
        self.phases = 0
        self.items, self.queue, self.flying = [], [], []
        self.saving, self.loading = [], {}

    def enter(self, more, barrier_all):
        place = self.place
        barrier = pltpu.get_barrier_semaphore()
        if barrier_all:
            partners = [device for device, _ in every_other(place)]
            expected = len(partners)
        else:
            x, zh, x_size = place.x, place.zh, lax.axis_size("x")
            partners = [place.beside(axis) for axis in ("core", "yl", "zl")] + more
            partners += [{"x": lax.rem(x + 1, x_size)}, {"x": lax.rem(x + x_size - 1, x_size)}]
            at_turn = jnp.logical_or(jnp.logical_and(x == x_size - 1, zh == 0), jnp.logical_and(x == 0, zh == 1))
            across = {"x": jnp.where(x == 0, x_size - 1, 0), "zh": 1 - zh}

            @pl.when(at_turn)
            def _():
                pl.semaphore_signal(barrier, inc=1, device_id=across, device_id_type=MESH)

            expected = len(partners) + jnp.where(at_turn, 1, 0)
        for partner in partners:
            pl.semaphore_signal(barrier, inc=1, device_id=partner, device_id_type=MESH)
        pl.semaphore_wait(barrier, expected)

    def begin(self, items):
        for item in items:
            item.left = len(item.pairs())
            self.queue += [(item,) + pair for pair in item.pairs()]
            self.items.append(item)

    def launch(self, count):
        for item, launch, land in self.queue[:count]:
            launch()
            self.flying.append((item, land))
        del self.queue[:count]

    def land(self, count):
        for item, land in self.flying[:count]:
            land()
            item.left -= 1
        del self.flying[:count]

    def step(self):
        if len(self.flying) >= FLYING:
            self.land(1)
        self.launch(1)

    def settle(self, items):
        for item in items:
            while any(queued is item for queued, _, _ in self.queue):
                self.launch(1)
            while item.left:
                self.land(1)
            item.finish()
            self.items.remove(item)

    def load(self, name, source, target):
        if target.shape != source.shape:
            rows = target.shape[0] - source.shape[0]
            target[source.shape[0] :] = jnp.zeros((rows,) + target.shape[1:], BF16)
            target = target.at[: source.shape[0]]
        self.loading[name] = self.place.copy(source, target)
        self.loading[name].start()

    def loaded(self, *names):
        for name in names:
            self.loading.pop(name).wait()

    def save(self, source, target):
        self.saving.append(self.place.copy(source, target))
        self.saving[-1].start()

    def saved(self):
        for copy in self.saving:
            copy.wait()
        self.saving = []

    def pair(self, chip):
        return pl.ds(self.place.rank(*chip, 0) - self.place.core, 2)

    def rows_of(self, values):
        return values.reshape(2 * self.tokens, values.shape[-1])

    def blocks_of(self, values):
        return values.reshape(2, self.tokens, values.shape[-1])

    def all_rows(self, values):
        return values.reshape(8 * self.tokens, values.shape[-1])

    def phase(self, mine, first, second, after, before_first=None, before_second=None, between=None, aside=None):
        place, buffers, halves, chips = self.place, self.buffers, self.halves, self.chips
        rank, sent = place.rank, []
        whole = buffers["whole"].at[self.phases % 2]
        self.phases += 1
        part, sib, yin, yout, zin, zout = (buffers[name] for name in ("part", "sib", "yin", "yout", "zin", "zout"))
        to_sibling, to_y, to_z = (place.beside(axis) for axis in ("core", "yl", "zl"))
        own, beside_z, beside_y, corner = (rank(*chip, 0) for chip in chips)

        def push(src, dst, device):
            sent.append(place.push(src, dst, device, False))
            return sent[-1]

        def sends(src, at, device):
            return [push(mine.at[rows] if src is None else src.at[at, rows], whole.at[at, rows], device) for rows in halves]

        def landed(copies):
            for copy in copies:
                copy.wait_recv()

        from_z, from_y, own_to_core = sends(None, own, to_z), sends(None, own, to_y), sends(None, own, to_sibling)
        from_corner = sends(whole, beside_z, to_y)
        z_to_core, y_to_core, corner_to_core = (sends(whole, at, to_sibling) for at in (beside_z, beside_y, corner))
        own_place = place.copy(mine, whole.at[own])
        own_place.start()
        for h in range(HALVES):
            for copies in (from_z, from_y, own_to_core):
                copies[h].start()
        self.step()
        if before_first is not None:
            before_first()
        own_place.wait()
        landed(own_to_core)
        first(whole, chips[0])
        for h in range(HALVES):
            from_z[h].wait_recv()
            from_corner[h].start()
            z_to_core[h].start()
        self.step()
        for h in range(HALVES):
            from_y[h].wait_recv()
            y_to_core[h].start()
        landed(z_to_core)
        first(whole, chips[1])
        self.step()
        landed(y_to_core)
        first(whole, chips[2])
        self.step()
        for h in range(HALVES):
            from_corner[h].wait_recv()
            corner_to_core[h].start()
        landed(corner_to_core)
        first(whole, chips[3])
        self.step()
        if between is not None:
            between(whole)
        if before_second is not None:
            before_second()

        order = (chips[3], chips[2], chips[1], chips[0])
        sib_copies = [push(part.at[i, 1 - place.core], sib.at[i], to_sibling) for i in range(4)]
        y_copies = [[push(yout.at[i, rows], yin.at[i, rows], to_y) for rows in halves] for i in range(2)]
        z_copies = [push(zout.at[rows], zin.at[rows], to_z) for rows in halves]

        def multiply(i):
            def columns(j):
                part[i, :, :, tile(j)] = self.blocks_of(second(order[i], j).astype(BF16))

            loop(self.features // TILE, columns)
            sib_copies[i].start()

        def chip_sum(i, rows):
            return part[i, place.core, rows].astype(F32) + sib[i, rows].astype(F32)

        def to_y_side(i):
            sib_copies[i].wait_recv()
            for h, rows in enumerate(halves):
                yout[i, rows] = chip_sum(i, rows).astype(BF16)
                y_copies[i][h].start()

        multiply(0)
        multiply(1)
        to_y_side(0)
        self.step()
        multiply(2)
        to_y_side(1)
        multiply(3)
        self.step()
        sib_copies[2].wait_recv()
        for h, rows in enumerate(halves):
            y_copies[0][h].wait_recv()
            zout[rows] = (chip_sum(2, rows) + yin[0, rows].astype(F32)).astype(BF16)
            z_copies[h].start()
        self.step()
        if aside is not None:
            aside(whole)
        self.step()
        sib_copies[3].wait_recv()
        for copy in sent:
            copy.wait_send()
        for h, rows in enumerate(halves):
            y_copies[1][h].wait_recv()
            z_copies[h].wait_recv()
            if h == HALVES - 1:
                self.step()
            after(h, rows, chip_sum(3, rows) + yin[1, rows].astype(F32) + zin[rows].astype(F32))
        self.step()


def c_columns(joint, b, lane):
    if lane == 0:
        return joint[b, :, LANES : 2 * LANES]
    return swap_half(joint[b, :, 3 * LANES : 4 * LANES])


def both_lanes():
    return [(lane, slice(lane, lane + LANES)) for lane in (0, LANES)]


def forward_kernel(plan, *refs):
    refs = list(refs)
    layers, moving, buffer_names = plan["layers"], plan["moving"], plan["buffers"]

    def take(count):
        taken = refs[:count]
        del refs[:count]
        return taken

    stream_in, gains, taps_ref, keep = take(4)
    weights = [dict(zip(WEIGHTS, take(2 if moving else 4))) for _ in range(1 if moving else layers)]
    mine = [take(4 if layer else 2) for layer in range(layers)] if moving else None
    stream_out, middles, sources = take(1)[0], take(layers), take(layers - 1)
    saves = [dict(zip(SAVED, take(len(SAVED)))) for _ in range(layers)]
    flat = []
    if moving:
        for layer in range(layers):
            names = WEIGHTS if layer else WEIGHTS[2:]
            wholes = dict(zip(names, take(len(names))))
            if layer:
                weights.append({})
            weights[layer].update(wholes)
    buffers = dict(zip(buffer_names, take(len(buffer_names))))
    place = Place(*take(3))
    run = Pass(place, buffers)
    tokens, features = run.tokens, run.features
    rows_of, blocks_of, pair = run.rows_of, run.blocks_of, run.pair
    joint, carried, mixed, gated = (buffers[name] for name in ("joint", "carried", "mixed", "gated"))
    gate_up, hidden = buffers["gate_up"], buffers["hidden"]
    in_w, out_w, both_w, down_w = (buffers["vmem_" + name] for name in WEIGHTS)
    main = gate_up.shape[2] // (2 * LANES) * LANES
    next_ref = buffers["next"]

    coming = {}

    def moves(layer, names):
        own = dict(zip(WEIGHTS if layer else WEIGHTS[2:], mine[layer]))
        for name in names:
            coming[layer, name] = Gather(place, own[name], weights[layer][name])
            run.begin([coming[layer, name]])

    def load(layer, names):
        for name in names:
            if (layer, name) in coming:
                run.settle([coming.pop((layer, name))])
            source, target = weights[layer][name], buffers["vmem_" + name]
            if len(source.shape) == 2:
                run.load(name, source, target)
                continue
            copies = []
            rows = source.shape[-2]
            lead = source.shape[:-2]
            for n, index in enumerate(itertools.product(*(range(size) for size in lead))):
                copies.append(place.copy(source.at[index], target.at[pl.ds(n * rows, rows)]))
                copies[-1].start()
            filled = rows * len(copies)
            if filled < target.shape[0]:
                target[filled:] = jnp.zeros((target.shape[0] - filled, target.shape[1]), BF16)
            run.loading[name] = Several(copies)

    def rounded(values, gain):
        return (values * rms_scale(values) * gain).astype(BF16)

    def conv(layer, stream):
        def before_first():
            load(layer, ("in_w",))
            run.loaded("in_w")

        def first(whole, chip):
            at = pair(chip)

            def columns(j):
                joint[at, :, tile(j)] = blocks_of(dot(rows_of(whole[at]), in_w[:, tile(j)]))

            loop(2, columns)
            joint[at, :, 2 * TILE :] = blocks_of(dot(rows_of(whole[at]), in_w[:, 2 * TILE :]))
            here = pl.ds(HALO, tokens)
            carried[at, here, :LANES] = joint[at, :, :LANES] * joint[at, :, 2 * LANES : 3 * LANES]
            carried[at, here, LANES:] = joint[at, :, 3 * LANES : 4 * LANES] * joint[at, :, 4 * LANES :]

        def between(whole):
            halo = Halo(place, carried, pl.ds(tokens, HALO), buffers["tails"].at[layer], True)
            halo.start()
            run.saved()
            run.save(joint, saves[layer]["joint"])
            run.save(whole, saves[layer]["conv_whole"])
            halo.wait_recv()
            carried[:, :HALO] = buffers["tails"][layer]

            def block(b):
                keep_one, keep_two = keep[0, b], keep[1, b]
                for lane, lanes in both_lanes():
                    result = (
                        taps_ref[layer, 0:1, lanes] * carried[b, HALO - 2 : HALO - 2 + tokens, lanes] * keep_two
                        + taps_ref[layer, 1:2, lanes] * carried[b, HALO - 1 : HALO - 1 + tokens, lanes] * keep_one
                        + taps_ref[layer, 2:3, lanes] * carried[b, HALO : HALO + tokens, lanes]
                    )
                    mixed[b, :, lanes] = result
                    gated[b, :, lanes] = (c_columns(joint, b, lane) * result).astype(BF16)

            loop(8, block)
            halo.wait_send()
            for name in ("carried", "mixed", "gated"):
                run.save(buffers[name], saves[layer][name])

        def second(chip, j):
            return dot(rows_of(gated[pair(chip)]), out_w[:, tile(j)])

        def after(h, rows, total):
            middle = stream[rows] + total
            middles[layer][rows] = middle
            next_ref[rows] = rounded(middle, gains[2 * layer + 1])

        def before_second():
            load(layer, ("out_w",))
            run.loaded("out_w")

        run.phase(next_ref, first, second, after, before_first, before_second, between)

    def ffn(layer):
        def before_first():
            load(layer, ("both_w",))
            run.loaded("both_w")

        def first(whole, chip):
            at = pair(chip)

            def columns(j):
                ups = pl.ds(pl.multiple_of(main + j * TILE, TILE), TILE)
                gate = dot(rows_of(whole[at]), both_w[:, tile(j)])
                up = dot(rows_of(whole[at]), both_w[:, ups])
                gate_up[at, :, tile(j)] = blocks_of(gate)
                gate_up[at, :, ups] = blocks_of(up)
                hidden[at, :, tile(j)] = blocks_of((gate * jax.nn.sigmoid(gate) * up).astype(BF16))

            loop(main // TILE, columns)
            both = dot(rows_of(whole[at]), both_w[:, 2 * main :])
            gate_up[at, :, 2 * main :] = blocks_of(both)
            lane = lax.broadcasted_iota(jnp.int32, both.shape, 1)
            tail = jnp.where(lane < LANES // 2, both * jax.nn.sigmoid(both) * swap_half(both), 0.0)
            hidden[at, :, main:] = blocks_of(tail.astype(BF16))

        def between(whole):
            run.saved()
            run.save(whole, saves[layer]["ffn_whole"])
            run.save(gate_up, saves[layer]["gate_up"])
            run.save(hidden, saves[layer]["hidden"])

        def second(chip, j):
            return dot(rows_of(hidden[pair(chip)]), down_w[:, tile(j)])

        def after(h, rows, total):
            result = middles[layer][rows] + total
            if layer + 1 < layers:
                sources[layer][rows] = result
                next_ref[rows] = rounded(result, gains[2 * layer + 2])
            else:
                stream_out[rows] = result

        def before_second():
            load(layer, ("down_w",))
            run.loaded("down_w")

        run.phase(next_ref, first, second, after, before_first, before_second, between)

    next_ref[...] = rounded(stream_in[...], gains[0])
    run.enter([place.beside("zh"), place.beside("x")] if moving else [], False)
    if moving:
        for layer in range(layers):
            moves(layer, WEIGHTS if layer else WEIGHTS[2:])
    for layer in range(layers):
        conv(layer, sources[layer - 1] if layer else stream_in)
        ffn(layer)
    run.saved()
    for copy in place.sent:
        copy.wait_send()


class Several:
    def __init__(self, copies):
        self.copies = copies

    def wait(self):
        for copy in self.copies:
            copy.wait()


def forward(stream, gains, taps, keep, weights, mine, tall):
    tokens, features = stream.shape
    layers = taps.shape[0]
    moving = mine is not None
    wide = (weights[0][0].shape[1], mine[0][0].shape[3] if moving else weights[0][2].shape[1])
    forms = forms_of(tokens, features, wide, tall, layers)
    inside = pl.BlockSpec(memory_space=pltpu.VMEM)
    anywhere = pl.BlockSpec(memory_space=pl.ANY)
    outs = [(forms["stream"], inside)] * (1 + layers + layers - 1)
    outs += [(forms[name], anywhere) for _ in range(layers) for name in SAVED]
    if moving:
        outs += [((whole_shape(array.shape), BF16), anywhere) for group in mine for array in group]
    buffers = {name: forms[name] for name in ("joint", "carried", "mixed", "gated", "gate_up", "hidden", "next", "tails")}
    buffers |= {name: forms[name] for name in ("whole", "part", "sib", "yin", "yout", "zin", "zout")}
    buffers |= {"vmem_in_w": forms["in_w"], "vmem_both_w": forms["both_w"]}
    buffers |= {"vmem_out_w": ((forms["gated"][0][2], features), BF16), "vmem_down_w": forms["tall_w"]}
    operands = [array for group in weights for array in group]
    operands += [array for group in mine for array in group] if moving else []
    results = pl.pallas_call(
        functools.partial(forward_kernel, {"layers": layers, "moving": moving, "buffers": tuple(buffers)}),
        out_shape=[jax.ShapeDtypeStruct(*form) for form, _ in outs],
        in_specs=[inside] * 4 + [anywhere] * len(operands),
        out_specs=[spec for _, spec in outs],
        scratch_shapes=[pltpu.VMEM(*form) for form in buffers.values()] + [pltpu.SemaphoreType.DMA((SEMAPHORES,))] * 3,
        compiler_params=pltpu.CompilerParams(
            collective_id=COLLECTIVE_ID["forward"], has_side_effects=True, vmem_limit_bytes=62 << 20
        ),
        name="forward",
    )(stream, gains, taps, keep, *operands)
    stream_out, results = results[0], results[1:]
    middles, results = results[:layers], results[layers:]
    sources, results = results[: layers - 1], results[layers - 1 :]
    count = layers * len(SAVED)
    return stream_out, middles, sources, results[:count], results[count:]


def backward_kernel(plan, *refs):
    refs = list(refs)
    layers, moving, buffer_names = plan["layers"], plan["moving"], plan["buffers"]

    def take(count):
        taken = refs[:count]
        del refs[:count]
        return taken

    grad_out, gains, taps_ref, keep = take(4)
    middles, sources = take(layers), take(layers)
    weights = [dict(zip(WEIGHTS, take(4))) for _ in range(layers)]
    saves = [dict(zip(SAVED, take(len(SAVED)))) for _ in range(layers)]
    (grad_in,) = take(1)
    if moving:
        small_sum, grad_in_w, grad_out_w, gate_out, up_out, down_out = take(6)
    else:
        gain_out, taps_out = take(2)
        raw = [take(4) for _ in range(layers)]
    buffers = dict(zip(buffer_names, take(len(buffer_names))))
    if moving:
        landing = {name: take(5 if name in ("in_w", "both_w") else 4) for name in WEIGHTS}
        staging, slabs, slabs_in = take(2), *take(2)
        free = dict(zip(("both", "down", "conv"), take(3)))
    place = Place(*take(3))
    run = Pass(place, buffers)
    tokens, features = run.tokens, run.features
    rows_of, blocks_of, all_rows, pair = run.rows_of, run.blocks_of, run.all_rows, run.pair
    wide = {"in_w": plan["wide"][0], "both_w": plan["wide"][1]}
    joint, gate_up = buffers["gate_up"].at[:, :, : wide["in_w"]], buffers["gate_up"]
    grad_joint, grad_gate_up = buffers["grad_rows"].at[:, :, : wide["in_w"]], buffers["grad_rows"]
    in_w, both_w = buffers["wide_w"].at[:, : wide["in_w"]], buffers["wide_w"]
    channels, units = buffers["mixed"].shape[2], buffers["hidden"].shape[2]
    out_w, down_w = buffers["tall_w"].at[:channels], buffers["tall_w"]
    gated, hidden = buffers["hidden"].at[:, :, :channels], buffers["hidden"]
    carried, mixed, edges, grad_gated = (buffers[name] for name in ("carried", "mixed", "edges", "grad_gated"))
    kept_whole, next_ref, grad_ref, held = (buffers[name] for name in ("conv_whole", "next", "stream", "held"))
    gain_grads, tap_grads = buffers["gain_grads"], buffers["tap_grads"]
    main = gate_up.shape[2] // (2 * LANES) * LANES

    def load_rows(name, source, target):
        if len(source.shape) == 2:
            run.load(name, source, target)
            return
        rows, lead = source.shape[-2], source.shape[:-2]
        copies = []
        for n, index in enumerate(itertools.product(*(range(size) for size in lead))):
            copies.append(place.copy(source.at[index], target.at[pl.ds(n * rows, rows)]))
            copies[-1].start()
        filled = rows * len(copies)
        if filled < target.shape[0]:
            target[filled:] = jnp.zeros((target.shape[0] - filled, target.shape[1]), BF16)
        run.loading[name] = Several(copies)

    def deliver_columns(outs, layer, views):
        def deliver(landed):
            run.saved()
            shards_to(landed, views)
            for source, out in outs:
                run.save(source, out.at[layer])

        return deliver

    def deliver_rows(out, layer):
        def deliver(final):
            run.save(final, out.at[layer])

        return deliver

    reduced = {"both": 0, "down": 0, "conv": 0}
    under_way = {"both": [], "down": [], "conv": []}

    def reduce(layer, kind, names):
        if not moving:
            for name in names:
                source = buffers["grad_" + name]
                target = raw[layer][WEIGHTS.index(name)]
                run.save(source.at[: target.shape[0]] if source.shape != target.shape else source, target)
            return
        if reduced[kind]:
            pl.semaphore_wait(free[kind], 9)
        reduced[kind] += 1
        run.saved()
        items = []
        for name in names:
            if name == "in_w":
                width = features
                views = [staging[0].at[:, i * width : (i + 1) * width] for i in range(3)]
                deliver = deliver_columns([(staging[0], grad_in_w)], layer, views)
            elif name == "both_w":
                deliver = deliver_columns([(staging[0], gate_out), (staging[1], up_out)], layer, list(staging))
            else:
                deliver = deliver_rows(grad_out_w if name == "out_w" else down_out, layer)
            total = buffers["grad_" + name]
            if name in ("out_w", "down_w"):
                total = total.at[: 4 * landing[name][3].shape[0]]
            items.append(Reduce(place, total, landing[name], deliver))
            items[-1].start()
        run.begin(items)
        under_way[kind] = items

    def settle(kind):
        items, under_way[kind] = under_way[kind], []
        run.settle(items)
        if items and reduced[kind] < layers:
            for device in [place.member(flips) for flips in FLIPS] + [place.beside("zh"), place.beside("x")]:
                pl.semaphore_signal(free[kind], inc=1, device_id=device, device_id_type=MESH)

    def step_back(h, rows, total, stream, gain, row):
        scale = rms_scale(stream)
        gain_grad = jnp.sum(total * stream * scale, axis=0, keepdims=True)
        gain_grads[row : row + 1] = gain_grad if h == 0 else gain_grads[row : row + 1] + gain_grad
        scaled = total * gain
        grad = (
            grad_ref[rows]
            + scale * scaled
            - stream * (scale * scale * scale) * jnp.mean(scaled * stream, axis=-1, keepdims=True)
        )
        grad_ref[rows] = grad
        next_ref[rows] = grad.astype(BF16)
        return grad

    def ffn_back(layer):
        def before_first():
            load_rows("down_w", weights[layer]["down_w"], down_w)
            run.load("gate_up", saves[layer]["gate_up"], gate_up)
            load_rows("both_w", weights[layer]["both_w"], both_w)
            run.load("hidden", saves[layer]["hidden"], hidden)
            run.load("whole", saves[layer]["ffn_whole"], kept_whole)
            run.load("held", middles[layer], held)
            run.loaded("down_w", "gate_up")

        def grads(grad_hidden, gate, up):
            sigmoid = jax.nn.sigmoid(gate)
            return grad_hidden * up * sigmoid * (1.0 + gate * (1.0 - sigmoid)), grad_hidden * gate * sigmoid

        def first(whole, chip):
            at = pair(chip)

            def columns(j):
                ups = pl.ds(pl.multiple_of(main + j * TILE, TILE), TILE)
                grad_hidden = dot_cols(rows_of(whole[at]), down_w[tile(j), :])
                gate, up = (rows_of(gate_up[at, :, lanes]) for lanes in (tile(j), ups))
                grad_gate, grad_up = grads(grad_hidden, gate, up)
                grad_gate_up[at, :, tile(j)] = blocks_of(grad_gate.astype(BF16))
                grad_gate_up[at, :, ups] = blocks_of(grad_up.astype(BF16))

            loop(main // TILE, columns)
            grad_hidden = dot_cols(rows_of(whole[at]), down_w[main:, :])
            both = rows_of(gate_up[at, :, 2 * main :])
            grad_gate, grad_up = grads(grad_hidden, both, swap_half(both))
            grad_gate_up[at, :, 2 * main :] = blocks_of((grad_gate + swap_half(grad_up)).astype(BF16))

        def second(chip, j):
            return dot_cols(rows_of(grad_gate_up[pair(chip)]), both_w[tile(j), :])

        def aside(whole):
            run.loaded("whole", "hidden")
            settle("both")
            settle("down")
            grad_both, grad_down = buffers["grad_both_w"], buffers["grad_down_w"]
            width = features // 4

            def both_rows(c):
                left = all_rows(kept_whole[:, :, tile(c, width)])
                result = dot_rows(left, all_rows(grad_gate_up[...])).astype(BF16)
                grad_both[c] = result.reshape(grad_both.shape[1:])

            def down_rows(j):
                left = all_rows(hidden[:, :, tile(j, LANES)])
                grad_down[tile(j, LANES), :] = dot_rows(left, all_rows(whole[...])).astype(BF16)

            loop(4, both_rows)
            reduce(layer, "both", ("both_w",))
            loop(units // LANES, down_rows)
            reduce(layer, "down", ("down_w",))

        def after(h, rows, total):
            step_back(h, rows, total, held[rows], gains[2 * layer + 1], 2 * layer + 1)

        run.phase(next_ref, first, second, after, before_first, lambda: run.loaded("both_w", "held"), None, aside)

    def conv_back(layer):
        taps = taps_ref.at[layer]

        def before_first():
            load_rows("out_w", weights[layer]["out_w"], out_w)
            for name, target in (("joint", joint), ("carried", carried), ("mixed", mixed)):
                run.load(name, saves[layer][name], target)
            load_rows("in_w", weights[layer]["in_w"], in_w)
            run.load("gated", saves[layer]["gated"], gated)
            run.load("whole", saves[layer]["conv_whole"], kept_whole)
            run.load("held", sources[layer], held)
            run.loaded("out_w")

        def first(whole, chip):
            at = pair(chip)
            grad_gated[at] = blocks_of(dot_cols(rows_of(whole[at]), out_w[...]))

        def between(whole):
            run.loaded("joint", "carried", "mixed")
            tap_grads[layer] = jnp.zeros(tap_grads.shape[1:], F32)

            def block(b):
                keep_one, keep_two = keep[0, b], keep[1, b]
                for lane, lanes in both_lanes():
                    grad_value = grad_gated[b, :, lanes]
                    grad_mixed = grad_value * c_columns(joint, b, lane)
                    first_tap, second_tap = grad_mixed * keep_two, grad_mixed * keep_one
                    edges[0, b, :tokens, lanes] = second_tap * taps[1:2, lanes]
                    edges[1, b, :tokens, lanes] = first_tap * taps[0:1, lanes]
                    mixed[b, :, lanes] = grad_value * mixed[b, :, lanes]
                    grad_gated[b, :, lanes] = grad_mixed * taps[2:3, lanes]
                    for row, grad, back_by in ((0, first_tap, 2), (1, second_tap, 1), (2, grad_mixed, 0)):
                        tap_in = carried[b, HALO - back_by : HALO - back_by + tokens, lanes]
                        tap_grads[layer, row : row + 1, lanes] += jnp.sum(grad * tap_in, axis=0, keepdims=True)

            loop(8, block)
            halo = Halo(place, edges, pl.ds(0, HALO), buffers["heads"].at[layer], False)
            halo.start()
            halo.wait_recv()
            edges[:, :, tokens:] = buffers["heads"][layer]

            def block_after(b):
                for lane, lanes in both_lanes():
                    grad_carried = (
                        grad_gated[b, :, lanes] + edges[0, b, 1 : 1 + tokens, lanes] + edges[1, b, 2 : 2 + tokens, lanes]
                    )
                    grad_c = mixed[b, :, lanes]
                    if lane == 0:
                        grad_joint[b, :, :LANES] = (grad_carried * joint[b, :, 2 * LANES : 3 * LANES]).astype(BF16)
                        grad_joint[b, :, LANES : 2 * LANES] = grad_c.astype(BF16)
                        grad_joint[b, :, 2 * LANES : 3 * LANES] = (grad_carried * joint[b, :, :LANES]).astype(BF16)
                    else:
                        grad_b = grad_carried * joint[b, :, 4 * LANES :]
                        grad_joint[b, :, 3 * LANES : 4 * LANES] = (grad_b + swap_half(grad_c)).astype(BF16)
                        grad_joint[b, :, 4 * LANES :] = (grad_carried * joint[b, :, 3 * LANES : 4 * LANES]).astype(BF16)

            loop(8, block_after)
            halo.wait_send()
            if layer == 0:
                gradients(whole)

        def second(chip, j):
            return dot_cols(rows_of(grad_joint[pair(chip)]), in_w[tile(j), :])

        def gradients(whole):
            run.loaded("whole", "gated")
            settle("conv")
            grad_in_rows, grad_out_rows = buffers["grad_in_w"], buffers["grad_out_w"]
            width = features // 4

            def in_rows(c):
                left = all_rows(kept_whole[:, :, tile(c, width)])
                result = dot_rows(left, all_rows(grad_joint[...])).astype(BF16)
                grad_in_rows[c] = result.reshape(grad_in_rows.shape[1:])

            def out_rows(j):
                left = all_rows(gated[:, :, tile(j, LANES)])
                grad_out_rows[tile(j, LANES), :] = dot_rows(left, all_rows(whole[...])).astype(BF16)

            loop(4, in_rows)
            loop(channels // LANES, out_rows)
            reduce(layer, "conv", ("in_w", "out_w"))

        def after(h, rows, total):
            grad = step_back(h, rows, total, held[rows], gains[2 * layer], 2 * layer)
            if layer == 0:
                grad_in[rows] = grad

        run.phase(
            next_ref, first, second, after, before_first, lambda: run.loaded("in_w", "held"), between, gradients if layer else None
        )

    grad_ref[...] = grad_out[...]
    next_ref[...] = grad_out[...].astype(BF16)
    run.enter([], moving)
    for layer in reversed(range(layers)):
        ffn_back(layer)
        conv_back(layer)
    if moving:
        owned = features // 32
        slabs[...] = jnp.zeros(slabs.shape, F32)
        for owner in range(32):
            slabs[owner, : 2 * layers, :owned] = gain_grads[:, owner * owned : (owner + 1) * owned]
        for layer in range(layers):
            row = 2 * layers + 3 * layer
            for zh, x in itertools.product(range(2), repeat=2):
                owner = ((place.yl * 2 + place.core) * 2 + zh) * 4 + place.zl * 2 + x
                low = (zh * 2 + x) * owned
                slabs[owner, row : row + 3, :owned] = tap_grads[layer, :3, low : low + owned]
        copies = []
        for i, (device, flips) in enumerate(every_other(place)):
            copies.append(place.push(slabs.at[place.owner(flips)], slabs_in.at[i], device))
            copies[-1].start()
        run.launch(len(run.queue))
        for kind in ("both", "down", "conv"):
            settle(kind)
        for copy in copies:
            copy.wait_recv()
        small_sum[...] = slabs[place.owner()] + jnp.sum(slabs_in[...], axis=0)
    else:
        gain_out[...] = gain_grads[...]
        taps_out[...] = tap_grads[...]
    run.saved()
    for copy in place.sent:
        copy.wait_send()


def backward(grad_out, gains, taps, keep, middles, sources, weights, saved, tall, moving):
    tokens, features = grad_out.shape
    layers = taps.shape[0]
    wide = (weights[0][0].shape[-1], weights[0][2].shape[-1])
    forms = forms_of(tokens, features, wide, tall, layers)
    inside = pl.BlockSpec(memory_space=pltpu.VMEM)
    anywhere = pl.BlockSpec(memory_space=pl.ANY)
    owned = features // 32
    outs = [(forms["stream"], inside)]
    if moving:
        outs.append((((16, LANES), F32), inside))
        shapes = ((owned, 3 * features), (owned, features), (owned, 4 * tall[1] * 2), (owned, 4 * tall[1] * 2), (tall[1] // 4, features))
        outs += [(((layers,) + shape, F32), anywhere) for shape in shapes]
    else:
        outs.append((((2 * layers, features), F32), inside))
        outs.append((((layers, HALO, forms["mixed"][0][2]), F32), inside))
        for _ in range(layers):
            for name in WEIGHTS:
                shape = forms["grad_" + name][0]
                outs.append((((tall[0] if name == "out_w" else tall[1], features) if len(shape) == 2 else shape, BF16), anywhere))
    names = ("conv_whole", "gate_up", "carried", "mixed", "hidden", "grad_rows", "grad_gated", "edges", "heads", "tall_w")
    names += ("next", "stream", "whole", "part", "sib", "yin", "yout", "zin", "zout")
    names += ("grad_in_w", "grad_both_w", "grad_out_w", "grad_down_w")
    buffers = {name: forms[name] for name in names}
    buffers["wide_w"], buffers["held"] = forms["both_w"], forms["stream"]
    buffers["gain_grads"] = ((2 * layers, features), F32)
    buffers["tap_grads"] = ((layers, HALO, forms["mixed"][0][2]), F32)
    scratch = [pltpu.VMEM(*form) for form in buffers.values()]
    if moving:
        for name in WEIGHTS:
            shape = forms["grad_" + name][0]
            if len(shape) == 2:
                shape = (tall[0] if name == "out_w" else tall[1], features)
            scratch += [pltpu.VMEM(*form) for form in landing_shapes(shape)]
        scratch += [pltpu.VMEM((owned, 3 * features), F32)] * 2
        scratch += [pltpu.VMEM((32, 16, LANES), F32), pltpu.VMEM((31, 16, LANES), F32)]
        scratch += [pltpu.SemaphoreType.REGULAR] * 3
    operands = list(middles) + list(sources) + [array for group in weights for array in group] + list(saved)
    plan = {"layers": layers, "moving": moving, "buffers": tuple(buffers), "wide": wide}
    return pl.pallas_call(
        functools.partial(backward_kernel, plan),
        out_shape=[jax.ShapeDtypeStruct(*form) for form, _ in outs],
        in_specs=[inside] * 4 + [anywhere] * len(operands),
        out_specs=[spec for _, spec in outs],
        scratch_shapes=scratch + [pltpu.SemaphoreType.DMA((SEMAPHORES,))] * 3,
        compiler_params=pltpu.CompilerParams(
            collective_id=COLLECTIVE_ID["backward"], has_side_effects=True, vmem_limit_bytes=63 << 20
        ),
        name="backward",
    )(grad_out, gains, taps, keep, *operands)


def sizes_of(axes):
    return tuple(lax.axis_size(axis) for axis in axes)


def split_owners(array, dim):
    owners = sizes_of(OWNERS)
    count = 1
    for size in owners:
        count *= size
    shape = array.shape
    return array.reshape(shape[:dim] + owners + (shape[dim] // count,) + shape[dim + 1 :])


def column_shards(weights):
    rows = weights[0].shape[0]
    mains, rests = [], []
    for weight in weights:
        parts = split_owners(weight, 1).transpose(5, 2, 3, 0, 1, 4, 6, 7).reshape(8, rows, -1)
        main = parts.shape[2] // LANES * LANES
        mains.append(parts[:, :, :main])
        rests.append(parts[:, :, main:])
    shards = jnp.concatenate(mains + rests, axis=2)
    return jnp.pad(shards, ((0, 0), (0, 0), (0, -shards.shape[2] % LANES)))


def column_whole(shards, groups, width):
    rows = shards.shape[1]
    yh, yl, core, zh, zl, x = sizes_of(OWNERS)
    wholes = []
    for group in range(groups):
        part = jnp.concatenate(
            [shards[..., a:b] for a, b in pieces_of(groups, width, group, 0, width)], axis=-1
        ).reshape(zl, yl, core, rows, yh, zh, x, -1)
        wholes.append(part.transpose(3, 4, 1, 2, 5, 0, 6, 7).reshape(rows, -1))
    return wholes


def gather_columns(shards):
    mine = lax.all_to_all(shards, TP, split_axis=0, concat_axis=0, tiled=True)
    whole = lax.all_gather(mine, DP, axis=0, tiled=False)
    yh, yl, core, zh, zl, x = sizes_of(OWNERS)
    rows, columns = shards.shape[1:]
    whole = whole.reshape(yh, zh, x, zl, yl, core, rows, columns)
    return whole.transpose(0, 4, 5, 1, 3, 2, 6, 7).reshape(-1, columns)


def scatter_columns(total):
    yh, yl, core, zh, zl, x = sizes_of(OWNERS)
    columns = total.shape[1]
    parts = split_owners(total, 0).transpose(0, 3, 5, 4, 1, 2, 6, 7)
    parts = parts.reshape(yh * zh * x, -1, columns)
    mine = lax.psum_scatter(parts, DP, scatter_dimension=0, tiled=False)
    mine = mine.reshape(8, -1, columns)
    return lax.all_to_all(mine, TP, split_axis=0, concat_axis=0, tiled=True)


def tap_masks(starts, token_count):
    zh, x, x_size = lax.axis_index("zh"), lax.axis_index("x"), lax.axis_size("x")
    blocks = (zh * 2 + jnp.arange(2, dtype=jnp.int32)) * x_size + x
    places = blocks[:, None] * token_count + jnp.arange(token_count, dtype=jnp.int32)

    def segment_of(where):
        return jnp.sum((starts[None, :, None, :] <= where[:, None, :, None]).astype(jnp.int32), axis=3)

    own_segment = segment_of(places)
    keep_one = (segment_of(places - 1) == own_segment).astype(F32)
    keep_two = (segment_of(places - 2) == own_segment).astype(F32)
    return keep_one.reshape(8, token_count, 1), keep_two.reshape(8, token_count, 1)


def local(stream_in, doc_starts, norm_mix, in_proj, conv_taps, out_proj, norm_ffn, w_gate, w_up, w_down, grad_out):
    _, token_count, features = stream_in.shape
    layers = norm_mix.shape[0]
    own_kernels = sizes_of(DP) == (1, 2, 2)
    stream = stream_in.reshape(-1, features)
    grad_stream = grad_out.reshape(-1, features)
    small = jnp.concatenate([norm_mix[:, None], norm_ffn[:, None], conv_taps.transpose(0, 2, 1)], axis=1)
    small = small.astype(BF16).astype(F32)
    owned = small.shape[2]
    tall = (features // 8, w_gate.shape[2] // 8)
    mine = None
    if own_kernels:
        packed = jnp.zeros((16, LANES), F32).at[: 5 * layers, :owned].set(small.reshape(-1, owned))
        packed = packed.at[15, : doc_starts.shape[1]].set(doc_starts[0].astype(F32))
        spread, shards, rounded, wholes = prepare(packed, in_proj, w_gate, w_up, out_proj, w_down)
        mine = [(shards[1], rounded[1])]
        for layer in range(1, layers):
            mine.append((shards[2 * layer], rounded[2 * layer], shards[2 * layer + 1], rounded[2 * layer + 1]))
        params = spread[:, : 5 * layers, :owned].transpose(1, 0, 2)
        gains = params.reshape(layers, 5, features)[:, :2].reshape(2 * layers, 1, features)
        params = params.reshape(layers, 5, 4, 2, 2, 2, owned)[:, 2:]
        others = lax.axis_index("yl") * 2 + lax.axis_index("core")
        params = lax.dynamic_index_in_dim(params, others, 2, False)
        taps = lax.dynamic_index_in_dim(params, lax.axis_index("zl"), 3, False).reshape(layers, 3, -1)
        starts = spread.reshape(4, 8, 16, LANES)[:, 0, 15, : doc_starts.shape[1]].astype(jnp.int32)
        weights = [tuple(whole.reshape(-1, whole.shape[-1]) for whole in wholes)]
    else:
        starts = lax.all_gather(doc_starts, ("yl", "core"), axis=0, tiled=True)
        small = small.astype(BF16)
        gains = lax.all_gather(small[:, :2], OWNERS, axis=2, tiled=True).astype(F32).reshape(2 * layers, 1, features)
        taps = lax.all_gather(small[:, 2:], DP, axis=2, tiled=True).astype(F32)
        weights = []
        for layer in range(layers):
            in_w = gather_columns(column_shards(jnp.split(in_proj[layer].astype(BF16), 3, axis=1)))
            both_w = gather_columns(column_shards([w_gate[layer].astype(BF16), w_up[layer].astype(BF16)]))
            out_w = lax.all_gather(out_proj[layer].astype(BF16), DP, axis=0, tiled=True)
            down_w = lax.all_gather(w_down[layer].astype(BF16), DP, axis=0, tiled=True)
            weights.append((in_w, out_w, both_w, down_w))
    channels = taps.shape[2]
    taps = jnp.pad(taps, ((0, 0), (0, HALO - 3), (0, -channels % LANES)))
    keep = jnp.stack(tap_masks(starts, token_count))

    stream_out, middles, sources, saved, wholes = forward(stream, gains, taps, keep, weights, mine, tall)
    if own_kernels:
        weights = [weights[0] + tuple(wholes[:2])]
        weights += [tuple(wholes[2 + 4 * i : 6 + 4 * i]) for i in range(layers - 1)]
    grad_in, *results = backward(
        grad_stream, gains, taps, keep, middles, [stream] + list(sources), weights, saved, tall, own_kernels
    )
    if own_kernels:
        small_sums, grad_in_w, grad_out_w, grad_gate, grad_up, grad_down = results
        small_sums = small_sums[:, :owned]
        gain_grads = small_sums[: 2 * layers].reshape(layers, 2, owned)
        tap_grads = small_sums[2 * layers : 5 * layers].reshape(layers, 3, owned)
    else:
        gain_grads, tap_grads, *raw = results
        gain_grads = lax.psum_scatter(gain_grads, OWNERS, scatter_dimension=1, tiled=True).reshape(layers, 2, -1)
        tap_grads = lax.psum_scatter(tap_grads[:, :3, :channels], DP, scatter_dimension=2, tiled=True)
        sums = []
        for layer in range(layers):
            grad_in_w, grad_out_w, grad_both, grad_down = raw[4 * layer : 4 * layer + 4]
            columns = [
                column_whole(scatter_columns(grad.reshape(features, -1)).astype(F32), groups, width)
                for grad, groups, width in ((grad_in_w, 3, tall[0]), (grad_both, 2, tall[1]))
            ]
            rows = [
                lax.psum_scatter(grad, DP, scatter_dimension=0, tiled=True).astype(F32) for grad in (grad_out_w, grad_down)
            ]
            sums.append((jnp.concatenate(columns[0], axis=1), rows[0], *columns[1], rows[1]))
        grad_in_w, grad_out_w, grad_gate, grad_up, grad_down = (jnp.stack(parts) for parts in zip(*sums))
    return (
        stream_out[None],
        grad_in[None],
        gain_grads[:, 0],
        grad_in_w,
        tap_grads.transpose(0, 2, 1),
        grad_out_w,
        gain_grads[:, 1],
        grad_gate,
        grad_up,
        grad_down,
    )


def solution(mesh):
    dp, seq = mesh.shape["dp"], mesh.shape["seq"]
    side = dp // 2
    split = Mesh(mesh.devices.reshape(side // 2, 2, 2, seq // side // 2, 2, side), OWNERS)
    token = P(ROW_AXES, SEQ_AXES, None)
    vector = P(None, OWNERS)
    matrix = P(None, OWNERS, None)
    return jax.shard_map(
        local,
        mesh=split,
        in_specs=(token, P(ROW_AXES, None), vector, matrix, matrix, matrix, vector, matrix, matrix, matrix, token),
        out_specs=(token, token, vector, matrix, matrix, matrix, vector, matrix, matrix, matrix),
        check_vma=False,
    )
```

```python
import functools
import itertools

import jax
import jax.numpy as jnp
from jax import lax
from jax.experimental import pallas as pl
from jax.experimental.pallas import tpu as pltpu
from jax.sharding import Mesh, PartitionSpec as P

EPSILON = 1e-05
TP = ("zl", "yl", "core")
DP = ("yh", "zh", "x")
ROW_AXES = ("yh", "yl", "core")
SEQ_AXES = ("zh", "zl", "x")
OWNERS = ROW_AXES + SEQ_AXES
BF16 = jnp.bfloat16
F32 = jnp.float32
MESH = pl.DeviceIdType.MESH
HALVES = 2
COLLECTIVE_ID = {"forward": 0, "backward": 1}
FLIPS = ((1, 1, 1), (1, 1, 0), (1, 0, 1), (1, 0, 0), (0, 1, 1), (0, 1, 0), (0, 0, 1))
OTHERS = tuple(itertools.product((0, 1), repeat=5))[1:]
OTHER_AXES = ("yl", "core", "zh", "zl", "x")
SEMAPHORES = 288
PACE = ((1, 1),) * 11
LANES = 128
TILE = 256
HALO = 8


def rms_scale(values):
    return lax.rsqrt(jnp.mean(values * values, axis=-1, keepdims=True) + EPSILON)


class Place:
    def __init__(self, send, recv, local):
        self.zl, self.yl, self.core = (lax.axis_index(axis) for axis in TP)
        self.zh, self.x = lax.axis_index("zh"), lax.axis_index("x")
        self.send, self.recv, self.local = send, recv, local
        self.remote_count = self.local_count = 0
        self.sent = []

    def rank(self, flip_z, flip_y, flip_core):
        return self.flipped("zl", flip_z) * 4 + self.flipped("yl", flip_y) * 2 + self.flipped("core", flip_core)

    def flipped(self, axis, flip):
        return 1 - getattr(self, axis) if flip else getattr(self, axis)

    def member(self, flips):
        return {axis: 1 - getattr(self, axis) for axis, flip in zip(TP, flips) if flip}

    def beside(self, axis):
        return {axis: 1 - getattr(self, axis)}

    def owner(self, flips=(0,) * 5):
        index = 0
        for axis, flip in zip(OTHER_AXES, flips):
            index = index * 2 + self.flipped(axis, flip)
        return index

    def push(self, src, dst, device, kept=True):
        index = self.remote_count
        self.remote_count += 1
        assert index < SEMAPHORES
        copy = pltpu.make_async_remote_copy(
            src_ref=src, dst_ref=dst, send_sem=self.send.at[index], recv_sem=self.recv.at[index],
            device_id=device, device_id_type=MESH,
        )
        if kept:
            self.sent.append(copy)
        return copy

    def copy(self, src, dst):
        index = self.local_count
        self.local_count += 1
        return pltpu.make_async_copy(src, dst, self.local.at[index])


def pieces_of(groups, width, group, low, high):
    main = width // LANES * LANES
    rest = width - main
    ranges = []
    if low < main:
        ranges.append((group * main + low, group * main + min(high, main)))
    if high > main:
        start = groups * main + group * rest - main
        ranges.append((start + max(low, main), start + high))
    return ranges


def shards_from(weights, out):
    width = weights[0].shape[1] // 8
    block = width // 4
    main = width // LANES * LANES
    rest = width - main
    for group, weight in enumerate(weights):
        for member in range(8):
            zl, others = member // 4, member % 4
            starts = [((others * 2 + zh) * 4 + zl * 2 + x) * block for zh in range(2) for x in range(2)]
            values = jnp.concatenate([weight[:, start : start + block] for start in starts], axis=1).astype(BF16)
            out[member, :, group * main : (group + 1) * main] = values[:, :main]
            if rest:
                low = len(weights) * main + group * rest
                out[member, :, low : low + rest] = values[:, main:]
    pad = out.shape[2] - len(weights) * width
    if pad:
        out[:, :, len(weights) * width :] = jnp.zeros((8, out.shape[1], pad), BF16)


def shards_to(shards, outs):
    groups, width = len(outs), outs[0].shape[1] // 8
    block = width // 4
    for group, out in enumerate(outs):
        for others in range(4):
            for zh in range(2):
                values = []
                for zl in range(2):
                    for x in range(2):
                        low = (zh * 2 + x) * block
                        for start, end in pieces_of(groups, width, group, low, low + block):
                            values.append(shards[zl * 4 + others, :, start:end].astype(F32))
                start = (others * 2 + zh) * 4 * block
                out[:, start : start + 4 * block] = jnp.concatenate(values, axis=1)


def every_other(place):
    return [
        ({axis: place.flipped(axis, 1) for axis, flip in zip(OTHER_AXES, flips) if flip}, flips) for flips in OTHERS
    ]


class Gather:
    def __init__(self, place, mine, whole):
        self.ready = None
        x, own, other = place.x, place.zh, 1 - place.zh
        if len(whole.shape) == 6:
            parts = [
                (mine.at[c, zl], whole.at[c, own, zl, x], whole.at[c, other, zl, x])
                for c in range(4)
                for zl in range(2)
            ]
        else:
            count = whole.shape[2]
            size = 48 if count % 48 == 0 else count
            parts = [
                (mine.at[rows], whole.at[own, x, rows], whole.at[other, x, rows])
                for rows in (pl.ds(low, size) for low in range(0, count, size))
            ]
        self.along_z = [place.push(src, here, place.beside("zh")) for src, here, _ in parts]
        self.along_x = [place.push(src, here, place.beside("x")) for src, here, _ in parts]
        self.onward = [place.push(there, there, place.beside("x")) for _, _, there in parts]
        self.kept = [place.copy(src, here) for src, here, _ in parts]

    def pairs(self):
        def launch(c):
            if c == 0 and self.ready is not None:
                self.ready()
            self.along_z[c].start()
            self.along_x[c].start()
            self.kept[c].start()

        def land(c):
            self.along_z[c].wait_recv()
            self.onward[c].start()

        return [(functools.partial(launch, c), functools.partial(land, c)) for c in range(len(self.kept))]

    def finish(self):
        for c in range(len(self.kept)):
            self.along_x[c].wait_recv()
            self.onward[c].wait_recv()
            self.kept[c].wait()


class Reduce:
    def __init__(self, place, total, landing, deliver):
        self.columns = len(total.shape) == 6
        self.place, self.total, self.deliver = place, total, deliver
        self.xin, self.zout, self.zin, self.final = landing[:4]
        self.landed = landing[4] if self.columns else None
        x, zh, beside = place.x, place.zh, place.beside
        self.flips = FLIPS + ((0, 0, 0),)
        self.chunks = self.zin.shape[0]
        self.along_x = [
            [
                place.push(self.part(j, to_zh, 1 - x), self.xin.at[j, i], beside("x"), False)
                for i, to_zh in enumerate((1 - zh, zh))
            ]
            for j in range(self.chunks)
        ]
        self.along_z = [place.push(self.zout.at[j], self.zin.at[j], beside("zh"), False) for j in range(self.chunks)]
        if self.columns:
            here = self.landed.at[place.rank(0, 0, 0)]
            self.back = [place.push(self.final.at[j], here, place.member(flips), False) for j, flips in enumerate(FLIPS)]
            self.back.append(place.copy(self.final.at[7], here))

    def part(self, j, zh, x):
        if self.columns:
            flip_z, flip_y, flip_core = self.flips[j]
            place = self.place
            chunk = place.flipped("yl", flip_y) * 2 + place.flipped("core", flip_core)
            return self.total.at[chunk, zh, place.flipped("zl", flip_z), x]
        count = self.zin.shape[1]
        low = ((zh * 2 + x) * self.chunks + j) * count
        return self.total.at[pl.ds(pl.multiple_of(low, 16), count)]

    def start(self):
        for copies in self.along_x:
            for copy in copies:
                copy.start()

    def pairs(self):
        x, zh = self.place.x, self.place.zh

        def launch(j):
            for copy in self.along_x[j]:
                copy.wait_recv()
            self.zout[j] = (self.part(j, 1 - zh, x)[...].astype(F32) + self.xin[j, 0].astype(F32)).astype(BF16)
            self.along_z[j].start()

        def land(j):
            self.along_z[j].wait_recv()
            total = self.part(j, zh, x)[...].astype(F32) + self.xin[j, 1].astype(F32) + self.zin[j].astype(F32)
            if self.columns:
                self.final[j] = total.astype(BF16)
                self.back[j].start()
            else:
                count = self.zin.shape[1]
                self.final[j * count : (j + 1) * count] = total

        return [(functools.partial(launch, j), functools.partial(land, j)) for j in range(self.chunks)]

    def finish(self):
        if self.columns:
            for copy in self.back[:-1]:
                copy.wait_recv()
            self.back[-1].wait()
        sent = [copy for copies in self.along_x for copy in copies] + self.along_z
        for copy in sent + (self.back[:-1] if self.columns else []):
            copy.wait_send()
        self.deliver(self.landed if self.columns else self.final)


def landing_shapes(total):
    if len(total) == 6:
        rows = total[4:]
        return [((8, 2) + rows, BF16)] + [((8,) + rows, BF16)] * 4
    count = total[0] // 4
    size = 48 if count % 48 == 0 else count
    rows = (size,) + total[1:]
    chunks = (count // size,)
    return [(chunks + (2,) + rows, BF16), (chunks + rows, BF16), (chunks + rows, BF16), ((count,) + total[1:], F32)]


def loop(count, body):
    def step(i, carry):
        body(i)
        return carry

    lax.fori_loop(0, count, step, 0)


def tile(i, width=TILE):
    return pl.ds(pl.multiple_of(i * width, width), width)


def dot(left, right):
    return jnp.dot(left, right, preferred_element_type=F32)


def dot_cols(left, right):
    return lax.dot_general(left, right, (((1,), (1,)), ((), ())), preferred_element_type=F32)


def dot_rows(left, right):
    return lax.dot_general(left, right, (((0,), (0,)), ((), ())), preferred_element_type=F32)


def swap_half(values):
    return pltpu.roll(values, LANES // 2, 1)


class Halo:
    def __init__(self, place, buffer, edge, landing, forward):
        x, zh, count = place.x, place.zh, lax.axis_size("x")
        first, final = x == 0, x == count - 1
        low, high, every = pl.ds(0, 4), pl.ds(4, 4), pl.ds(0, 8)
        lead = (slice(None),) * (len(buffer.shape) - 3)
        step = lax.rem(x + 1, count) if forward else lax.rem(x + count - 1, count)
        if forward:
            within, turn, beyond = jnp.logical_not(final), final, jnp.logical_and(final, zh == 0)
            into, turned, entered = jnp.logical_not(first), first, jnp.logical_and(first, zh == 1)
            sent, landed = low, high
        else:
            within, turn, beyond = jnp.logical_not(first), first, jnp.logical_and(first, zh == 1)
            into, turned, entered = jnp.logical_not(final), final, jnp.logical_and(final, zh == 0)
            sent, landed = high, low

        def push(src, dst, device):
            return place.push(buffer.at[lead + (src, edge)], landing.at[lead + (dst,)], device, False)

        copies = [
            push(every, every, {"x": step}),
            push(sent, landed, {"x": step}),
            push(landed, sent, {"x": step, "zh": 1 - zh}),
        ]
        self.sends = list(zip((within, turn, beyond), copies))
        self.lands = list(zip((into, turned, entered), copies))
        self.unreached = jnp.logical_and(turned, jnp.logical_not(entered))
        self.landing, self.open_end = landing, lead + (sent,)

    def start(self):
        for condition, copy in self.sends:
            pl.when(condition)(copy.start)

        @pl.when(self.unreached)
        def _():
            shape = self.landing.at[self.open_end].shape
            self.landing[self.open_end] = jnp.zeros(shape, self.landing.dtype)

    def wait_recv(self):
        for condition, copy in self.lands:
            pl.when(condition)(copy.wait_recv)

    def wait_send(self):
        for condition, copy in self.sends:
            pl.when(condition)(copy.wait_send)


SAVED = ("conv_whole", "joint", "carried", "mixed", "gated", "ffn_whole", "gate_up", "hidden")
WEIGHTS = ("in_w", "out_w", "both_w", "down_w")


def forms_of(tokens, features, wide, tall, layers):
    channels, units = (-(-rows // LANES) * LANES for rows in tall)
    block = (tokens, features)
    return {
        "in_w": ((features, wide[0]), BF16),
        "both_w": ((features, wide[1]), BF16),
        "out_w": ((tall[0], features), BF16),
        "down_w": ((tall[1], features), BF16),
        "conv_whole": ((8,) + block, BF16),
        "ffn_whole": ((8,) + block, BF16),
        "joint": ((8, tokens, wide[0]), F32),
        "gate_up": ((8, tokens, wide[1]), F32),
        "carried": ((8, tokens + HALO, channels), F32),
        "mixed": ((8, tokens, channels), F32),
        "gated": ((8, tokens, channels), BF16),
        "hidden": ((8, tokens, units), BF16),
        "tall_w": ((units, features), BF16),
        "grad_rows": ((8, tokens, wide[1]), BF16),
        "grad_gated": ((8, tokens, channels), F32),
        "edges": ((2, 8, tokens + HALO, channels), F32),
        "heads": ((layers, 2, 8, HALO, channels), F32),
        "tails": ((layers, 8, HALO, channels), F32),
        "stream": (block, F32),
        "next": (block, BF16),
        "whole": ((2, 8) + block, BF16),
        "part": ((4, 2) + block, BF16),
        "sib": ((4,) + block, BF16),
        "yin": ((2,) + block, BF16),
        "yout": ((2,) + block, BF16),
        "zin": (block, BF16),
        "zout": (block, BF16),
        "grad_in_w": ((4, 2, 2, 2, features // 32, wide[0]), BF16),
        "grad_both_w": ((4, 2, 2, 2, features // 32, wide[1]), BF16),
        "grad_out_w": ((channels, features), BF16),
        "grad_down_w": ((units, features), BF16),
    }


class Pass:
    def __init__(self, place, buffers):
        self.place, self.buffers = place, buffers
        self.tokens, self.features = buffers["zin"].shape
        half = self.tokens // HALVES
        self.halves = [pl.ds(h * half, half) for h in range(HALVES)]
        self.chips = ((0, 0), (1, 0), (0, 1), (1, 1))
        self.phases = 0
        self.items, self.queue, self.flying = [], [], []
        self.saving, self.loading = [], {}

    def enter(self, more, barrier_all):
        place = self.place
        barrier = pltpu.get_barrier_semaphore()
        if barrier_all:
            partners = [device for device, _ in every_other(place)]
            expected = len(partners)
        else:
            x, zh, x_size = place.x, place.zh, lax.axis_size("x")
            partners = [place.beside(axis) for axis in ("core", "yl", "zl")] + more
            partners += [{"x": lax.rem(x + 1, x_size)}, {"x": lax.rem(x + x_size - 1, x_size)}]
            at_turn = jnp.logical_or(jnp.logical_and(x == x_size - 1, zh == 0), jnp.logical_and(x == 0, zh == 1))
            across = {"x": jnp.where(x == 0, x_size - 1, 0), "zh": 1 - zh}

            @pl.when(at_turn)
            def _():
                pl.semaphore_signal(barrier, inc=1, device_id=across, device_id_type=MESH)

            expected = len(partners) + jnp.where(at_turn, 1, 0)
        for partner in partners:
            pl.semaphore_signal(barrier, inc=1, device_id=partner, device_id_type=MESH)
        pl.semaphore_wait(barrier, expected)

    def begin(self, items):
        for item in items:
            item.left = len(item.pairs())
            self.queue += [(item,) + pair for pair in item.pairs()]
            self.items.append(item)

    def launch(self, count):
        for item, launch, land in self.queue[:count]:
            launch()
            self.flying.append((item, land))
        del self.queue[:count]

    def land(self, count):
        for item, land in self.flying[:count]:
            land()
            item.left -= 1
        del self.flying[:count]

    def step(self, point):
        fly, count = PACE[point]
        while len(self.flying) > fly:
            self.land(1)
        self.launch(count)

    def settle(self, items):
        for item in items:
            while any(queued is item for queued, _, _ in self.queue):
                self.launch(1)
            while item.left:
                self.land(1)
            item.finish()
            self.items.remove(item)

    def load(self, name, source, target):
        if target.shape != source.shape:
            rows = target.shape[0] - source.shape[0]
            target[source.shape[0] :] = jnp.zeros((rows,) + target.shape[1:], BF16)
            target = target.at[: source.shape[0]]
        self.loading[name] = self.place.copy(source, target)
        self.loading[name].start()

    def loaded(self, *names):
        for name in names:
            self.loading.pop(name).wait()

    def save(self, source, target):
        self.saving.append(self.place.copy(source, target))
        self.saving[-1].start()

    def saved(self):
        for copy in self.saving:
            copy.wait()
        self.saving = []

    def pair(self, chip):
        return pl.ds(self.place.rank(*chip, 0) - self.place.core, 2)

    def rows_of(self, values):
        return values.reshape(2 * self.tokens, values.shape[-1])

    def blocks_of(self, values):
        return values.reshape(2, self.tokens, values.shape[-1])

    def all_rows(self, values):
        return values.reshape(8 * self.tokens, values.shape[-1])

    def phase(self, mine, first, second, after, before_first=None, before_second=None, between=None, aside=None):
        place, buffers, halves, chips = self.place, self.buffers, self.halves, self.chips
        rank, sent = place.rank, []
        whole = buffers["whole"].at[self.phases % 2]
        self.phases += 1
        part, sib, yin, yout, zin, zout = (buffers[name] for name in ("part", "sib", "yin", "yout", "zin", "zout"))
        to_sibling, to_y, to_z = (place.beside(axis) for axis in ("core", "yl", "zl"))
        own, beside_z, beside_y, corner = (rank(*chip, 0) for chip in chips)

        def push(src, dst, device):
            sent.append(place.push(src, dst, device, False))
            return sent[-1]

        def sends(src, at, device):
            return [push(mine.at[rows] if src is None else src.at[at, rows], whole.at[at, rows], device) for rows in halves]

        def landed(copies):
            for copy in copies:
                copy.wait_recv()

        from_z, from_y, own_to_core = sends(None, own, to_z), sends(None, own, to_y), sends(None, own, to_sibling)
        from_corner = sends(whole, beside_z, to_y)
        z_to_core, y_to_core, corner_to_core = (sends(whole, at, to_sibling) for at in (beside_z, beside_y, corner))
        own_place = place.copy(mine, whole.at[own])
        own_place.start()
        for h in range(HALVES):
            for copies in (from_z, from_y, own_to_core):
                copies[h].start()
        self.step(0)
        if before_first is not None:
            before_first()
        own_place.wait()
        landed(own_to_core)
        first(whole, chips[0])
        for h in range(HALVES):
            from_z[h].wait_recv()
            from_corner[h].start()
            z_to_core[h].start()
        self.step(1)
        for h in range(HALVES):
            from_y[h].wait_recv()
            y_to_core[h].start()
        landed(z_to_core)
        first(whole, chips[1])
        self.step(2)
        landed(y_to_core)
        first(whole, chips[2])
        self.step(3)
        for h in range(HALVES):
            from_corner[h].wait_recv()
            corner_to_core[h].start()
        landed(corner_to_core)
        first(whole, chips[3])
        self.step(4)
        if between is not None:
            between(whole)
        if before_second is not None:
            before_second()

        order = (chips[3], chips[2], chips[1], chips[0])
        sib_copies = [push(part.at[i, 1 - place.core], sib.at[i], to_sibling) for i in range(4)]
        y_copies = [[push(yout.at[i, rows], yin.at[i, rows], to_y) for rows in halves] for i in range(2)]
        z_copies = [push(zout.at[rows], zin.at[rows], to_z) for rows in halves]

        def multiply(i):
            def columns(j):
                part[i, :, :, tile(j)] = self.blocks_of(second(order[i], j).astype(BF16))

            loop(self.features // TILE, columns)
            sib_copies[i].start()

        def chip_sum(i, rows):
            return part[i, place.core, rows].astype(F32) + sib[i, rows].astype(F32)

        def to_y_side(i):
            sib_copies[i].wait_recv()
            for h, rows in enumerate(halves):
                yout[i, rows] = chip_sum(i, rows).astype(BF16)
                y_copies[i][h].start()

        multiply(0)
        multiply(1)
        to_y_side(0)
        self.step(5)
        multiply(2)
        to_y_side(1)
        multiply(3)
        self.step(6)
        sib_copies[2].wait_recv()
        for h, rows in enumerate(halves):
            y_copies[0][h].wait_recv()
            zout[rows] = (chip_sum(2, rows) + yin[0, rows].astype(F32)).astype(BF16)
            z_copies[h].start()
        self.step(7)
        if aside is not None:
            aside(whole)
        self.step(8)
        sib_copies[3].wait_recv()
        for copy in sent:
            copy.wait_send()
        for h, rows in enumerate(halves):
            y_copies[1][h].wait_recv()
            z_copies[h].wait_recv()
            if h == HALVES - 1:
                self.step(9)
            after(h, rows, chip_sum(3, rows) + yin[1, rows].astype(F32) + zin[rows].astype(F32))
        self.step(10)


def c_columns(joint, b, lane):
    if lane == 0:
        return joint[b, :, LANES : 2 * LANES]
    return swap_half(joint[b, :, 3 * LANES : 4 * LANES])


def both_lanes():
    return [(lane, slice(lane, lane + LANES)) for lane in (0, LANES)]


def forward_kernel(plan, *refs):
    refs = list(refs)
    layers, moving, buffer_names = plan["layers"], plan["moving"], plan["buffers"]

    def take(count):
        taken = refs[:count]
        del refs[:count]
        return taken

    (stream_in,) = take(1)
    if moving:
        small, in_proj, gate_in, up_in, out_in, down_in = take(6)
    else:
        gains, taps_ref, keep = take(3)
        weights = [dict(zip(WEIGHTS, take(4))) for _ in range(layers)]
    stream_out, middles, sources = take(1)[0], take(layers), take(layers - 1)
    saves = [dict(zip(SAVED, take(len(SAVED)))) for _ in range(layers)]
    if moving:
        weights = [dict(zip(WEIGHTS, take(4))) for _ in range(layers)]
        gains, taps_ref, keep = take(3)
    buffers = dict(zip(buffer_names, take(len(buffer_names))))
    if moving:
        (spread,) = take(1)
        shards, mine = ([dict(zip(WEIGHTS[::2], take(2))) for _ in range(layers)] for _ in range(2))
        rounds = [dict(zip(WEIGHTS[1::2], take(2))) for _ in range(layers)]
    place = Place(*take(3))
    run = Pass(place, buffers)
    tokens, features = run.tokens, run.features
    rows_of, blocks_of, pair = run.rows_of, run.blocks_of, run.pair
    joint, carried, mixed, gated = (buffers[name] for name in ("joint", "carried", "mixed", "gated"))
    gate_up, hidden = buffers["gate_up"], buffers["hidden"]
    in_w, out_w, both_w, down_w = (buffers["vmem_" + name] for name in WEIGHTS)
    main = gate_up.shape[2] // (2 * LANES) * LANES
    next_ref = buffers["next"]

    coming, scattered = {}, {}

    def moves(layer, names):
        for name in names:
            own = mine[layer][name] if name in mine[layer] else rounds[layer][name]
            coming[layer, name] = Gather(place, own, weights[layer][name])
            if name in mine[layer]:
                coming[layer, name].ready = functools.partial(landed, layer, name)
            run.begin([coming[layer, name]])

    def cut(layer, name):
        if name == "in_w":
            width = in_proj.shape[2] // 3
            groups = [in_proj.at[layer, :, i * width : (i + 1) * width] for i in range(3)]
        else:
            groups = [gate_in.at[layer], up_in.at[layer]]
        shards_from(groups, shards[layer][name])

    def scatter(layer, name):
        source = shards[layer][name]
        here = mine[layer][name].at[place.yl * 2 + place.core, place.zl]
        copies = [place.push(source.at[place.rank(*flips)], here, place.member(flips)) for flips in FLIPS]
        copies.append(place.copy(source.at[place.rank(0, 0, 0)], here))
        for copy in copies:
            copy.start()
        scattered[layer, name] = copies

    def landed(layer, name):
        copies = scattered.pop((layer, name))
        for copy in copies[:-1]:
            copy.wait_recv()
        copies[-1].wait()

    def parameters():
        owned = features // 32
        for layer in range(layers):
            for i in range(2):
                row = 5 * layer + i
                gains[2 * layer + i] = jnp.concatenate([spread[o, row : row + 1, :owned] for o in range(32)], axis=1)
            rows = pl.ds(5 * layer + 2, 3)
            parts = [
                spread[((place.yl * 2 + place.core) * 2 + zh) * 4 + place.zl * 2 + x, rows, :owned]
                for zh, x in itertools.product(range(2), repeat=2)
            ]
            taps_ref[layer] = jnp.zeros(taps_ref.shape[1:], F32)
            taps_ref[layer, :3, : 4 * owned] = jnp.concatenate(parts, axis=1)
        count = lax.broadcasted_iota(jnp.int32, (tokens, 1), 0)
        for block in range(8):
            zl, others = block // 4, block % 4
            places = (((place.zh * 2 + zl) * 2 + place.x) * tokens + count).astype(F32)
            starts = [spread[others * 8, 15:16, n : n + 1] for n in range(plan["documents"])]

            def segment(where):
                return sum(jnp.where(start <= where, 1.0, 0.0) for start in starts)

            own = segment(places)
            keep[0, block] = jnp.where(segment(places - 1.0) == own, 1.0, 0.0)
            keep[1, block] = jnp.where(segment(places - 2.0) == own, 1.0, 0.0)

    def load(layer, names):
        for name in names:
            if (layer, name) in coming:
                run.settle([coming.pop((layer, name))])
            source, target = weights[layer][name], buffers["vmem_" + name]
            if len(source.shape) == 2:
                run.load(name, source, target)
                continue
            copies = []
            rows = source.shape[-2]
            lead = source.shape[:-2]
            for n, index in enumerate(itertools.product(*(range(size) for size in lead))):
                copies.append(place.copy(source.at[index], target.at[pl.ds(n * rows, rows)]))
                copies[-1].start()
            filled = rows * len(copies)
            if filled < target.shape[0]:
                target[filled:] = jnp.zeros((target.shape[0] - filled, target.shape[1]), BF16)
            run.loading[name] = Several(copies)

    def rounded(values, gain):
        return (values * rms_scale(values) * gain).astype(BF16)

    def conv(layer, stream):
        def before_first():
            load(layer, ("in_w",))
            run.loaded("in_w")

        def first(whole, chip):
            at = pair(chip)

            def columns(j):
                joint[at, :, tile(j)] = blocks_of(dot(rows_of(whole[at]), in_w[:, tile(j)]))

            loop(2, columns)
            joint[at, :, 2 * TILE :] = blocks_of(dot(rows_of(whole[at]), in_w[:, 2 * TILE :]))
            here = pl.ds(HALO, tokens)
            carried[at, here, :LANES] = joint[at, :, :LANES] * joint[at, :, 2 * LANES : 3 * LANES]
            carried[at, here, LANES:] = joint[at, :, 3 * LANES : 4 * LANES] * joint[at, :, 4 * LANES :]

        def between(whole):
            halo = Halo(place, carried, pl.ds(tokens, HALO), buffers["tails"].at[layer], True)
            halo.start()
            run.saved()
            run.save(joint, saves[layer]["joint"])
            run.save(whole, saves[layer]["conv_whole"])
            halo.wait_recv()
            carried[:, :HALO] = buffers["tails"][layer]

            def block(b):
                keep_one, keep_two = keep[0, b], keep[1, b]
                for lane, lanes in both_lanes():
                    result = (
                        taps_ref[layer, 0:1, lanes] * carried[b, HALO - 2 : HALO - 2 + tokens, lanes] * keep_two
                        + taps_ref[layer, 1:2, lanes] * carried[b, HALO - 1 : HALO - 1 + tokens, lanes] * keep_one
                        + taps_ref[layer, 2:3, lanes] * carried[b, HALO : HALO + tokens, lanes]
                    )
                    mixed[b, :, lanes] = result
                    gated[b, :, lanes] = (c_columns(joint, b, lane) * result).astype(BF16)

            loop(8, block)
            halo.wait_send()
            for name in ("carried", "mixed", "gated"):
                run.save(buffers[name], saves[layer][name])

        def second(chip, j):
            return dot(rows_of(gated[pair(chip)]), out_w[:, tile(j)])

        def after(h, rows, total):
            middle = stream[rows] + total
            middles[layer][rows] = middle
            next_ref[rows] = rounded(middle, gains[2 * layer + 1])

        def before_second():
            load(layer, ("out_w",))
            if moving and layer + 1 < layers:
                scatter(layer + 1, "in_w")
            run.loaded("out_w")

        run.phase(next_ref, first, second, after, before_first, before_second, between)

    def ffn(layer):
        def before_first():
            load(layer, ("both_w",))
            run.loaded("both_w")

        def first(whole, chip):
            at = pair(chip)

            def columns(j):
                ups = pl.ds(pl.multiple_of(main + j * TILE, TILE), TILE)
                gate = dot(rows_of(whole[at]), both_w[:, tile(j)])
                up = dot(rows_of(whole[at]), both_w[:, ups])
                gate_up[at, :, tile(j)] = blocks_of(gate)
                gate_up[at, :, ups] = blocks_of(up)
                hidden[at, :, tile(j)] = blocks_of((gate * jax.nn.sigmoid(gate) * up).astype(BF16))

            loop(main // TILE, columns)
            both = dot(rows_of(whole[at]), both_w[:, 2 * main :])
            gate_up[at, :, 2 * main :] = blocks_of(both)
            lane = lax.broadcasted_iota(jnp.int32, both.shape, 1)
            tail = jnp.where(lane < LANES // 2, both * jax.nn.sigmoid(both) * swap_half(both), 0.0)
            hidden[at, :, main:] = blocks_of(tail.astype(BF16))

        def between(whole):
            run.saved()
            run.save(whole, saves[layer]["ffn_whole"])
            run.save(gate_up, saves[layer]["gate_up"])
            run.save(hidden, saves[layer]["hidden"])

        def second(chip, j):
            return dot(rows_of(hidden[pair(chip)]), down_w[:, tile(j)])

        def after(h, rows, total):
            result = middles[layer][rows] + total
            if layer + 1 < layers:
                sources[layer][rows] = result
                next_ref[rows] = rounded(result, gains[2 * layer + 2])
            else:
                stream_out[rows] = result

        def before_second():
            load(layer, ("down_w",))
            if moving and layer + 1 < layers:
                scatter(layer + 1, "both_w")
            run.loaded("down_w")

        run.phase(next_ref, first, second, after, before_first, before_second, between)

    if moving:
        cut(0, "in_w")
        rounds[0]["out_w"][...] = out_in[0].astype(BF16)
        run.enter([], True)
        kept = place.copy(small, spread.at[place.owner()])
        kept.start()
        spreads = [place.push(small, spread.at[place.owner()], device) for device, _ in every_other(place)]
        scatter(0, "in_w")
        for copy in spreads:
            copy.start()
        moves(0, ("out_w", "in_w", "both_w", "down_w"))
        run.launch(1)
        cut(0, "both_w")
        run.launch(8)
        scatter(0, "both_w")
        rounds[0]["down_w"][...] = down_in[0].astype(BF16)
        for layer in range(1, layers):
            cut(layer, "in_w")
            cut(layer, "both_w")
            rounds[layer]["out_w"][...] = out_in[layer].astype(BF16)
            rounds[layer]["down_w"][...] = down_in[layer].astype(BF16)
            moves(layer, WEIGHTS)
        kept.wait()
        for copy in spreads:
            copy.wait_recv()
        parameters()
        next_ref[...] = rounded(stream_in[...], gains[0])
    else:
        next_ref[...] = rounded(stream_in[...], gains[0])
        run.enter([], False)
    for layer in range(layers):
        conv(layer, sources[layer - 1] if layer else stream_in)
        ffn(layer)
    run.saved()
    for copy in place.sent:
        copy.wait_send()


class Several:
    def __init__(self, copies):
        self.copies = copies

    def wait(self):
        for copy in self.copies:
            copy.wait()


def whole_shape(mine):
    return (4, 2, 2, 2) + mine[2:] if len(mine) == 4 else (2, 2) + mine


def forward(stream, given, tall, moving, documents=0):
    tokens, features = stream.shape
    if moving:
        layers, owned = given[1].shape[:2]
        wide = (-(-3 * tall[0] // LANES) * LANES, 2 * tall[1])
    else:
        layers = given[1].shape[0]
        wide = (given[3].shape[1], given[5].shape[1])
    forms = forms_of(tokens, features, wide, tall, layers)
    inside = pl.BlockSpec(memory_space=pltpu.VMEM)
    anywhere = pl.BlockSpec(memory_space=pl.ANY)
    outs = [(forms["stream"], inside)] * (1 + layers + layers - 1)
    outs += [(forms[name], anywhere) for _ in range(layers) for name in SAVED]
    buffers = {name: forms[name] for name in ("joint", "carried", "mixed", "gated", "gate_up", "hidden", "next", "tails")}
    buffers |= {name: forms[name] for name in ("whole", "part", "sib", "yin", "yout", "zin", "zout")}
    buffers |= {"vmem_in_w": forms["in_w"], "vmem_both_w": forms["both_w"]}
    buffers |= {"vmem_out_w": ((forms["gated"][0][2], features), BF16), "vmem_down_w": forms["tall_w"]}
    scratch = [pltpu.VMEM(*form) for form in buffers.values()]
    if moving:
        columns = [(4, 2, owned, width) for width in wide]
        rows = [(owned, features), (tall[1] // 4, features)]
        wholes = [whole_shape(shape) for pair in zip(columns, rows) for shape in pair]
        outs += [((shape, BF16), anywhere) for _ in range(layers) for shape in wholes]
        outs += [(((2 * layers, 1, features), F32), inside), (((layers, HALO, forms["mixed"][0][2]), F32), inside)]
        outs.append((((2, 8, tokens, 1), F32), inside))
        scratch.append(pltpu.VMEM((32,) + given[0].shape, F32))
        scratch += [pltpu.VMEM((8, owned, width), BF16) for _ in range(layers) for width in wide]
        scratch += [pltpu.VMEM(shape, BF16) for _ in range(layers) for shape in columns]
        scratch += [pltpu.VMEM(shape, BF16) for _ in range(layers) for shape in rows]
    plan = {"layers": layers, "moving": moving, "buffers": tuple(buffers), "documents": documents}
    results = pl.pallas_call(
        functools.partial(forward_kernel, plan),
        out_shape=[jax.ShapeDtypeStruct(*form) for form, _ in outs],
        in_specs=[inside] * 7 if moving else [inside] * 4 + [anywhere] * (len(given) - 3),
        out_specs=[spec for _, spec in outs],
        scratch_shapes=scratch + [pltpu.SemaphoreType.DMA((SEMAPHORES,))] * 3,
        compiler_params=pltpu.CompilerParams(
            collective_id=COLLECTIVE_ID["forward"], has_side_effects=True, vmem_limit_bytes=62 << 20
        ),
        name="forward",
    )(stream, *given)
    stream_out, results = results[0], results[1:]
    middles, results = results[:layers], results[layers:]
    sources, results = results[: layers - 1], results[layers - 1 :]
    count = layers * len(SAVED)
    saved, results = results[:count], results[count:]
    if not moving:
        return stream_out, middles, sources, saved, given[3:], given[:3]
    return stream_out, middles, sources, saved, results[:-3], results[-3:]


def backward_kernel(plan, *refs):
    refs = list(refs)
    layers, moving, buffer_names = plan["layers"], plan["moving"], plan["buffers"]

    def take(count):
        taken = refs[:count]
        del refs[:count]
        return taken

    grad_out, gains, taps_ref, keep = take(4)
    middles, sources = take(layers), take(layers)
    weights = [dict(zip(WEIGHTS, take(4))) for _ in range(layers)]
    saves = [dict(zip(SAVED, take(len(SAVED)))) for _ in range(layers)]
    (grad_in,) = take(1)
    if moving:
        small_sum, grad_in_w, grad_out_w, gate_out, up_out, down_out = take(6)
    else:
        gain_out, taps_out = take(2)
        raw = [take(4) for _ in range(layers)]
    buffers = dict(zip(buffer_names, take(len(buffer_names))))
    if moving:
        landing = {name: take(5 if name in ("in_w", "both_w") else 4) for name in WEIGHTS}
        staging, slabs, slabs_in = take(2), *take(2)
        free = dict(zip(("both", "down", "conv"), take(3)))
    place = Place(*take(3))
    run = Pass(place, buffers)
    tokens, features = run.tokens, run.features
    rows_of, blocks_of, all_rows, pair = run.rows_of, run.blocks_of, run.all_rows, run.pair
    wide = {"in_w": plan["wide"][0], "both_w": plan["wide"][1]}
    joint, gate_up = buffers["gate_up"].at[:, :, : wide["in_w"]], buffers["gate_up"]
    grad_joint, grad_gate_up = buffers["grad_rows"].at[:, :, : wide["in_w"]], buffers["grad_rows"]
    in_w, both_w = buffers["wide_w"].at[:, : wide["in_w"]], buffers["wide_w"]
    channels, units = buffers["mixed"].shape[2], buffers["hidden"].shape[2]
    out_w, down_w = buffers["tall_w"].at[:channels], buffers["tall_w"]
    gated, hidden = buffers["hidden"].at[:, :, :channels], buffers["hidden"]
    carried, mixed, edges, grad_gated = (buffers[name] for name in ("carried", "mixed", "edges", "grad_gated"))
    kept_whole, next_ref, grad_ref, held = (buffers[name] for name in ("conv_whole", "next", "stream", "held"))
    gain_grads, tap_grads = buffers["gain_grads"], buffers["tap_grads"]
    main = gate_up.shape[2] // (2 * LANES) * LANES

    def load_rows(name, source, target):
        if len(source.shape) == 2:
            run.load(name, source, target)
            return
        rows, lead = source.shape[-2], source.shape[:-2]
        copies = []
        for n, index in enumerate(itertools.product(*(range(size) for size in lead))):
            copies.append(place.copy(source.at[index], target.at[pl.ds(n * rows, rows)]))
            copies[-1].start()
        filled = rows * len(copies)
        if filled < target.shape[0]:
            target[filled:] = jnp.zeros((target.shape[0] - filled, target.shape[1]), BF16)
        run.loading[name] = Several(copies)

    def deliver_columns(outs, layer, views):
        def deliver(landed):
            run.saved()
            shards_to(landed, views)
            for source, out in outs:
                run.save(source, out.at[layer])

        return deliver

    def deliver_rows(out, layer):
        def deliver(final):
            run.save(final, out.at[layer])

        return deliver

    reduced = {"both": 0, "down": 0, "conv": 0}
    under_way = {"both": [], "down": [], "conv": []}

    def reduce(layer, kind, names):
        if not moving:
            for name in names:
                source = buffers["grad_" + name]
                target = raw[layer][WEIGHTS.index(name)]
                run.save(source.at[: target.shape[0]] if source.shape != target.shape else source, target)
            return
        if reduced[kind]:
            pl.semaphore_wait(free[kind], 9)
        reduced[kind] += 1
        run.saved()
        items = []
        for name in names:
            if name == "in_w":
                width = features
                views = [staging[0].at[:, i * width : (i + 1) * width] for i in range(3)]
                deliver = deliver_columns([(staging[0], grad_in_w)], layer, views)
            elif name == "both_w":
                deliver = deliver_columns([(staging[0], gate_out), (staging[1], up_out)], layer, list(staging))
            else:
                deliver = deliver_rows(grad_out_w if name == "out_w" else down_out, layer)
            total = buffers["grad_" + name]
            if name in ("out_w", "down_w"):
                total = total.at[: 4 * landing[name][3].shape[0]]
            items.append(Reduce(place, total, landing[name], deliver))
            items[-1].start()
        run.begin(items)
        under_way[kind] = items

    def settle(kind):
        items, under_way[kind] = under_way[kind], []
        run.settle(items)
        if items and reduced[kind] < layers:
            for device in [place.member(flips) for flips in FLIPS] + [place.beside("zh"), place.beside("x")]:
                pl.semaphore_signal(free[kind], inc=1, device_id=device, device_id_type=MESH)

    def step_back(h, rows, total, stream, gain, row):
        scale = rms_scale(stream)
        gain_grad = jnp.sum(total * stream * scale, axis=0, keepdims=True)
        gain_grads[row : row + 1] = gain_grad if h == 0 else gain_grads[row : row + 1] + gain_grad
        scaled = total * gain
        grad = (
            grad_ref[rows]
            + scale * scaled
            - stream * (scale * scale * scale) * jnp.mean(scaled * stream, axis=-1, keepdims=True)
        )
        grad_ref[rows] = grad
        next_ref[rows] = grad.astype(BF16)
        return grad

    def ffn_back(layer):
        def before_first():
            load_rows("down_w", weights[layer]["down_w"], down_w)
            run.load("gate_up", saves[layer]["gate_up"], gate_up)
            load_rows("both_w", weights[layer]["both_w"], both_w)
            run.load("hidden", saves[layer]["hidden"], hidden)
            run.load("whole", saves[layer]["ffn_whole"], kept_whole)
            run.load("held", middles[layer], held)
            run.loaded("down_w", "gate_up")

        def grads(grad_hidden, gate, up):
            sigmoid = jax.nn.sigmoid(gate)
            return grad_hidden * up * sigmoid * (1.0 + gate * (1.0 - sigmoid)), grad_hidden * gate * sigmoid

        def first(whole, chip):
            at = pair(chip)

            def columns(j):
                ups = pl.ds(pl.multiple_of(main + j * TILE, TILE), TILE)
                grad_hidden = dot_cols(rows_of(whole[at]), down_w[tile(j), :])
                gate, up = (rows_of(gate_up[at, :, lanes]) for lanes in (tile(j), ups))
                grad_gate, grad_up = grads(grad_hidden, gate, up)
                grad_gate_up[at, :, tile(j)] = blocks_of(grad_gate.astype(BF16))
                grad_gate_up[at, :, ups] = blocks_of(grad_up.astype(BF16))

            loop(main // TILE, columns)
            grad_hidden = dot_cols(rows_of(whole[at]), down_w[main:, :])
            both = rows_of(gate_up[at, :, 2 * main :])
            grad_gate, grad_up = grads(grad_hidden, both, swap_half(both))
            grad_gate_up[at, :, 2 * main :] = blocks_of((grad_gate + swap_half(grad_up)).astype(BF16))

        def second(chip, j):
            return dot_cols(rows_of(grad_gate_up[pair(chip)]), both_w[tile(j), :])

        def aside(whole):
            run.loaded("whole", "hidden")
            settle("both")
            settle("down")
            grad_both, grad_down = buffers["grad_both_w"], buffers["grad_down_w"]
            width = features // 4

            def both_rows(c):
                left = all_rows(kept_whole[:, :, tile(c, width)])
                result = dot_rows(left, all_rows(grad_gate_up[...])).astype(BF16)
                grad_both[c] = result.reshape(grad_both.shape[1:])

            def down_rows(j):
                left = all_rows(hidden[:, :, tile(j, LANES)])
                grad_down[tile(j, LANES), :] = dot_rows(left, all_rows(whole[...])).astype(BF16)

            loop(4, both_rows)
            reduce(layer, "both", ("both_w",))
            loop(units // LANES, down_rows)
            reduce(layer, "down", ("down_w",))

        def after(h, rows, total):
            step_back(h, rows, total, held[rows], gains[2 * layer + 1], 2 * layer + 1)

        run.phase(next_ref, first, second, after, before_first, lambda: run.loaded("both_w", "held"), None, aside)

    def conv_back(layer):
        taps = taps_ref.at[layer]

        def before_first():
            load_rows("out_w", weights[layer]["out_w"], out_w)
            for name, target in (("joint", joint), ("carried", carried), ("mixed", mixed)):
                run.load(name, saves[layer][name], target)
            load_rows("in_w", weights[layer]["in_w"], in_w)
            run.load("gated", saves[layer]["gated"], gated)
            run.load("whole", saves[layer]["conv_whole"], kept_whole)
            run.load("held", sources[layer], held)
            run.loaded("out_w")

        def first(whole, chip):
            at = pair(chip)
            grad_gated[at] = blocks_of(dot_cols(rows_of(whole[at]), out_w[...]))

        def between(whole):
            run.loaded("joint", "carried", "mixed")
            tap_grads[layer] = jnp.zeros(tap_grads.shape[1:], F32)

            def block(b):
                keep_one, keep_two = keep[0, b], keep[1, b]
                for lane, lanes in both_lanes():
                    grad_value = grad_gated[b, :, lanes]
                    grad_mixed = grad_value * c_columns(joint, b, lane)
                    first_tap, second_tap = grad_mixed * keep_two, grad_mixed * keep_one
                    edges[0, b, :tokens, lanes] = second_tap * taps[1:2, lanes]
                    edges[1, b, :tokens, lanes] = first_tap * taps[0:1, lanes]
                    mixed[b, :, lanes] = grad_value * mixed[b, :, lanes]
                    grad_gated[b, :, lanes] = grad_mixed * taps[2:3, lanes]
                    for row, grad, back_by in ((0, first_tap, 2), (1, second_tap, 1), (2, grad_mixed, 0)):
                        tap_in = carried[b, HALO - back_by : HALO - back_by + tokens, lanes]
                        tap_grads[layer, row : row + 1, lanes] += jnp.sum(grad * tap_in, axis=0, keepdims=True)

            loop(8, block)
            halo = Halo(place, edges, pl.ds(0, HALO), buffers["heads"].at[layer], False)
            halo.start()
            halo.wait_recv()
            edges[:, :, tokens:] = buffers["heads"][layer]

            def block_after(b):
                for lane, lanes in both_lanes():
                    grad_carried = (
                        grad_gated[b, :, lanes] + edges[0, b, 1 : 1 + tokens, lanes] + edges[1, b, 2 : 2 + tokens, lanes]
                    )
                    grad_c = mixed[b, :, lanes]
                    if lane == 0:
                        grad_joint[b, :, :LANES] = (grad_carried * joint[b, :, 2 * LANES : 3 * LANES]).astype(BF16)
                        grad_joint[b, :, LANES : 2 * LANES] = grad_c.astype(BF16)
                        grad_joint[b, :, 2 * LANES : 3 * LANES] = (grad_carried * joint[b, :, :LANES]).astype(BF16)
                    else:
                        grad_b = grad_carried * joint[b, :, 4 * LANES :]
                        grad_joint[b, :, 3 * LANES : 4 * LANES] = (grad_b + swap_half(grad_c)).astype(BF16)
                        grad_joint[b, :, 4 * LANES :] = (grad_carried * joint[b, :, 3 * LANES : 4 * LANES]).astype(BF16)

            loop(8, block_after)
            halo.wait_send()
            if layer == 0:
                gradients(whole)

        def second(chip, j):
            return dot_cols(rows_of(grad_joint[pair(chip)]), in_w[tile(j), :])

        def gradients(whole):
            run.loaded("whole", "gated")
            settle("conv")
            grad_in_rows, grad_out_rows = buffers["grad_in_w"], buffers["grad_out_w"]
            width = features // 4

            def in_rows(c):
                left = all_rows(kept_whole[:, :, tile(c, width)])
                result = dot_rows(left, all_rows(grad_joint[...])).astype(BF16)
                grad_in_rows[c] = result.reshape(grad_in_rows.shape[1:])

            def out_rows(j):
                left = all_rows(gated[:, :, tile(j, LANES)])
                grad_out_rows[tile(j, LANES), :] = dot_rows(left, all_rows(whole[...])).astype(BF16)

            loop(4, in_rows)
            loop(channels // LANES, out_rows)
            reduce(layer, "conv", ("in_w", "out_w"))

        def after(h, rows, total):
            grad = step_back(h, rows, total, held[rows], gains[2 * layer], 2 * layer)
            if layer == 0:
                grad_in[rows] = grad

        run.phase(
            next_ref, first, second, after, before_first, lambda: run.loaded("in_w", "held"), between, gradients if layer else None
        )

    grad_ref[...] = grad_out[...]
    next_ref[...] = grad_out[...].astype(BF16)
    run.enter([], moving)
    for layer in reversed(range(layers)):
        ffn_back(layer)
        conv_back(layer)
    if moving:
        owned = features // 32
        slabs[...] = jnp.zeros(slabs.shape, F32)
        for owner in range(32):
            slabs[owner, : 2 * layers, :owned] = gain_grads[:, owner * owned : (owner + 1) * owned]
        for layer in range(layers):
            row = 2 * layers + 3 * layer
            for zh, x in itertools.product(range(2), repeat=2):
                owner = ((place.yl * 2 + place.core) * 2 + zh) * 4 + place.zl * 2 + x
                low = (zh * 2 + x) * owned
                slabs[owner, row : row + 3, :owned] = tap_grads[layer, :3, low : low + owned]
        copies = []
        for i, (device, flips) in enumerate(every_other(place)):
            copies.append(place.push(slabs.at[place.owner(flips)], slabs_in.at[i], device))
            copies[-1].start()
        run.launch(len(run.queue))
        for kind in ("both", "down", "conv"):
            settle(kind)
        for copy in copies:
            copy.wait_recv()
        small_sum[...] = slabs[place.owner()] + jnp.sum(slabs_in[...], axis=0)
    else:
        gain_out[...] = gain_grads[...]
        taps_out[...] = tap_grads[...]
    run.saved()
    for copy in place.sent:
        copy.wait_send()


def backward(grad_out, gains, taps, keep, middles, sources, weights, saved, tall, moving):
    tokens, features = grad_out.shape
    layers = taps.shape[0]
    wide = (weights[0][0].shape[-1], weights[0][2].shape[-1])
    forms = forms_of(tokens, features, wide, tall, layers)
    inside = pl.BlockSpec(memory_space=pltpu.VMEM)
    anywhere = pl.BlockSpec(memory_space=pl.ANY)
    owned = features // 32
    outs = [(forms["stream"], inside)]
    if moving:
        outs.append((((16, LANES), F32), inside))
        shapes = ((owned, 3 * features), (owned, features), (owned, 4 * tall[1] * 2), (owned, 4 * tall[1] * 2), (tall[1] // 4, features))
        outs += [(((layers,) + shape, F32), anywhere) for shape in shapes]
    else:
        outs.append((((2 * layers, features), F32), inside))
        outs.append((((layers, HALO, forms["mixed"][0][2]), F32), inside))
        for _ in range(layers):
            for name in WEIGHTS:
                shape = forms["grad_" + name][0]
                outs.append((((tall[0] if name == "out_w" else tall[1], features) if len(shape) == 2 else shape, BF16), anywhere))
    names = ("conv_whole", "gate_up", "carried", "mixed", "hidden", "grad_rows", "grad_gated", "edges", "heads", "tall_w")
    names += ("next", "stream", "whole", "part", "sib", "yin", "yout", "zin", "zout")
    names += ("grad_in_w", "grad_both_w", "grad_out_w", "grad_down_w")
    buffers = {name: forms[name] for name in names}
    buffers["wide_w"], buffers["held"] = forms["both_w"], forms["stream"]
    buffers["gain_grads"] = ((2 * layers, features), F32)
    buffers["tap_grads"] = ((layers, HALO, forms["mixed"][0][2]), F32)
    scratch = [pltpu.VMEM(*form) for form in buffers.values()]
    if moving:
        for name in WEIGHTS:
            shape = forms["grad_" + name][0]
            if len(shape) == 2:
                shape = (tall[0] if name == "out_w" else tall[1], features)
            scratch += [pltpu.VMEM(*form) for form in landing_shapes(shape)]
        scratch += [pltpu.VMEM((owned, 3 * features), F32)] * 2
        scratch += [pltpu.VMEM((32, 16, LANES), F32), pltpu.VMEM((31, 16, LANES), F32)]
        scratch += [pltpu.SemaphoreType.REGULAR] * 3
    operands = list(middles) + list(sources) + [array for group in weights for array in group] + list(saved)
    plan = {"layers": layers, "moving": moving, "buffers": tuple(buffers), "wide": wide}
    return pl.pallas_call(
        functools.partial(backward_kernel, plan),
        out_shape=[jax.ShapeDtypeStruct(*form) for form, _ in outs],
        in_specs=[inside] * 4 + [anywhere] * len(operands),
        out_specs=[spec for _, spec in outs],
        scratch_shapes=scratch + [pltpu.SemaphoreType.DMA((SEMAPHORES,))] * 3,
        compiler_params=pltpu.CompilerParams(
            collective_id=COLLECTIVE_ID["backward"], has_side_effects=True, vmem_limit_bytes=63 << 20
        ),
        name="backward",
    )(grad_out, gains, taps, keep, *operands)


def sizes_of(axes):
    return tuple(lax.axis_size(axis) for axis in axes)


def split_owners(array, dim):
    owners = sizes_of(OWNERS)
    count = 1
    for size in owners:
        count *= size
    shape = array.shape
    return array.reshape(shape[:dim] + owners + (shape[dim] // count,) + shape[dim + 1 :])


def column_shards(weights):
    rows = weights[0].shape[0]
    mains, rests = [], []
    for weight in weights:
        parts = split_owners(weight, 1).transpose(5, 2, 3, 0, 1, 4, 6, 7).reshape(8, rows, -1)
        main = parts.shape[2] // LANES * LANES
        mains.append(parts[:, :, :main])
        rests.append(parts[:, :, main:])
    shards = jnp.concatenate(mains + rests, axis=2)
    return jnp.pad(shards, ((0, 0), (0, 0), (0, -shards.shape[2] % LANES)))


def column_whole(shards, groups, width):
    rows = shards.shape[1]
    yh, yl, core, zh, zl, x = sizes_of(OWNERS)
    wholes = []
    for group in range(groups):
        part = jnp.concatenate(
            [shards[..., a:b] for a, b in pieces_of(groups, width, group, 0, width)], axis=-1
        ).reshape(zl, yl, core, rows, yh, zh, x, -1)
        wholes.append(part.transpose(3, 4, 1, 2, 5, 0, 6, 7).reshape(rows, -1))
    return wholes


def gather_columns(shards):
    mine = lax.all_to_all(shards, TP, split_axis=0, concat_axis=0, tiled=True)
    whole = lax.all_gather(mine, DP, axis=0, tiled=False)
    yh, yl, core, zh, zl, x = sizes_of(OWNERS)
    rows, columns = shards.shape[1:]
    whole = whole.reshape(yh, zh, x, zl, yl, core, rows, columns)
    return whole.transpose(0, 4, 5, 1, 3, 2, 6, 7).reshape(-1, columns)


def scatter_columns(total):
    yh, yl, core, zh, zl, x = sizes_of(OWNERS)
    columns = total.shape[1]
    parts = split_owners(total, 0).transpose(0, 3, 5, 4, 1, 2, 6, 7)
    parts = parts.reshape(yh * zh * x, -1, columns)
    mine = lax.psum_scatter(parts, DP, scatter_dimension=0, tiled=False)
    mine = mine.reshape(8, -1, columns)
    return lax.all_to_all(mine, TP, split_axis=0, concat_axis=0, tiled=True)


def tap_masks(starts, token_count):
    zh, x, x_size = lax.axis_index("zh"), lax.axis_index("x"), lax.axis_size("x")
    blocks = (zh * 2 + jnp.arange(2, dtype=jnp.int32)) * x_size + x
    places = blocks[:, None] * token_count + jnp.arange(token_count, dtype=jnp.int32)

    def segment_of(where):
        return jnp.sum((starts[None, :, None, :] <= where[:, None, :, None]).astype(jnp.int32), axis=3)

    own_segment = segment_of(places)
    keep_one = (segment_of(places - 1) == own_segment).astype(F32)
    keep_two = (segment_of(places - 2) == own_segment).astype(F32)
    return keep_one.reshape(8, token_count, 1), keep_two.reshape(8, token_count, 1)


def local(stream_in, doc_starts, norm_mix, in_proj, conv_taps, out_proj, norm_ffn, w_gate, w_up, w_down, grad_out):
    _, token_count, features = stream_in.shape
    layers = norm_mix.shape[0]
    own_kernels = sizes_of(DP) == (1, 2, 2)
    stream = stream_in.reshape(-1, features)
    grad_stream = grad_out.reshape(-1, features)
    small = jnp.concatenate([norm_mix[:, None], norm_ffn[:, None], conv_taps.transpose(0, 2, 1)], axis=1)
    small = small.astype(BF16).astype(F32)
    owned = small.shape[2]
    tall = (features // 8, w_gate.shape[2] // 8)
    if own_kernels:
        packed = jnp.zeros((16, LANES), F32).at[: 5 * layers, :owned].set(small.reshape(-1, owned))
        packed = packed.at[15, : doc_starts.shape[1]].set(doc_starts[0].astype(F32))
        given = (packed, in_proj, w_gate, w_up, out_proj, w_down)
    else:
        starts = lax.all_gather(doc_starts, ("yl", "core"), axis=0, tiled=True)
        small = small.astype(BF16)
        gains = lax.all_gather(small[:, :2], OWNERS, axis=2, tiled=True).astype(F32).reshape(2 * layers, 1, features)
        taps = lax.all_gather(small[:, 2:], DP, axis=2, tiled=True).astype(F32)
        taps = jnp.pad(taps, ((0, 0), (0, HALO - 3), (0, -taps.shape[2] % LANES)))
        given = (gains, taps, jnp.stack(tap_masks(starts, token_count)))
        for layer in range(layers):
            in_w = gather_columns(column_shards(jnp.split(in_proj[layer].astype(BF16), 3, axis=1)))
            both_w = gather_columns(column_shards([w_gate[layer].astype(BF16), w_up[layer].astype(BF16)]))
            out_w = lax.all_gather(out_proj[layer].astype(BF16), DP, axis=0, tiled=True)
            down_w = lax.all_gather(w_down[layer].astype(BF16), DP, axis=0, tiled=True)
            given += (in_w, out_w, both_w, down_w)

    stream_out, middles, sources, saved, weights, params = forward(stream, given, tall, own_kernels, doc_starts.shape[1])
    weights = [tuple(weights[4 * layer : 4 * layer + 4]) for layer in range(layers)]
    grad_in, *results = backward(
        grad_stream, *params, middles, [stream] + list(sources), weights, saved, tall, own_kernels
    )
    if own_kernels:
        small_sums, grad_in_w, grad_out_w, grad_gate, grad_up, grad_down = results
        small_sums = small_sums[:, :owned]
        gain_grads = small_sums[: 2 * layers].reshape(layers, 2, owned)
        tap_grads = small_sums[2 * layers : 5 * layers].reshape(layers, 3, owned)
    else:
        gain_grads, tap_grads, *raw = results
        gain_grads = lax.psum_scatter(gain_grads, OWNERS, scatter_dimension=1, tiled=True).reshape(layers, 2, -1)
        tap_grads = lax.psum_scatter(tap_grads[:, :3, : tall[0]], DP, scatter_dimension=2, tiled=True)
        sums = []
        for layer in range(layers):
            grad_in_w, grad_out_w, grad_both, grad_down = raw[4 * layer : 4 * layer + 4]
            columns = [
                column_whole(scatter_columns(grad.reshape(features, -1)).astype(F32), groups, width)
                for grad, groups, width in ((grad_in_w, 3, tall[0]), (grad_both, 2, tall[1]))
            ]
            rows = [
                lax.psum_scatter(grad, DP, scatter_dimension=0, tiled=True).astype(F32) for grad in (grad_out_w, grad_down)
            ]
            sums.append((jnp.concatenate(columns[0], axis=1), rows[0], *columns[1], rows[1]))
        grad_in_w, grad_out_w, grad_gate, grad_up, grad_down = (jnp.stack(parts) for parts in zip(*sums))
    return (
        stream_out[None],
        grad_in[None],
        gain_grads[:, 0],
        grad_in_w,
        tap_grads.transpose(0, 2, 1),
        grad_out_w,
        gain_grads[:, 1],
        grad_gate,
        grad_up,
        grad_down,
    )


def solution(mesh):
    dp, seq = mesh.shape["dp"], mesh.shape["seq"]
    side = dp // 2
    split = Mesh(mesh.devices.reshape(side // 2, 2, 2, seq // side // 2, 2, side), OWNERS)
    token = P(ROW_AXES, SEQ_AXES, None)
    vector = P(None, OWNERS)
    matrix = P(None, OWNERS, None)
    return jax.shard_map(
        local,
        mesh=split,
        in_specs=(token, P(ROW_AXES, None), vector, matrix, matrix, matrix, vector, matrix, matrix, matrix, token),
        out_specs=(token, token, vector, matrix, matrix, matrix, vector, matrix, matrix, matrix),
        check_vma=False,
    )
```

```python
import functools
import itertools

import jax
import jax.numpy as jnp
from jax import lax
from jax.experimental import pallas as pl
from jax.experimental.pallas import tpu as pltpu
from jax.sharding import Mesh, PartitionSpec as P

EPSILON = 1e-05
TP = ("zl", "yl", "core")
DP = ("yh", "zh", "x")
ROW_AXES = ("yh", "yl", "core")
SEQ_AXES = ("zh", "zl", "x")
OWNERS = ROW_AXES + SEQ_AXES
BF16 = jnp.bfloat16
F32 = jnp.float32
MESH = pl.DeviceIdType.MESH
HALVES = 2
COLLECTIVE_ID = {"forward": 0, "backward": 1}
FLIPS = ((1, 1, 1), (1, 1, 0), (1, 0, 1), (1, 0, 0), (0, 1, 1), (0, 1, 0), (0, 0, 1))
OTHERS = tuple(itertools.product((0, 1), repeat=5))[1:]
OTHER_AXES = ("yl", "core", "zh", "zl", "x")
SEMAPHORES = 288
FORWARD_PACE = ((1, 1),) * 7 + ((1, 0),) + ((1, 1),) * 3
BACKWARD_PACE = ((1, 1), (1, 2)) + ((2, 1),) * 8 + ((1, 1),)
LANES = 128
TILE = 256
HALO = 8


def rms_scale(values):
    return lax.rsqrt(jnp.mean(values * values, axis=-1, keepdims=True) + EPSILON)


class Place:
    def __init__(self, send, recv, local):
        self.zl, self.yl, self.core = (lax.axis_index(axis) for axis in TP)
        self.zh, self.x = lax.axis_index("zh"), lax.axis_index("x")
        self.send, self.recv, self.local = send, recv, local
        self.remote_count = self.local_count = 0
        self.sent = []

    def rank(self, flip_z, flip_y, flip_core):
        return self.flipped("zl", flip_z) * 4 + self.flipped("yl", flip_y) * 2 + self.flipped("core", flip_core)

    def flipped(self, axis, flip):
        return 1 - getattr(self, axis) if flip else getattr(self, axis)

    def member(self, flips):
        return {axis: 1 - getattr(self, axis) for axis, flip in zip(TP, flips) if flip}

    def beside(self, axis):
        return {axis: 1 - getattr(self, axis)}

    def owner(self, flips=(0,) * 5):
        index = 0
        for axis, flip in zip(OTHER_AXES, flips):
            index = index * 2 + self.flipped(axis, flip)
        return index

    def push(self, src, dst, device, kept=True):
        index = self.remote_count
        self.remote_count += 1
        assert index < SEMAPHORES
        copy = pltpu.make_async_remote_copy(
            src_ref=src, dst_ref=dst, send_sem=self.send.at[index], recv_sem=self.recv.at[index],
            device_id=device, device_id_type=MESH,
        )
        if kept:
            self.sent.append(copy)
        return copy

    def copy(self, src, dst):
        index = self.local_count
        self.local_count += 1
        return pltpu.make_async_copy(src, dst, self.local.at[index])


def pieces_of(groups, width, group, low, high):
    main = width // LANES * LANES
    rest = width - main
    ranges = []
    if low < main:
        ranges.append((group * main + low, group * main + min(high, main)))
    if high > main:
        start = groups * main + group * rest - main
        ranges.append((start + max(low, main), start + high))
    return ranges


def shards_from(weights, out):
    width = weights[0].shape[1] // 8
    block = width // 4
    main = width // LANES * LANES
    rest = width - main
    for group, weight in enumerate(weights):
        for member in range(8):
            zl, others = member // 4, member % 4
            starts = [((others * 2 + zh) * 4 + zl * 2 + x) * block for zh in range(2) for x in range(2)]
            values = jnp.concatenate([weight[:, start : start + block] for start in starts], axis=1).astype(BF16)
            out[member, :, group * main : (group + 1) * main] = values[:, :main]
            if rest:
                low = len(weights) * main + group * rest
                out[member, :, low : low + rest] = values[:, main:]
    pad = out.shape[2] - len(weights) * width
    if pad:
        out[:, :, len(weights) * width :] = jnp.zeros((8, out.shape[1], pad), BF16)


def shards_to(shards, outs):
    groups, width = len(outs), outs[0].shape[1] // 8
    block = width // 4
    for group, out in enumerate(outs):
        for others in range(4):
            for zh in range(2):
                values = []
                for zl in range(2):
                    for x in range(2):
                        low = (zh * 2 + x) * block
                        for start, end in pieces_of(groups, width, group, low, low + block):
                            values.append(shards[zl * 4 + others, :, start:end].astype(F32))
                start = (others * 2 + zh) * 4 * block
                out[:, start : start + 4 * block] = jnp.concatenate(values, axis=1)


def every_other(place):
    return [
        ({axis: place.flipped(axis, 1) for axis, flip in zip(OTHER_AXES, flips) if flip}, flips) for flips in OTHERS
    ]


class Gather:
    def __init__(self, place, mine, whole):
        self.ready = None
        x, own, other = place.x, place.zh, 1 - place.zh
        if len(whole.shape) == 6:
            parts = [
                (mine.at[c, zl], whole.at[c, own, zl, x], whole.at[c, other, zl, x])
                for c in range(4)
                for zl in range(2)
            ]
        else:
            count = whole.shape[2]
            size = 48 if count % 48 == 0 else count
            parts = [
                (mine.at[rows], whole.at[own, x, rows], whole.at[other, x, rows])
                for rows in (pl.ds(low, size) for low in range(0, count, size))
            ]
        self.along_z = [place.push(src, here, place.beside("zh")) for src, here, _ in parts]
        self.along_x = [place.push(src, here, place.beside("x")) for src, here, _ in parts]
        self.onward = [place.push(there, there, place.beside("x")) for _, _, there in parts]
        self.kept = [place.copy(src, here) for src, here, _ in parts]

    def pairs(self):
        def launch(c):
            if c == 0 and self.ready is not None:
                self.ready()
            self.along_z[c].start()
            self.along_x[c].start()
            self.kept[c].start()

        def land(c):
            self.along_z[c].wait_recv()
            self.onward[c].start()

        return [(functools.partial(launch, c), functools.partial(land, c)) for c in range(len(self.kept))]

    def finish(self):
        for c in range(len(self.kept)):
            self.along_x[c].wait_recv()
            self.onward[c].wait_recv()
            self.kept[c].wait()


class Reduce:
    def __init__(self, place, total, landing, deliver):
        self.columns = len(total.shape) == 6
        self.place, self.total, self.deliver = place, total, deliver
        self.xin, self.zout, self.zin, self.final = landing[:4]
        self.landed = landing[4] if self.columns else None
        x, zh, beside = place.x, place.zh, place.beside
        self.flips = FLIPS + ((0, 0, 0),)
        self.chunks = self.zin.shape[0]
        self.along_x = [
            [
                place.push(self.part(j, to_zh, 1 - x), self.xin.at[j, i], beside("x"), False)
                for i, to_zh in enumerate((1 - zh, zh))
            ]
            for j in range(self.chunks)
        ]
        self.along_z = [place.push(self.zout.at[j], self.zin.at[j], beside("zh"), False) for j in range(self.chunks)]
        if self.columns:
            here = self.landed.at[place.rank(0, 0, 0)]
            self.back = [place.push(self.final.at[j], here, place.member(flips), False) for j, flips in enumerate(FLIPS)]
            self.back.append(place.copy(self.final.at[7], here))

    def part(self, j, zh, x):
        if self.columns:
            flip_z, flip_y, flip_core = self.flips[j]
            place = self.place
            chunk = place.flipped("yl", flip_y) * 2 + place.flipped("core", flip_core)
            return self.total.at[chunk, zh, place.flipped("zl", flip_z), x]
        count = self.zin.shape[1]
        low = ((zh * 2 + x) * self.chunks + j) * count
        return self.total.at[pl.ds(pl.multiple_of(low, 16), count)]

    def start(self):
        for copies in self.along_x:
            for copy in copies:
                copy.start()

    def pairs(self):
        x, zh = self.place.x, self.place.zh

        def launch(j):
            for copy in self.along_x[j]:
                copy.wait_recv()
            self.zout[j] = (self.part(j, 1 - zh, x)[...].astype(F32) + self.xin[j, 0].astype(F32)).astype(BF16)
            self.along_z[j].start()

        def land(j):
            self.along_z[j].wait_recv()
            total = self.part(j, zh, x)[...].astype(F32) + self.xin[j, 1].astype(F32) + self.zin[j].astype(F32)
            if self.columns:
                self.final[j] = total.astype(BF16)
                self.back[j].start()
            else:
                count = self.zin.shape[1]
                self.final[j * count : (j + 1) * count] = total

        return [(functools.partial(launch, j), functools.partial(land, j)) for j in range(self.chunks)]

    def finish(self):
        if self.columns:
            for copy in self.back[:-1]:
                copy.wait_recv()
            self.back[-1].wait()
        sent = [copy for copies in self.along_x for copy in copies] + self.along_z
        for copy in sent + (self.back[:-1] if self.columns else []):
            copy.wait_send()
        self.deliver(self.landed if self.columns else self.final)


def landing_shapes(total):
    if len(total) == 6:
        rows = total[4:]
        return [((8, 2) + rows, BF16)] + [((8,) + rows, BF16)] * 4
    count = total[0] // 4
    size = 48 if count % 48 == 0 else count
    rows = (size,) + total[1:]
    chunks = (count // size,)
    return [(chunks + (2,) + rows, BF16), (chunks + rows, BF16), (chunks + rows, BF16), ((count,) + total[1:], F32)]


def loop(count, body):
    def step(i, carry):
        body(i)
        return carry

    lax.fori_loop(0, count, step, 0)


def tile(i, width=TILE):
    return pl.ds(pl.multiple_of(i * width, width), width)


def dot(left, right):
    return jnp.dot(left, right, preferred_element_type=F32)


def dot_cols(left, right):
    return lax.dot_general(left, right, (((1,), (1,)), ((), ())), preferred_element_type=F32)


def dot_rows(left, right):
    return lax.dot_general(left, right, (((0,), (0,)), ((), ())), preferred_element_type=F32)


def swap_half(values):
    return pltpu.roll(values, LANES // 2, 1)


class Halo:
    def __init__(self, place, buffer, edge, landing, forward):
        x, zh, count = place.x, place.zh, lax.axis_size("x")
        first, final = x == 0, x == count - 1
        low, high, every = pl.ds(0, 4), pl.ds(4, 4), pl.ds(0, 8)
        lead = (slice(None),) * (len(buffer.shape) - 3)
        step = lax.rem(x + 1, count) if forward else lax.rem(x + count - 1, count)
        if forward:
            within, turn, beyond = jnp.logical_not(final), final, jnp.logical_and(final, zh == 0)
            into, turned, entered = jnp.logical_not(first), first, jnp.logical_and(first, zh == 1)
            sent, landed = low, high
        else:
            within, turn, beyond = jnp.logical_not(first), first, jnp.logical_and(first, zh == 1)
            into, turned, entered = jnp.logical_not(final), final, jnp.logical_and(final, zh == 0)
            sent, landed = high, low

        def push(src, dst, device):
            return place.push(buffer.at[lead + (src, edge)], landing.at[lead + (dst,)], device, False)

        copies = [
            push(every, every, {"x": step}),
            push(sent, landed, {"x": step}),
            push(landed, sent, {"x": step, "zh": 1 - zh}),
        ]
        self.sends = list(zip((within, turn, beyond), copies))
        self.lands = list(zip((into, turned, entered), copies))
        self.unreached = jnp.logical_and(turned, jnp.logical_not(entered))
        self.landing, self.open_end = landing, lead + (sent,)

    def start(self):
        for condition, copy in self.sends:
            pl.when(condition)(copy.start)

        @pl.when(self.unreached)
        def _():
            shape = self.landing.at[self.open_end].shape
            self.landing[self.open_end] = jnp.zeros(shape, self.landing.dtype)

    def wait_recv(self):
        for condition, copy in self.lands:
            pl.when(condition)(copy.wait_recv)

    def wait_send(self):
        for condition, copy in self.sends:
            pl.when(condition)(copy.wait_send)


SAVED = ("conv_whole", "joint", "carried", "mixed", "gated", "ffn_whole", "gate_up", "hidden")
WEIGHTS = ("in_w", "out_w", "both_w", "down_w")


def forms_of(tokens, features, wide, tall, layers):
    channels, units = (-(-rows // LANES) * LANES for rows in tall)
    block = (tokens, features)
    return {
        "in_w": ((features, wide[0]), BF16),
        "both_w": ((features, wide[1]), BF16),
        "out_w": ((tall[0], features), BF16),
        "down_w": ((tall[1], features), BF16),
        "conv_whole": ((8,) + block, BF16),
        "ffn_whole": ((8,) + block, BF16),
        "joint": ((8, tokens, wide[0]), F32),
        "gate_up": ((8, tokens, wide[1]), F32),
        "carried": ((8, tokens + HALO, channels), F32),
        "mixed": ((8, tokens, channels), F32),
        "gated": ((8, tokens, channels), BF16),
        "hidden": ((8, tokens, units), BF16),
        "tall_w": ((units, features), BF16),
        "grad_rows": ((8, tokens, wide[1]), BF16),
        "grad_gated": ((8, tokens, channels), F32),
        "edges": ((2, 8, tokens + HALO, channels), F32),
        "heads": ((layers, 2, 8, HALO, channels), F32),
        "tails": ((layers, 8, HALO, channels), F32),
        "stream": (block, F32),
        "next": (block, BF16),
        "whole": ((2, 8) + block, BF16),
        "part": ((4, 2) + block, BF16),
        "sib": ((4,) + block, BF16),
        "yin": ((2,) + block, BF16),
        "yout": ((2,) + block, BF16),
        "zin": (block, BF16),
        "zout": (block, BF16),
        "grad_in_w": ((4, 2, 2, 2, features // 32, wide[0]), BF16),
        "grad_both_w": ((4, 2, 2, 2, features // 32, wide[1]), BF16),
        "grad_out_w": ((channels, features), BF16),
        "grad_down_w": ((units, features), BF16),
    }


class Pass:
    def __init__(self, place, buffers, pace):
        self.place, self.buffers, self.pace = place, buffers, pace
        self.tokens, self.features = buffers["zin"].shape
        half = self.tokens // HALVES
        self.halves = [pl.ds(h * half, half) for h in range(HALVES)]
        self.chips = ((0, 0), (1, 0), (0, 1), (1, 1))
        self.phases = 0
        self.items, self.queue, self.flying = [], [], []
        self.saving, self.loading = [], {}

    def enter(self, more, barrier_all):
        place = self.place
        barrier = pltpu.get_barrier_semaphore()
        if barrier_all:
            partners = [device for device, _ in every_other(place)]
            expected = len(partners)
        else:
            x, zh, x_size = place.x, place.zh, lax.axis_size("x")
            partners = [place.beside(axis) for axis in ("core", "yl", "zl")] + more
            partners += [{"x": lax.rem(x + 1, x_size)}, {"x": lax.rem(x + x_size - 1, x_size)}]
            at_turn = jnp.logical_or(jnp.logical_and(x == x_size - 1, zh == 0), jnp.logical_and(x == 0, zh == 1))
            across = {"x": jnp.where(x == 0, x_size - 1, 0), "zh": 1 - zh}

            @pl.when(at_turn)
            def _():
                pl.semaphore_signal(barrier, inc=1, device_id=across, device_id_type=MESH)

            expected = len(partners) + jnp.where(at_turn, 1, 0)
        for partner in partners:
            pl.semaphore_signal(barrier, inc=1, device_id=partner, device_id_type=MESH)
        pl.semaphore_wait(barrier, expected)

    def begin(self, items):
        for item in items:
            item.left = len(item.pairs())
            self.queue += [(item,) + pair for pair in item.pairs()]
            self.items.append(item)

    def launch(self, count):
        for item, launch, land in self.queue[:count]:
            launch()
            self.flying.append((item, land))
        del self.queue[:count]

    def land(self, count):
        for item, land in self.flying[:count]:
            land()
            item.left -= 1
        del self.flying[:count]

    def step(self, point):
        fly, count = self.pace[point]
        while len(self.flying) > fly:
            self.land(1)
        self.launch(count)

    def settle(self, items):
        for item in items:
            while any(queued is item for queued, _, _ in self.queue):
                self.launch(1)
            while item.left:
                self.land(1)
            item.finish()
            self.items.remove(item)

    def load(self, name, source, target):
        if target.shape != source.shape:
            rows = target.shape[0] - source.shape[0]
            target[source.shape[0] :] = jnp.zeros((rows,) + target.shape[1:], BF16)
            target = target.at[: source.shape[0]]
        self.loading[name] = self.place.copy(source, target)
        self.loading[name].start()

    def loaded(self, *names):
        for name in names:
            self.loading.pop(name).wait()

    def save(self, source, target):
        self.saving.append(self.place.copy(source, target))
        self.saving[-1].start()

    def saved(self):
        for copy in self.saving:
            copy.wait()
        self.saving = []

    def pair(self, chip):
        return pl.ds(self.place.rank(*chip, 0) - self.place.core, 2)

    def rows_of(self, values):
        return values.reshape(2 * self.tokens, values.shape[-1])

    def blocks_of(self, values):
        return values.reshape(2, self.tokens, values.shape[-1])

    def all_rows(self, values):
        return values.reshape(8 * self.tokens, values.shape[-1])

    def phase(self, mine, first, second, after, before_first=None, before_second=None, between=None, aside=None):
        place, buffers, halves, chips = self.place, self.buffers, self.halves, self.chips
        rank, sent = place.rank, []
        whole = buffers["whole"].at[self.phases % 2]
        self.phases += 1
        part, sib, yin, yout, zin, zout = (buffers[name] for name in ("part", "sib", "yin", "yout", "zin", "zout"))
        to_sibling, to_y, to_z = (place.beside(axis) for axis in ("core", "yl", "zl"))
        own, beside_z, beside_y, corner = (rank(*chip, 0) for chip in chips)

        def push(src, dst, device):
            sent.append(place.push(src, dst, device, False))
            return sent[-1]

        def sends(src, at, device):
            return [push(mine.at[rows] if src is None else src.at[at, rows], whole.at[at, rows], device) for rows in halves]

        def landed(copies):
            for copy in copies:
                copy.wait_recv()

        from_z, from_y, own_to_core = sends(None, own, to_z), sends(None, own, to_y), sends(None, own, to_sibling)
        from_corner = sends(whole, beside_z, to_y)
        z_to_core, y_to_core, corner_to_core = (sends(whole, at, to_sibling) for at in (beside_z, beside_y, corner))
        own_place = place.copy(mine, whole.at[own])
        own_place.start()
        for h in range(HALVES):
            for copies in (from_z, from_y, own_to_core):
                copies[h].start()
        self.step(0)
        if before_first is not None:
            before_first()
        own_place.wait()
        landed(own_to_core)
        first(whole, chips[0])
        for h in range(HALVES):
            from_z[h].wait_recv()
            from_corner[h].start()
            z_to_core[h].start()
        self.step(1)
        for h in range(HALVES):
            from_y[h].wait_recv()
            y_to_core[h].start()
        landed(z_to_core)
        first(whole, chips[1])
        self.step(2)
        landed(y_to_core)
        first(whole, chips[2])
        self.step(3)
        for h in range(HALVES):
            from_corner[h].wait_recv()
            corner_to_core[h].start()
        landed(corner_to_core)
        first(whole, chips[3])
        self.step(4)
        if between is not None:
            between(whole)
        if before_second is not None:
            before_second()

        order = (chips[3], chips[2], chips[1], chips[0])
        sib_copies = [push(part.at[i, 1 - place.core], sib.at[i], to_sibling) for i in range(4)]
        y_copies = [[push(yout.at[i, rows], yin.at[i, rows], to_y) for rows in halves] for i in range(2)]
        z_copies = [push(zout.at[rows], zin.at[rows], to_z) for rows in halves]

        def multiply(i):
            def columns(j):
                part[i, :, :, tile(j)] = self.blocks_of(second(order[i], j).astype(BF16))

            loop(self.features // TILE, columns)
            sib_copies[i].start()

        def chip_sum(i, rows):
            return part[i, place.core, rows].astype(F32) + sib[i, rows].astype(F32)

        def to_y_side(i):
            sib_copies[i].wait_recv()
            for h, rows in enumerate(halves):
                yout[i, rows] = chip_sum(i, rows).astype(BF16)
                y_copies[i][h].start()

        multiply(0)
        multiply(1)
        to_y_side(0)
        self.step(5)
        multiply(2)
        to_y_side(1)
        multiply(3)
        self.step(6)
        sib_copies[2].wait_recv()
        for h, rows in enumerate(halves):
            y_copies[0][h].wait_recv()
            zout[rows] = (chip_sum(2, rows) + yin[0, rows].astype(F32)).astype(BF16)
            z_copies[h].start()
        self.step(7)
        if aside is not None:
            aside(whole)
        self.step(8)
        sib_copies[3].wait_recv()
        for copy in sent:
            copy.wait_send()
        for h, rows in enumerate(halves):
            y_copies[1][h].wait_recv()
            z_copies[h].wait_recv()
            if h == HALVES - 1:
                self.step(9)
            after(h, rows, chip_sum(3, rows) + yin[1, rows].astype(F32) + zin[rows].astype(F32))
        self.step(10)


def c_columns(joint, b, lane):
    if lane == 0:
        return joint[b, :, LANES : 2 * LANES]
    return swap_half(joint[b, :, 3 * LANES : 4 * LANES])


def both_lanes():
    return [(lane, slice(lane, lane + LANES)) for lane in (0, LANES)]


def forward_kernel(plan, *refs):
    refs = list(refs)
    layers, moving, buffer_names = plan["layers"], plan["moving"], plan["buffers"]

    def take(count):
        taken = refs[:count]
        del refs[:count]
        return taken

    (stream_in,) = take(1)
    if moving:
        small, in_proj, gate_in, up_in, out_in, down_in = take(6)
    else:
        gains, taps_ref, keep = take(3)
        weights = [dict(zip(WEIGHTS, take(4))) for _ in range(layers)]
    stream_out, middles, sources = take(1)[0], take(layers), take(layers - 1)
    saves = [dict(zip(SAVED, take(len(SAVED)))) for _ in range(layers)]
    if moving:
        weights = [dict(zip(WEIGHTS, take(4))) for _ in range(layers)]
        gains, taps_ref, keep = take(3)
    buffers = dict(zip(buffer_names, take(len(buffer_names))))
    if moving:
        (spread,) = take(1)
        shards, mine = ([dict(zip(WEIGHTS[::2], take(2))) for _ in range(layers)] for _ in range(2))
        rounds = [dict(zip(WEIGHTS[1::2], take(2))) for _ in range(layers)]
    place = Place(*take(3))
    run = Pass(place, buffers, FORWARD_PACE)
    tokens, features = run.tokens, run.features
    rows_of, blocks_of, pair = run.rows_of, run.blocks_of, run.pair
    joint, carried, mixed, gated = (buffers[name] for name in ("joint", "carried", "mixed", "gated"))
    gate_up, hidden = buffers["gate_up"], buffers["hidden"]
    in_w, out_w, both_w, down_w = (buffers["vmem_" + name] for name in WEIGHTS)
    main = gate_up.shape[2] // (2 * LANES) * LANES
    next_ref = buffers["next"]

    coming, scattered = {}, {}

    def moves(layer, names):
        for name in names:
            own = mine[layer][name] if name in mine[layer] else rounds[layer][name]
            coming[layer, name] = Gather(place, own, weights[layer][name])
            if name in mine[layer]:
                coming[layer, name].ready = functools.partial(landed, layer, name)
            run.begin([coming[layer, name]])

    def cut(layer, name):
        if name == "in_w":
            width = in_proj.shape[2] // 3
            groups = [in_proj.at[layer, :, i * width : (i + 1) * width] for i in range(3)]
        else:
            groups = [gate_in.at[layer], up_in.at[layer]]
        shards_from(groups, shards[layer][name])

    def scatter(layer, name):
        source = shards[layer][name]
        here = mine[layer][name].at[place.yl * 2 + place.core, place.zl]
        copies = [place.push(source.at[place.rank(*flips)], here, place.member(flips)) for flips in FLIPS]
        copies.append(place.copy(source.at[place.rank(0, 0, 0)], here))
        for copy in copies:
            copy.start()
        scattered[layer, name] = copies

    def landed(layer, name):
        copies = scattered.pop((layer, name))
        for copy in copies[:-1]:
            copy.wait_recv()
        copies[-1].wait()

    def parameters():
        owned = features // 32
        for layer in range(layers):
            for i in range(2):
                row = 5 * layer + i
                gains[2 * layer + i] = jnp.concatenate([spread[o, row : row + 1, :owned] for o in range(32)], axis=1)
            rows = pl.ds(5 * layer + 2, 3)
            parts = [
                spread[((place.yl * 2 + place.core) * 2 + zh) * 4 + place.zl * 2 + x, rows, :owned]
                for zh, x in itertools.product(range(2), repeat=2)
            ]
            taps_ref[layer] = jnp.zeros(taps_ref.shape[1:], F32)
            taps_ref[layer, :3, : 4 * owned] = jnp.concatenate(parts, axis=1)
        count = lax.broadcasted_iota(jnp.int32, (tokens, 1), 0)
        for block in range(8):
            zl, others = block // 4, block % 4
            places = (((place.zh * 2 + zl) * 2 + place.x) * tokens + count).astype(F32)
            starts = [spread[others * 8, 15:16, n : n + 1] for n in range(plan["documents"])]

            def segment(where):
                return sum(jnp.where(start <= where, 1.0, 0.0) for start in starts)

            own = segment(places)
            keep[0, block] = jnp.where(segment(places - 1.0) == own, 1.0, 0.0)
            keep[1, block] = jnp.where(segment(places - 2.0) == own, 1.0, 0.0)

    def load(layer, names):
        for name in names:
            if (layer, name) in coming:
                run.settle([coming.pop((layer, name))])
            source, target = weights[layer][name], buffers["vmem_" + name]
            if len(source.shape) == 2:
                run.load(name, source, target)
                continue
            copies = []
            rows = source.shape[-2]
            lead = source.shape[:-2]
            for n, index in enumerate(itertools.product(*(range(size) for size in lead))):
                copies.append(place.copy(source.at[index], target.at[pl.ds(n * rows, rows)]))
                copies[-1].start()
            filled = rows * len(copies)
            if filled < target.shape[0]:
                target[filled:] = jnp.zeros((target.shape[0] - filled, target.shape[1]), BF16)
            run.loading[name] = Several(copies)

    def rounded(values, gain):
        return (values * rms_scale(values) * gain).astype(BF16)

    def conv(layer, stream):
        def before_first():
            load(layer, ("in_w",))
            run.loaded("in_w")

        def first(whole, chip):
            at = pair(chip)

            def columns(j):
                joint[at, :, tile(j)] = blocks_of(dot(rows_of(whole[at]), in_w[:, tile(j)]))

            loop(2, columns)
            joint[at, :, 2 * TILE :] = blocks_of(dot(rows_of(whole[at]), in_w[:, 2 * TILE :]))
            here = pl.ds(HALO, tokens)
            carried[at, here, :LANES] = joint[at, :, :LANES] * joint[at, :, 2 * LANES : 3 * LANES]
            carried[at, here, LANES:] = joint[at, :, 3 * LANES : 4 * LANES] * joint[at, :, 4 * LANES :]

        def between(whole):
            halo = Halo(place, carried, pl.ds(tokens, HALO), buffers["tails"].at[layer], True)
            halo.start()
            run.saved()
            run.save(joint, saves[layer]["joint"])
            run.save(whole, saves[layer]["conv_whole"])
            halo.wait_recv()
            carried[:, :HALO] = buffers["tails"][layer]

            def block(b):
                keep_one, keep_two = keep[0, b], keep[1, b]
                for lane, lanes in both_lanes():
                    result = (
                        taps_ref[layer, 0:1, lanes] * carried[b, HALO - 2 : HALO - 2 + tokens, lanes] * keep_two
                        + taps_ref[layer, 1:2, lanes] * carried[b, HALO - 1 : HALO - 1 + tokens, lanes] * keep_one
                        + taps_ref[layer, 2:3, lanes] * carried[b, HALO : HALO + tokens, lanes]
                    )
                    mixed[b, :, lanes] = result
                    gated[b, :, lanes] = (c_columns(joint, b, lane) * result).astype(BF16)

            loop(8, block)
            halo.wait_send()
            for name in ("carried", "mixed", "gated"):
                run.save(buffers[name], saves[layer][name])

        def second(chip, j):
            return dot(rows_of(gated[pair(chip)]), out_w[:, tile(j)])

        def after(h, rows, total):
            middle = stream[rows] + total
            middles[layer][rows] = middle
            next_ref[rows] = rounded(middle, gains[2 * layer + 1])

        def before_second():
            load(layer, ("out_w",))
            if moving and layer + 1 < layers:
                scatter(layer + 1, "in_w")
            run.loaded("out_w")

        run.phase(next_ref, first, second, after, before_first, before_second, between)

    def ffn(layer):
        def before_first():
            load(layer, ("both_w",))
            run.loaded("both_w")

        def first(whole, chip):
            at = pair(chip)

            def columns(j):
                ups = pl.ds(pl.multiple_of(main + j * TILE, TILE), TILE)
                gate = dot(rows_of(whole[at]), both_w[:, tile(j)])
                up = dot(rows_of(whole[at]), both_w[:, ups])
                gate_up[at, :, tile(j)] = blocks_of(gate)
                gate_up[at, :, ups] = blocks_of(up)
                hidden[at, :, tile(j)] = blocks_of((gate * jax.nn.sigmoid(gate) * up).astype(BF16))

            loop(main // TILE, columns)
            both = dot(rows_of(whole[at]), both_w[:, 2 * main :])
            gate_up[at, :, 2 * main :] = blocks_of(both)
            lane = lax.broadcasted_iota(jnp.int32, both.shape, 1)
            tail = jnp.where(lane < LANES // 2, both * jax.nn.sigmoid(both) * swap_half(both), 0.0)
            hidden[at, :, main:] = blocks_of(tail.astype(BF16))

        def between(whole):
            run.saved()
            run.save(whole, saves[layer]["ffn_whole"])
            run.save(gate_up, saves[layer]["gate_up"])
            run.save(hidden, saves[layer]["hidden"])

        def second(chip, j):
            return dot(rows_of(hidden[pair(chip)]), down_w[:, tile(j)])

        def after(h, rows, total):
            result = middles[layer][rows] + total
            if layer + 1 < layers:
                sources[layer][rows] = result
                next_ref[rows] = rounded(result, gains[2 * layer + 2])
            else:
                stream_out[rows] = result

        def before_second():
            load(layer, ("down_w",))
            if moving and layer + 1 < layers:
                scatter(layer + 1, "both_w")
            run.loaded("down_w")

        run.phase(next_ref, first, second, after, before_first, before_second, between)

    if moving:
        cut(0, "in_w")
        rounds[0]["out_w"][...] = out_in[0].astype(BF16)
        run.enter([], True)
        kept = place.copy(small, spread.at[place.owner()])
        kept.start()
        spreads = [place.push(small, spread.at[place.owner()], device) for device, _ in every_other(place)]
        scatter(0, "in_w")
        for copy in spreads:
            copy.start()
        moves(0, ("out_w", "in_w", "both_w", "down_w"))
        run.launch(1)
        cut(0, "both_w")
        run.launch(8)
        rounds[0]["down_w"][...] = down_in[0].astype(BF16)
        for layer in range(1, layers):
            cut(layer, "in_w")
            cut(layer, "both_w")
            rounds[layer]["out_w"][...] = out_in[layer].astype(BF16)
            rounds[layer]["down_w"][...] = down_in[layer].astype(BF16)
            moves(layer, WEIGHTS)
        kept.wait()
        for copy in spreads:
            copy.wait_recv()
        scatter(0, "both_w")
        parameters()
        next_ref[...] = rounded(stream_in[...], gains[0])
    else:
        next_ref[...] = rounded(stream_in[...], gains[0])
        run.enter([], False)
    for layer in range(layers):
        conv(layer, sources[layer - 1] if layer else stream_in)
        ffn(layer)
    run.saved()
    for copy in place.sent:
        copy.wait_send()


class Several:
    def __init__(self, copies):
        self.copies = copies

    def wait(self):
        for copy in self.copies:
            copy.wait()


def whole_shape(mine):
    return (4, 2, 2, 2) + mine[2:] if len(mine) == 4 else (2, 2) + mine


def forward(stream, given, tall, moving, documents=0):
    tokens, features = stream.shape
    if moving:
        layers, owned = given[1].shape[:2]
        wide = (-(-3 * tall[0] // LANES) * LANES, 2 * tall[1])
    else:
        layers = given[1].shape[0]
        wide = (given[3].shape[1], given[5].shape[1])
    forms = forms_of(tokens, features, wide, tall, layers)
    inside = pl.BlockSpec(memory_space=pltpu.VMEM)
    anywhere = pl.BlockSpec(memory_space=pl.ANY)
    outs = [(forms["stream"], inside)] * (1 + layers + layers - 1)
    outs += [(forms[name], anywhere) for _ in range(layers) for name in SAVED]
    buffers = {name: forms[name] for name in ("joint", "carried", "mixed", "gated", "gate_up", "hidden", "next", "tails")}
    buffers |= {name: forms[name] for name in ("whole", "part", "sib", "yin", "yout", "zin", "zout")}
    buffers |= {"vmem_in_w": forms["in_w"], "vmem_both_w": forms["both_w"]}
    buffers |= {"vmem_out_w": ((forms["gated"][0][2], features), BF16), "vmem_down_w": forms["tall_w"]}
    scratch = [pltpu.VMEM(*form) for form in buffers.values()]
    if moving:
        columns = [(4, 2, owned, width) for width in wide]
        rows = [(owned, features), (tall[1] // 4, features)]
        wholes = [whole_shape(shape) for pair in zip(columns, rows) for shape in pair]
        outs += [((shape, BF16), anywhere) for _ in range(layers) for shape in wholes]
        outs += [(((2 * layers, 1, features), F32), inside), (((layers, HALO, forms["mixed"][0][2]), F32), inside)]
        outs.append((((2, 8, tokens, 1), F32), inside))
        scratch.append(pltpu.VMEM((32,) + given[0].shape, F32))
        scratch += [pltpu.VMEM((8, owned, width), BF16) for _ in range(layers) for width in wide]
        scratch += [pltpu.VMEM(shape, BF16) for _ in range(layers) for shape in columns]
        scratch += [pltpu.VMEM(shape, BF16) for _ in range(layers) for shape in rows]
    plan = {"layers": layers, "moving": moving, "buffers": tuple(buffers), "documents": documents}
    results = pl.pallas_call(
        functools.partial(forward_kernel, plan),
        out_shape=[jax.ShapeDtypeStruct(*form) for form, _ in outs],
        in_specs=[inside] * 7 if moving else [inside] * 4 + [anywhere] * (len(given) - 3),
        out_specs=[spec for _, spec in outs],
        scratch_shapes=scratch + [pltpu.SemaphoreType.DMA((SEMAPHORES,))] * 3,
        compiler_params=pltpu.CompilerParams(
            collective_id=COLLECTIVE_ID["forward"], has_side_effects=True, vmem_limit_bytes=62 << 20
        ),
        name="forward",
    )(stream, *given)
    stream_out, results = results[0], results[1:]
    middles, results = results[:layers], results[layers:]
    sources, results = results[: layers - 1], results[layers - 1 :]
    count = layers * len(SAVED)
    saved, results = results[:count], results[count:]
    if not moving:
        return stream_out, middles, sources, saved, given[3:], given[:3]
    return stream_out, middles, sources, saved, results[:-3], results[-3:]


def backward_kernel(plan, *refs):
    refs = list(refs)
    layers, moving, buffer_names = plan["layers"], plan["moving"], plan["buffers"]

    def take(count):
        taken = refs[:count]
        del refs[:count]
        return taken

    grad_out, gains, taps_ref, keep = take(4)
    middles, sources = take(layers), take(layers)
    weights = [dict(zip(WEIGHTS, take(4))) for _ in range(layers)]
    saves = [dict(zip(SAVED, take(len(SAVED)))) for _ in range(layers)]
    (grad_in,) = take(1)
    if moving:
        small_sum, grad_in_w, grad_out_w, gate_out, up_out, down_out = take(6)
    else:
        gain_out, taps_out = take(2)
        raw = [take(4) for _ in range(layers)]
    buffers = dict(zip(buffer_names, take(len(buffer_names))))
    if moving:
        landing = {name: take(5 if name in ("in_w", "both_w") else 4) for name in WEIGHTS}
        staging, slabs, slabs_in = take(2), *take(2)
        free = dict(zip(("both", "down", "conv"), take(3)))
    place = Place(*take(3))
    run = Pass(place, buffers, BACKWARD_PACE)
    tokens, features = run.tokens, run.features
    rows_of, blocks_of, all_rows, pair = run.rows_of, run.blocks_of, run.all_rows, run.pair
    wide = {"in_w": plan["wide"][0], "both_w": plan["wide"][1]}
    joint, gate_up = buffers["gate_up"].at[:, :, : wide["in_w"]], buffers["gate_up"]
    grad_joint, grad_gate_up = buffers["grad_rows"].at[:, :, : wide["in_w"]], buffers["grad_rows"]
    in_w, both_w = buffers["wide_w"].at[:, : wide["in_w"]], buffers["wide_w"]
    channels, units = buffers["mixed"].shape[2], buffers["hidden"].shape[2]
    out_w, down_w = buffers["tall_w"].at[:channels], buffers["tall_w"]
    gated, hidden = buffers["hidden"].at[:, :, :channels], buffers["hidden"]
    carried, mixed, edges, grad_gated = (buffers[name] for name in ("carried", "mixed", "edges", "grad_gated"))
    kept_whole, next_ref, grad_ref, held = (buffers[name] for name in ("conv_whole", "next", "stream", "held"))
    gain_grads, tap_grads = buffers["gain_grads"], buffers["tap_grads"]
    main = gate_up.shape[2] // (2 * LANES) * LANES

    def load_rows(name, source, target):
        if len(source.shape) == 2:
            run.load(name, source, target)
            return
        rows, lead = source.shape[-2], source.shape[:-2]
        copies = []
        for n, index in enumerate(itertools.product(*(range(size) for size in lead))):
            copies.append(place.copy(source.at[index], target.at[pl.ds(n * rows, rows)]))
            copies[-1].start()
        filled = rows * len(copies)
        if filled < target.shape[0]:
            target[filled:] = jnp.zeros((target.shape[0] - filled, target.shape[1]), BF16)
        run.loading[name] = Several(copies)

    def deliver_columns(outs, layer, views):
        def deliver(landed):
            run.saved()
            shards_to(landed, views)
            for source, out in outs:
                run.save(source, out.at[layer])

        return deliver

    def deliver_rows(out, layer):
        def deliver(final):
            run.save(final, out.at[layer])

        return deliver

    reduced = {"both": 0, "down": 0, "conv": 0}
    under_way = {"both": [], "down": [], "conv": []}

    def reduce(layer, kind, names):
        if not moving:
            for name in names:
                source = buffers["grad_" + name]
                target = raw[layer][WEIGHTS.index(name)]
                run.save(source.at[: target.shape[0]] if source.shape != target.shape else source, target)
            return
        if reduced[kind]:
            pl.semaphore_wait(free[kind], 9)
        reduced[kind] += 1
        run.saved()
        items = []
        for name in names:
            if name == "in_w":
                width = features
                views = [staging[0].at[:, i * width : (i + 1) * width] for i in range(3)]
                deliver = deliver_columns([(staging[0], grad_in_w)], layer, views)
            elif name == "both_w":
                deliver = deliver_columns([(staging[0], gate_out), (staging[1], up_out)], layer, list(staging))
            else:
                deliver = deliver_rows(grad_out_w if name == "out_w" else down_out, layer)
            total = buffers["grad_" + name]
            if name in ("out_w", "down_w"):
                total = total.at[: 4 * landing[name][3].shape[0]]
            items.append(Reduce(place, total, landing[name], deliver))
            items[-1].start()
        run.begin(items)
        under_way[kind] = items

    def settle(kind):
        items, under_way[kind] = under_way[kind], []
        run.settle(items)
        if items and reduced[kind] < layers:
            for device in [place.member(flips) for flips in FLIPS] + [place.beside("zh"), place.beside("x")]:
                pl.semaphore_signal(free[kind], inc=1, device_id=device, device_id_type=MESH)

    def step_back(h, rows, total, stream, gain, row):
        scale = rms_scale(stream)
        gain_grad = jnp.sum(total * stream * scale, axis=0, keepdims=True)
        gain_grads[row : row + 1] = gain_grad if h == 0 else gain_grads[row : row + 1] + gain_grad
        scaled = total * gain
        grad = (
            grad_ref[rows]
            + scale * scaled
            - stream * (scale * scale * scale) * jnp.mean(scaled * stream, axis=-1, keepdims=True)
        )
        grad_ref[rows] = grad
        next_ref[rows] = grad.astype(BF16)
        return grad

    def ffn_back(layer):
        def before_first():
            load_rows("down_w", weights[layer]["down_w"], down_w)
            run.load("gate_up", saves[layer]["gate_up"], gate_up)
            load_rows("both_w", weights[layer]["both_w"], both_w)
            run.load("hidden", saves[layer]["hidden"], hidden)
            run.load("whole", saves[layer]["ffn_whole"], kept_whole)
            run.load("held", middles[layer], held)
            run.loaded("down_w", "gate_up")

        def grads(grad_hidden, gate, up):
            sigmoid = jax.nn.sigmoid(gate)
            return grad_hidden * up * sigmoid * (1.0 + gate * (1.0 - sigmoid)), grad_hidden * gate * sigmoid

        def first(whole, chip):
            at = pair(chip)

            def columns(j):
                ups = pl.ds(pl.multiple_of(main + j * TILE, TILE), TILE)
                grad_hidden = dot_cols(rows_of(whole[at]), down_w[tile(j), :])
                gate, up = (rows_of(gate_up[at, :, lanes]) for lanes in (tile(j), ups))
                grad_gate, grad_up = grads(grad_hidden, gate, up)
                grad_gate_up[at, :, tile(j)] = blocks_of(grad_gate.astype(BF16))
                grad_gate_up[at, :, ups] = blocks_of(grad_up.astype(BF16))

            loop(main // TILE, columns)
            grad_hidden = dot_cols(rows_of(whole[at]), down_w[main:, :])
            both = rows_of(gate_up[at, :, 2 * main :])
            grad_gate, grad_up = grads(grad_hidden, both, swap_half(both))
            grad_gate_up[at, :, 2 * main :] = blocks_of((grad_gate + swap_half(grad_up)).astype(BF16))

        def second(chip, j):
            return dot_cols(rows_of(grad_gate_up[pair(chip)]), both_w[tile(j), :])

        def aside(whole):
            run.loaded("whole", "hidden")
            settle("both")
            settle("down")
            grad_both, grad_down = buffers["grad_both_w"], buffers["grad_down_w"]
            width = features // 4

            def both_rows(c):
                left = all_rows(kept_whole[:, :, tile(c, width)])
                result = dot_rows(left, all_rows(grad_gate_up[...])).astype(BF16)
                grad_both[c] = result.reshape(grad_both.shape[1:])

            def down_rows(j):
                left = all_rows(hidden[:, :, tile(j, LANES)])
                grad_down[tile(j, LANES), :] = dot_rows(left, all_rows(whole[...])).astype(BF16)

            loop(4, both_rows)
            reduce(layer, "both", ("both_w",))
            loop(units // LANES, down_rows)
            reduce(layer, "down", ("down_w",))

        def after(h, rows, total):
            step_back(h, rows, total, held[rows], gains[2 * layer + 1], 2 * layer + 1)

        run.phase(next_ref, first, second, after, before_first, lambda: run.loaded("both_w", "held"), None, aside)

    def conv_back(layer):
        taps = taps_ref.at[layer]

        def before_first():
            load_rows("out_w", weights[layer]["out_w"], out_w)
            for name, target in (("joint", joint), ("carried", carried), ("mixed", mixed)):
                run.load(name, saves[layer][name], target)
            load_rows("in_w", weights[layer]["in_w"], in_w)
            run.load("gated", saves[layer]["gated"], gated)
            run.load("whole", saves[layer]["conv_whole"], kept_whole)
            run.load("held", sources[layer], held)
            run.loaded("out_w")

        def first(whole, chip):
            at = pair(chip)
            grad_gated[at] = blocks_of(dot_cols(rows_of(whole[at]), out_w[...]))

        def between(whole):
            run.loaded("joint", "carried", "mixed")
            tap_grads[layer] = jnp.zeros(tap_grads.shape[1:], F32)

            def block(b):
                keep_one, keep_two = keep[0, b], keep[1, b]
                for lane, lanes in both_lanes():
                    grad_value = grad_gated[b, :, lanes]
                    grad_mixed = grad_value * c_columns(joint, b, lane)
                    first_tap, second_tap = grad_mixed * keep_two, grad_mixed * keep_one
                    edges[0, b, :tokens, lanes] = second_tap * taps[1:2, lanes]
                    edges[1, b, :tokens, lanes] = first_tap * taps[0:1, lanes]
                    mixed[b, :, lanes] = grad_value * mixed[b, :, lanes]
                    grad_gated[b, :, lanes] = grad_mixed * taps[2:3, lanes]
                    for row, grad, back_by in ((0, first_tap, 2), (1, second_tap, 1), (2, grad_mixed, 0)):
                        tap_in = carried[b, HALO - back_by : HALO - back_by + tokens, lanes]
                        tap_grads[layer, row : row + 1, lanes] += jnp.sum(grad * tap_in, axis=0, keepdims=True)

            loop(8, block)
            halo = Halo(place, edges, pl.ds(0, HALO), buffers["heads"].at[layer], False)
            halo.start()
            halo.wait_recv()
            edges[:, :, tokens:] = buffers["heads"][layer]

            def block_after(b):
                for lane, lanes in both_lanes():
                    grad_carried = (
                        grad_gated[b, :, lanes] + edges[0, b, 1 : 1 + tokens, lanes] + edges[1, b, 2 : 2 + tokens, lanes]
                    )
                    grad_c = mixed[b, :, lanes]
                    if lane == 0:
                        grad_joint[b, :, :LANES] = (grad_carried * joint[b, :, 2 * LANES : 3 * LANES]).astype(BF16)
                        grad_joint[b, :, LANES : 2 * LANES] = grad_c.astype(BF16)
                        grad_joint[b, :, 2 * LANES : 3 * LANES] = (grad_carried * joint[b, :, :LANES]).astype(BF16)
                    else:
                        grad_b = grad_carried * joint[b, :, 4 * LANES :]
                        grad_joint[b, :, 3 * LANES : 4 * LANES] = (grad_b + swap_half(grad_c)).astype(BF16)
                        grad_joint[b, :, 4 * LANES :] = (grad_carried * joint[b, :, 3 * LANES : 4 * LANES]).astype(BF16)

            loop(8, block_after)
            halo.wait_send()
            if layer == 0:
                gradients(whole)

        def second(chip, j):
            return dot_cols(rows_of(grad_joint[pair(chip)]), in_w[tile(j), :])

        def gradients(whole):
            run.loaded("whole", "gated")
            settle("conv")
            grad_in_rows, grad_out_rows = buffers["grad_in_w"], buffers["grad_out_w"]
            width = features // 4

            def in_rows(c):
                left = all_rows(kept_whole[:, :, tile(c, width)])
                result = dot_rows(left, all_rows(grad_joint[...])).astype(BF16)
                grad_in_rows[c] = result.reshape(grad_in_rows.shape[1:])

            def out_rows(j):
                left = all_rows(gated[:, :, tile(j, LANES)])
                grad_out_rows[tile(j, LANES), :] = dot_rows(left, all_rows(whole[...])).astype(BF16)

            loop(4, in_rows)
            loop(channels // LANES, out_rows)
            reduce(layer, "conv", ("in_w", "out_w"))

        def after(h, rows, total):
            grad = step_back(h, rows, total, held[rows], gains[2 * layer], 2 * layer)
            if layer == 0:
                grad_in[rows] = grad

        run.phase(
            next_ref, first, second, after, before_first, lambda: run.loaded("in_w", "held"), between, gradients if layer else None
        )

    grad_ref[...] = grad_out[...]
    next_ref[...] = grad_out[...].astype(BF16)
    run.enter([], moving)
    for layer in reversed(range(layers)):
        ffn_back(layer)
        conv_back(layer)
    if moving:
        owned = features // 32
        slabs[...] = jnp.zeros(slabs.shape, F32)
        for owner in range(32):
            slabs[owner, : 2 * layers, :owned] = gain_grads[:, owner * owned : (owner + 1) * owned]
        for layer in range(layers):
            row = 2 * layers + 3 * layer
            for zh, x in itertools.product(range(2), repeat=2):
                owner = ((place.yl * 2 + place.core) * 2 + zh) * 4 + place.zl * 2 + x
                low = (zh * 2 + x) * owned
                slabs[owner, row : row + 3, :owned] = tap_grads[layer, :3, low : low + owned]
        copies = []
        for i, (device, flips) in enumerate(every_other(place)):
            copies.append(place.push(slabs.at[place.owner(flips)], slabs_in.at[i], device))
            copies[-1].start()
        run.launch(len(run.queue))
        for kind in ("both", "down", "conv"):
            settle(kind)
        for copy in copies:
            copy.wait_recv()
        small_sum[...] = slabs[place.owner()] + jnp.sum(slabs_in[...], axis=0)
    else:
        gain_out[...] = gain_grads[...]
        taps_out[...] = tap_grads[...]
    run.saved()
    for copy in place.sent:
        copy.wait_send()


def backward(grad_out, gains, taps, keep, middles, sources, weights, saved, tall, moving):
    tokens, features = grad_out.shape
    layers = taps.shape[0]
    wide = (weights[0][0].shape[-1], weights[0][2].shape[-1])
    forms = forms_of(tokens, features, wide, tall, layers)
    inside = pl.BlockSpec(memory_space=pltpu.VMEM)
    anywhere = pl.BlockSpec(memory_space=pl.ANY)
    owned = features // 32
    outs = [(forms["stream"], inside)]
    if moving:
        outs.append((((16, LANES), F32), inside))
        shapes = ((owned, 3 * features), (owned, features), (owned, 4 * tall[1] * 2), (owned, 4 * tall[1] * 2), (tall[1] // 4, features))
        outs += [(((layers,) + shape, F32), anywhere) for shape in shapes]
    else:
        outs.append((((2 * layers, features), F32), inside))
        outs.append((((layers, HALO, forms["mixed"][0][2]), F32), inside))
        for _ in range(layers):
            for name in WEIGHTS:
                shape = forms["grad_" + name][0]
                outs.append((((tall[0] if name == "out_w" else tall[1], features) if len(shape) == 2 else shape, BF16), anywhere))
    names = ("conv_whole", "gate_up", "carried", "mixed", "hidden", "grad_rows", "grad_gated", "edges", "heads", "tall_w")
    names += ("next", "stream", "whole", "part", "sib", "yin", "yout", "zin", "zout")
    names += ("grad_in_w", "grad_both_w", "grad_out_w", "grad_down_w")
    buffers = {name: forms[name] for name in names}
    buffers["wide_w"], buffers["held"] = forms["both_w"], forms["stream"]
    buffers["gain_grads"] = ((2 * layers, features), F32)
    buffers["tap_grads"] = ((layers, HALO, forms["mixed"][0][2]), F32)
    scratch = [pltpu.VMEM(*form) for form in buffers.values()]
    if moving:
        for name in WEIGHTS:
            shape = forms["grad_" + name][0]
            if len(shape) == 2:
                shape = (tall[0] if name == "out_w" else tall[1], features)
            scratch += [pltpu.VMEM(*form) for form in landing_shapes(shape)]
        scratch += [pltpu.VMEM((owned, 3 * features), F32)] * 2
        scratch += [pltpu.VMEM((32, 16, LANES), F32), pltpu.VMEM((31, 16, LANES), F32)]
        scratch += [pltpu.SemaphoreType.REGULAR] * 3
    operands = list(middles) + list(sources) + [array for group in weights for array in group] + list(saved)
    plan = {"layers": layers, "moving": moving, "buffers": tuple(buffers), "wide": wide}
    return pl.pallas_call(
        functools.partial(backward_kernel, plan),
        out_shape=[jax.ShapeDtypeStruct(*form) for form, _ in outs],
        in_specs=[inside] * 4 + [anywhere] * len(operands),
        out_specs=[spec for _, spec in outs],
        scratch_shapes=scratch + [pltpu.SemaphoreType.DMA((SEMAPHORES,))] * 3,
        compiler_params=pltpu.CompilerParams(
            collective_id=COLLECTIVE_ID["backward"], has_side_effects=True, vmem_limit_bytes=63 << 20
        ),
        name="backward",
    )(grad_out, gains, taps, keep, *operands)


def sizes_of(axes):
    return tuple(lax.axis_size(axis) for axis in axes)


def split_owners(array, dim):
    owners = sizes_of(OWNERS)
    count = 1
    for size in owners:
        count *= size
    shape = array.shape
    return array.reshape(shape[:dim] + owners + (shape[dim] // count,) + shape[dim + 1 :])


def column_shards(weights):
    rows = weights[0].shape[0]
    mains, rests = [], []
    for weight in weights:
        parts = split_owners(weight, 1).transpose(5, 2, 3, 0, 1, 4, 6, 7).reshape(8, rows, -1)
        main = parts.shape[2] // LANES * LANES
        mains.append(parts[:, :, :main])
        rests.append(parts[:, :, main:])
    shards = jnp.concatenate(mains + rests, axis=2)
    return jnp.pad(shards, ((0, 0), (0, 0), (0, -shards.shape[2] % LANES)))


def column_whole(shards, groups, width):
    rows = shards.shape[1]
    yh, yl, core, zh, zl, x = sizes_of(OWNERS)
    wholes = []
    for group in range(groups):
        part = jnp.concatenate(
            [shards[..., a:b] for a, b in pieces_of(groups, width, group, 0, width)], axis=-1
        ).reshape(zl, yl, core, rows, yh, zh, x, -1)
        wholes.append(part.transpose(3, 4, 1, 2, 5, 0, 6, 7).reshape(rows, -1))
    return wholes


def gather_columns(shards):
    mine = lax.all_to_all(shards, TP, split_axis=0, concat_axis=0, tiled=True)
    whole = lax.all_gather(mine, DP, axis=0, tiled=False)
    yh, yl, core, zh, zl, x = sizes_of(OWNERS)
    rows, columns = shards.shape[1:]
    whole = whole.reshape(yh, zh, x, zl, yl, core, rows, columns)
    return whole.transpose(0, 4, 5, 1, 3, 2, 6, 7).reshape(-1, columns)


def scatter_columns(total):
    yh, yl, core, zh, zl, x = sizes_of(OWNERS)
    columns = total.shape[1]
    parts = split_owners(total, 0).transpose(0, 3, 5, 4, 1, 2, 6, 7)
    parts = parts.reshape(yh * zh * x, -1, columns)
    mine = lax.psum_scatter(parts, DP, scatter_dimension=0, tiled=False)
    mine = mine.reshape(8, -1, columns)
    return lax.all_to_all(mine, TP, split_axis=0, concat_axis=0, tiled=True)


def tap_masks(starts, token_count):
    zh, x, x_size = lax.axis_index("zh"), lax.axis_index("x"), lax.axis_size("x")
    blocks = (zh * 2 + jnp.arange(2, dtype=jnp.int32)) * x_size + x
    places = blocks[:, None] * token_count + jnp.arange(token_count, dtype=jnp.int32)

    def segment_of(where):
        return jnp.sum((starts[None, :, None, :] <= where[:, None, :, None]).astype(jnp.int32), axis=3)

    own_segment = segment_of(places)
    keep_one = (segment_of(places - 1) == own_segment).astype(F32)
    keep_two = (segment_of(places - 2) == own_segment).astype(F32)
    return keep_one.reshape(8, token_count, 1), keep_two.reshape(8, token_count, 1)


def local(stream_in, doc_starts, norm_mix, in_proj, conv_taps, out_proj, norm_ffn, w_gate, w_up, w_down, grad_out):
    _, token_count, features = stream_in.shape
    layers = norm_mix.shape[0]
    own_kernels = sizes_of(DP) == (1, 2, 2)
    stream = stream_in.reshape(-1, features)
    grad_stream = grad_out.reshape(-1, features)
    small = jnp.concatenate([norm_mix[:, None], norm_ffn[:, None], conv_taps.transpose(0, 2, 1)], axis=1)
    small = small.astype(BF16).astype(F32)
    owned = small.shape[2]
    tall = (features // 8, w_gate.shape[2] // 8)
    if own_kernels:
        packed = jnp.zeros((16, LANES), F32).at[: 5 * layers, :owned].set(small.reshape(-1, owned))
        packed = packed.at[15, : doc_starts.shape[1]].set(doc_starts[0].astype(F32))
        given = (packed, in_proj, w_gate, w_up, out_proj, w_down)
    else:
        starts = lax.all_gather(doc_starts, ("yl", "core"), axis=0, tiled=True)
        small = small.astype(BF16)
        gains = lax.all_gather(small[:, :2], OWNERS, axis=2, tiled=True).astype(F32).reshape(2 * layers, 1, features)
        taps = lax.all_gather(small[:, 2:], DP, axis=2, tiled=True).astype(F32)
        taps = jnp.pad(taps, ((0, 0), (0, HALO - 3), (0, -taps.shape[2] % LANES)))
        given = (gains, taps, jnp.stack(tap_masks(starts, token_count)))
        for layer in range(layers):
            in_w = gather_columns(column_shards(jnp.split(in_proj[layer].astype(BF16), 3, axis=1)))
            both_w = gather_columns(column_shards([w_gate[layer].astype(BF16), w_up[layer].astype(BF16)]))
            out_w = lax.all_gather(out_proj[layer].astype(BF16), DP, axis=0, tiled=True)
            down_w = lax.all_gather(w_down[layer].astype(BF16), DP, axis=0, tiled=True)
            given += (in_w, out_w, both_w, down_w)

    stream_out, middles, sources, saved, weights, params = forward(stream, given, tall, own_kernels, doc_starts.shape[1])
    weights = [tuple(weights[4 * layer : 4 * layer + 4]) for layer in range(layers)]
    grad_in, *results = backward(
        grad_stream, *params, middles, [stream] + list(sources), weights, saved, tall, own_kernels
    )
    if own_kernels:
        small_sums, grad_in_w, grad_out_w, grad_gate, grad_up, grad_down = results
        small_sums = small_sums[:, :owned]
        gain_grads = small_sums[: 2 * layers].reshape(layers, 2, owned)
        tap_grads = small_sums[2 * layers : 5 * layers].reshape(layers, 3, owned)
    else:
        gain_grads, tap_grads, *raw = results
        gain_grads = lax.psum_scatter(gain_grads, OWNERS, scatter_dimension=1, tiled=True).reshape(layers, 2, -1)
        tap_grads = lax.psum_scatter(tap_grads[:, :3, : tall[0]], DP, scatter_dimension=2, tiled=True)
        sums = []
        for layer in range(layers):
            grad_in_w, grad_out_w, grad_both, grad_down = raw[4 * layer : 4 * layer + 4]
            columns = [
                column_whole(scatter_columns(grad.reshape(features, -1)).astype(F32), groups, width)
                for grad, groups, width in ((grad_in_w, 3, tall[0]), (grad_both, 2, tall[1]))
            ]
            rows = [
                lax.psum_scatter(grad, DP, scatter_dimension=0, tiled=True).astype(F32) for grad in (grad_out_w, grad_down)
            ]
            sums.append((jnp.concatenate(columns[0], axis=1), rows[0], *columns[1], rows[1]))
        grad_in_w, grad_out_w, grad_gate, grad_up, grad_down = (jnp.stack(parts) for parts in zip(*sums))
    return (
        stream_out[None],
        grad_in[None],
        gain_grads[:, 0],
        grad_in_w,
        tap_grads.transpose(0, 2, 1),
        grad_out_w,
        gain_grads[:, 1],
        grad_gate,
        grad_up,
        grad_down,
    )


def solution(mesh):
    dp, seq = mesh.shape["dp"], mesh.shape["seq"]
    side = dp // 2
    split = Mesh(mesh.devices.reshape(side // 2, 2, 2, seq // side // 2, 2, side), OWNERS)
    token = P(ROW_AXES, SEQ_AXES, None)
    vector = P(None, OWNERS)
    matrix = P(None, OWNERS, None)
    return jax.shard_map(
        local,
        mesh=split,
        in_specs=(token, P(ROW_AXES, None), vector, matrix, matrix, matrix, vector, matrix, matrix, matrix, token),
        out_specs=(token, token, vector, matrix, matrix, matrix, vector, matrix, matrix, matrix),
        check_vma=False,
    )
```

```python
import functools
import itertools

import jax
import jax.numpy as jnp
from jax import lax
from jax.experimental import pallas as pl
from jax.experimental.pallas import tpu as pltpu
from jax.sharding import Mesh, PartitionSpec as P

EPSILON = 1e-05
TP = ("zl", "yl", "core")
DP = ("yh", "zh", "x")
ROW_AXES = ("yh", "yl", "core")
SEQ_AXES = ("zh", "zl", "x")
OWNERS = ROW_AXES + SEQ_AXES
BF16 = jnp.bfloat16
F32 = jnp.float32
MESH = pl.DeviceIdType.MESH
HALVES = 2
COLLECTIVE_ID = {"forward": 0, "backward": 1}
FLIPS = ((1, 1, 1), (1, 1, 0), (1, 0, 1), (1, 0, 0), (0, 1, 1), (0, 1, 0), (0, 0, 1))
OTHERS = tuple(itertools.product((0, 1), repeat=5))[1:]
OTHER_AXES = ("yl", "core", "zh", "zl", "x")
SEMAPHORES = 288
FORWARD_PACE = ((1, 1),) * 7 + ((1, 0),) + ((1, 1),) * 3
BACKWARD_PACE = ((1, 1), (1, 2)) + ((2, 1),) * 8 + ((1, 1),)
LANES = 128
TILE = 256
HALO = 8


def rms_scale(values):
    return lax.rsqrt(jnp.mean(values * values, axis=-1, keepdims=True) + EPSILON)


class Place:
    def __init__(self, send, recv, local):
        self.zl, self.yl, self.core = (lax.axis_index(axis) for axis in TP)
        self.zh, self.x = lax.axis_index("zh"), lax.axis_index("x")
        self.send, self.recv, self.local = send, recv, local
        self.remote_count = self.local_count = 0
        self.sent = []

    def rank(self, flip_z, flip_y, flip_core):
        return self.flipped("zl", flip_z) * 4 + self.flipped("yl", flip_y) * 2 + self.flipped("core", flip_core)

    def flipped(self, axis, flip):
        return 1 - getattr(self, axis) if flip else getattr(self, axis)

    def member(self, flips):
        return {axis: 1 - getattr(self, axis) for axis, flip in zip(TP, flips) if flip}

    def beside(self, axis):
        return {axis: 1 - getattr(self, axis)}

    def owner(self, flips=(0,) * 5):
        index = 0
        for axis, flip in zip(OTHER_AXES, flips):
            index = index * 2 + self.flipped(axis, flip)
        return index

    def push(self, src, dst, device, kept=True):
        index = self.remote_count
        self.remote_count += 1
        assert index < SEMAPHORES
        copy = pltpu.make_async_remote_copy(
            src_ref=src, dst_ref=dst, send_sem=self.send.at[index], recv_sem=self.recv.at[index],
            device_id=device, device_id_type=MESH,
        )
        if kept:
            self.sent.append(copy)
        return copy

    def copy(self, src, dst):
        index = self.local_count
        self.local_count += 1
        return pltpu.make_async_copy(src, dst, self.local.at[index])


def pieces_of(groups, width, group, low, high):
    main = width // LANES * LANES
    rest = width - main
    ranges = []
    if low < main:
        ranges.append((group * main + low, group * main + min(high, main)))
    if high > main:
        start = groups * main + group * rest - main
        ranges.append((start + max(low, main), start + high))
    return ranges


def shards_from(weights, out):
    width = weights[0].shape[1] // 8
    block = width // 4
    main = width // LANES * LANES
    rest = width - main
    for group, weight in enumerate(weights):
        for member in range(8):
            zl, others = member // 4, member % 4
            starts = [((others * 2 + zh) * 4 + zl * 2 + x) * block for zh in range(2) for x in range(2)]
            values = jnp.concatenate([weight[:, start : start + block] for start in starts], axis=1).astype(BF16)
            out[member, :, group * main : (group + 1) * main] = values[:, :main]
            if rest:
                low = len(weights) * main + group * rest
                out[member, :, low : low + rest] = values[:, main:]
    pad = out.shape[2] - len(weights) * width
    if pad:
        out[:, :, len(weights) * width :] = jnp.zeros((8, out.shape[1], pad), BF16)


def shards_to(shards, outs):
    groups, width = len(outs), outs[0].shape[1] // 8
    block = width // 4
    for group, out in enumerate(outs):
        for others in range(4):
            for zh in range(2):
                values = []
                for zl in range(2):
                    for x in range(2):
                        low = (zh * 2 + x) * block
                        for start, end in pieces_of(groups, width, group, low, low + block):
                            values.append(shards[zl * 4 + others, :, start:end].astype(F32))
                start = (others * 2 + zh) * 4 * block
                out[:, start : start + 4 * block] = jnp.concatenate(values, axis=1)


def every_other(place):
    return [
        ({axis: place.flipped(axis, 1) for axis, flip in zip(OTHER_AXES, flips) if flip}, flips) for flips in OTHERS
    ]


class Gather:
    def __init__(self, place, mine, whole):
        self.ready = None
        x, own, other = place.x, place.zh, 1 - place.zh
        if len(whole.shape) == 6:
            parts = [
                (mine.at[c, zl], whole.at[c, own, zl, x], whole.at[c, other, zl, x])
                for c in range(4)
                for zl in range(2)
            ]
        else:
            count = whole.shape[2]
            size = 48 if count % 48 == 0 else count
            parts = [
                (mine.at[rows], whole.at[own, x, rows], whole.at[other, x, rows])
                for rows in (pl.ds(low, size) for low in range(0, count, size))
            ]
        self.along_z = [place.push(src, here, place.beside("zh")) for src, here, _ in parts]
        self.along_x = [place.push(src, here, place.beside("x")) for src, here, _ in parts]
        self.onward = [place.push(there, there, place.beside("x")) for _, _, there in parts]
        self.kept = [place.copy(src, here) for src, here, _ in parts]

    def pairs(self):
        def launch(c):
            if c == 0 and self.ready is not None:
                self.ready()
            self.along_z[c].start()
            self.along_x[c].start()
            self.kept[c].start()

        def land(c):
            self.along_z[c].wait_recv()
            self.onward[c].start()

        return [(functools.partial(launch, c), functools.partial(land, c)) for c in range(len(self.kept))]

    def finish(self):
        for c in range(len(self.kept)):
            self.along_x[c].wait_recv()
            self.onward[c].wait_recv()
            self.kept[c].wait()


class Reduce:
    def __init__(self, place, total, landing, deliver):
        self.columns = len(total.shape) == 6
        self.place, self.total, self.deliver = place, total, deliver
        self.xin, self.zout, self.zin, self.final = landing[:4]
        self.landed = landing[4] if self.columns else None
        x, zh, beside = place.x, place.zh, place.beside
        self.flips = FLIPS + ((0, 0, 0),)
        self.chunks = self.zin.shape[0]
        self.along_x = [
            [
                place.push(self.part(j, to_zh, 1 - x), self.xin.at[j, i], beside("x"), False)
                for i, to_zh in enumerate((1 - zh, zh))
            ]
            for j in range(self.chunks)
        ]
        self.along_z = [place.push(self.zout.at[j], self.zin.at[j], beside("zh"), False) for j in range(self.chunks)]
        if self.columns:
            here = self.landed.at[place.rank(0, 0, 0)]
            self.back = [place.push(self.final.at[j], here, place.member(flips), False) for j, flips in enumerate(FLIPS)]
            self.back.append(place.copy(self.final.at[7], here))

    def part(self, j, zh, x):
        if self.columns:
            flip_z, flip_y, flip_core = self.flips[j]
            place = self.place
            chunk = place.flipped("yl", flip_y) * 2 + place.flipped("core", flip_core)
            return self.total.at[chunk, zh, place.flipped("zl", flip_z), x]
        count = self.zin.shape[1]
        low = ((zh * 2 + x) * self.chunks + j) * count
        return self.total.at[pl.ds(pl.multiple_of(low, 16), count)]

    def start(self):
        for copies in self.along_x:
            for copy in copies:
                copy.start()

    def pairs(self):
        x, zh = self.place.x, self.place.zh

        def launch(j):
            for copy in self.along_x[j]:
                copy.wait_recv()
            self.zout[j] = (self.part(j, 1 - zh, x)[...].astype(F32) + self.xin[j, 0].astype(F32)).astype(BF16)
            self.along_z[j].start()

        def land(j):
            self.along_z[j].wait_recv()
            total = self.part(j, zh, x)[...].astype(F32) + self.xin[j, 1].astype(F32) + self.zin[j].astype(F32)
            if self.columns:
                self.final[j] = total.astype(BF16)
                self.back[j].start()
            else:
                count = self.zin.shape[1]
                self.final[j * count : (j + 1) * count] = total

        return [(functools.partial(launch, j), functools.partial(land, j)) for j in range(self.chunks)]

    def finish(self):
        if self.columns:
            for copy in self.back[:-1]:
                copy.wait_recv()
            self.back[-1].wait()
        sent = [copy for copies in self.along_x for copy in copies] + self.along_z
        for copy in sent + (self.back[:-1] if self.columns else []):
            copy.wait_send()
        self.deliver(self.landed if self.columns else self.final)


def landing_shapes(total):
    if len(total) == 6:
        rows = total[4:]
        return [((8, 2) + rows, BF16)] + [((8,) + rows, BF16)] * 4
    count = total[0] // 4
    size = 48 if count % 48 == 0 else count
    rows = (size,) + total[1:]
    chunks = (count // size,)
    return [(chunks + (2,) + rows, BF16), (chunks + rows, BF16), (chunks + rows, BF16), ((count,) + total[1:], F32)]


def loop(count, body):
    def step(i, carry):
        body(i)
        return carry

    lax.fori_loop(0, count, step, 0)


def tile(i, width=TILE):
    return pl.ds(pl.multiple_of(i * width, width), width)


def dot(left, right):
    return jnp.dot(left, right, preferred_element_type=F32)


def dot_cols(left, right):
    return lax.dot_general(left, right, (((1,), (1,)), ((), ())), preferred_element_type=F32)


def dot_rows(left, right):
    return lax.dot_general(left, right, (((0,), (0,)), ((), ())), preferred_element_type=F32)


def swap_half(values):
    return pltpu.roll(values, LANES // 2, 1)


class Halo:
    def __init__(self, place, buffer, edge, landing, forward):
        x, zh, count = place.x, place.zh, lax.axis_size("x")
        first, final = x == 0, x == count - 1
        low, high, every = pl.ds(0, 4), pl.ds(4, 4), pl.ds(0, 8)
        lead = (slice(None),) * (len(buffer.shape) - 3)
        step = lax.rem(x + 1, count) if forward else lax.rem(x + count - 1, count)
        if forward:
            within, turn, beyond = jnp.logical_not(final), final, jnp.logical_and(final, zh == 0)
            into, turned, entered = jnp.logical_not(first), first, jnp.logical_and(first, zh == 1)
            sent, landed = low, high
        else:
            within, turn, beyond = jnp.logical_not(first), first, jnp.logical_and(first, zh == 1)
            into, turned, entered = jnp.logical_not(final), final, jnp.logical_and(final, zh == 0)
            sent, landed = high, low

        def push(src, dst, device):
            return place.push(buffer.at[lead + (src, edge)], landing.at[lead + (dst,)], device, False)

        copies = [
            push(every, every, {"x": step}),
            push(sent, landed, {"x": step}),
            push(landed, sent, {"x": step, "zh": 1 - zh}),
        ]
        self.sends = list(zip((within, turn, beyond), copies))
        self.lands = list(zip((into, turned, entered), copies))
        self.unreached = jnp.logical_and(turned, jnp.logical_not(entered))
        self.landing, self.open_end = landing, lead + (sent,)

    def start(self):
        for condition, copy in self.sends:
            pl.when(condition)(copy.start)

        @pl.when(self.unreached)
        def _():
            shape = self.landing.at[self.open_end].shape
            self.landing[self.open_end] = jnp.zeros(shape, self.landing.dtype)

    def wait_recv(self):
        for condition, copy in self.lands:
            pl.when(condition)(copy.wait_recv)

    def wait_send(self):
        for condition, copy in self.sends:
            pl.when(condition)(copy.wait_send)


SAVED = ("conv_whole", "joint", "carried", "mixed", "gated", "ffn_whole", "gate_up", "hidden")
WEIGHTS = ("in_w", "out_w", "both_w", "down_w")


def forms_of(tokens, features, wide, tall, layers):
    channels, units = (-(-rows // LANES) * LANES for rows in tall)
    block = (tokens, features)
    return {
        "in_w": ((features, wide[0]), BF16),
        "both_w": ((features, wide[1]), BF16),
        "out_w": ((tall[0], features), BF16),
        "down_w": ((tall[1], features), BF16),
        "conv_whole": ((8,) + block, BF16),
        "ffn_whole": ((8,) + block, BF16),
        "joint": ((8, tokens, wide[0]), F32),
        "gate_up": ((8, tokens, wide[1]), F32),
        "carried": ((8, tokens + HALO, channels), F32),
        "mixed": ((8, tokens, channels), F32),
        "gated": ((8, tokens, channels), BF16),
        "hidden": ((8, tokens, units), BF16),
        "tall_w": ((units, features), BF16),
        "grad_rows": ((8, tokens, wide[1]), BF16),
        "grad_gated": ((8, tokens, channels), F32),
        "edges": ((2, 8, tokens + HALO, channels), F32),
        "heads": ((layers, 2, 8, HALO, channels), F32),
        "tails": ((layers, 8, HALO, channels), F32),
        "stream": (block, F32),
        "next": (block, BF16),
        "whole": ((2, 8) + block, BF16),
        "part": ((4, 2) + block, BF16),
        "sib": ((4,) + block, BF16),
        "yin": ((2,) + block, BF16),
        "yout": ((2,) + block, BF16),
        "zin": (block, BF16),
        "zout": (block, BF16),
        "grad_in_w": ((4, 2, 2, 2, features // 32, wide[0]), BF16),
        "grad_both_w": ((4, 2, 2, 2, features // 32, wide[1]), BF16),
        "grad_out_w": ((channels, features), BF16),
        "grad_down_w": ((units, features), BF16),
    }


class Pass:
    def __init__(self, place, buffers, pace):
        self.place, self.buffers, self.pace = place, buffers, pace
        self.tokens, self.features = buffers["zin"].shape
        half = self.tokens // HALVES
        self.halves = [pl.ds(h * half, half) for h in range(HALVES)]
        self.chips = ((0, 0), (1, 0), (0, 1), (1, 1))
        self.phases = 0
        self.items, self.queue, self.flying = [], [], []
        self.saving, self.loading = [], {}

    def enter(self, more, barrier_all):
        place = self.place
        barrier = pltpu.get_barrier_semaphore()
        if barrier_all:
            partners = [device for device, _ in every_other(place)]
            expected = len(partners)
        else:
            x, zh, x_size = place.x, place.zh, lax.axis_size("x")
            partners = [place.beside(axis) for axis in ("core", "yl", "zl")] + more
            partners += [{"x": lax.rem(x + 1, x_size)}, {"x": lax.rem(x + x_size - 1, x_size)}]
            at_turn = jnp.logical_or(jnp.logical_and(x == x_size - 1, zh == 0), jnp.logical_and(x == 0, zh == 1))
            across = {"x": jnp.where(x == 0, x_size - 1, 0), "zh": 1 - zh}

            @pl.when(at_turn)
            def _():
                pl.semaphore_signal(barrier, inc=1, device_id=across, device_id_type=MESH)

            expected = len(partners) + jnp.where(at_turn, 1, 0)
        for partner in partners:
            pl.semaphore_signal(barrier, inc=1, device_id=partner, device_id_type=MESH)
        pl.semaphore_wait(barrier, expected)

    def begin(self, items):
        for item in items:
            item.left = len(item.pairs())
            self.queue += [(item,) + pair for pair in item.pairs()]
            self.items.append(item)

    def launch(self, count):
        for item, launch, land in self.queue[:count]:
            launch()
            self.flying.append((item, land))
        del self.queue[:count]

    def land(self, count):
        for item, land in self.flying[:count]:
            land()
            item.left -= 1
        del self.flying[:count]

    def step(self, point):
        fly, count = self.pace[point]
        while len(self.flying) > fly:
            self.land(1)
        self.launch(count)

    def settle(self, items):
        for item in items:
            while any(queued is item for queued, _, _ in self.queue):
                self.launch(1)
            while item.left:
                self.land(1)
            item.finish()
            self.items.remove(item)

    def load(self, name, source, target):
        if target.shape != source.shape:
            rows = target.shape[0] - source.shape[0]
            target[source.shape[0] :] = jnp.zeros((rows,) + target.shape[1:], BF16)
            target = target.at[: source.shape[0]]
        self.loading[name] = self.place.copy(source, target)
        self.loading[name].start()

    def loaded(self, *names):
        for name in names:
            self.loading.pop(name).wait()

    def save(self, source, target):
        self.saving.append(self.place.copy(source, target))
        self.saving[-1].start()

    def saved(self):
        for copy in self.saving:
            copy.wait()
        self.saving = []

    def pair(self, chip):
        return pl.ds(self.place.rank(*chip, 0) - self.place.core, 2)

    def rows_of(self, values):
        return values.reshape(2 * self.tokens, values.shape[-1])

    def blocks_of(self, values):
        return values.reshape(2, self.tokens, values.shape[-1])

    def all_rows(self, values):
        return values.reshape(8 * self.tokens, values.shape[-1])

    def phase(self, mine, first, second, after, before_first=None, before_second=None, between=None, aside=None):
        place, buffers, halves, chips = self.place, self.buffers, self.halves, self.chips
        rank, sent = place.rank, []
        whole = buffers["whole"].at[self.phases % 2]
        self.phases += 1
        part, sib, yin, yout, zin, zout = (buffers[name] for name in ("part", "sib", "yin", "yout", "zin", "zout"))
        to_sibling, to_y, to_z = (place.beside(axis) for axis in ("core", "yl", "zl"))
        own, beside_z, beside_y, corner = (rank(*chip, 0) for chip in chips)

        def push(src, dst, device):
            sent.append(place.push(src, dst, device, False))
            return sent[-1]

        def sends(src, at, device):
            return [push(mine.at[rows] if src is None else src.at[at, rows], whole.at[at, rows], device) for rows in halves]

        def landed(copies):
            for copy in copies:
                copy.wait_recv()

        from_z, from_y, own_to_core = sends(None, own, to_z), sends(None, own, to_y), sends(None, own, to_sibling)
        from_corner = sends(whole, beside_z, to_y)
        z_to_core, y_to_core, corner_to_core = (sends(whole, at, to_sibling) for at in (beside_z, beside_y, corner))
        own_place = place.copy(mine, whole.at[own])
        own_place.start()
        for h in range(HALVES):
            for copies in (from_z, from_y, own_to_core):
                copies[h].start()
        self.step(0)
        if before_first is not None:
            before_first()
        own_place.wait()
        landed(own_to_core)
        first(whole, chips[0])
        for h in range(HALVES):
            from_z[h].wait_recv()
            from_corner[h].start()
            z_to_core[h].start()
        self.step(1)
        for h in range(HALVES):
            from_y[h].wait_recv()
            y_to_core[h].start()
        landed(z_to_core)
        first(whole, chips[1])
        self.step(2)
        landed(y_to_core)
        first(whole, chips[2])
        self.step(3)
        for h in range(HALVES):
            from_corner[h].wait_recv()
            corner_to_core[h].start()
        landed(corner_to_core)
        first(whole, chips[3])
        self.step(4)
        if between is not None:
            between(whole)
        if before_second is not None:
            before_second()

        order = (chips[3], chips[2], chips[1], chips[0])
        sib_copies = [push(part.at[i, 1 - place.core], sib.at[i], to_sibling) for i in range(4)]
        y_copies = [[push(yout.at[i, rows], yin.at[i, rows], to_y) for rows in halves] for i in range(2)]
        z_copies = [push(zout.at[rows], zin.at[rows], to_z) for rows in halves]

        def multiply(i):
            def columns(j):
                part[i, :, :, tile(j)] = self.blocks_of(second(order[i], j).astype(BF16))

            loop(self.features // TILE, columns)
            sib_copies[i].start()

        def chip_sum(i, rows):
            return part[i, place.core, rows].astype(F32) + sib[i, rows].astype(F32)

        def to_y_side(i):
            sib_copies[i].wait_recv()
            for h, rows in enumerate(halves):
                yout[i, rows] = chip_sum(i, rows).astype(BF16)
                y_copies[i][h].start()

        multiply(0)
        multiply(1)
        to_y_side(0)
        self.step(5)
        multiply(2)
        to_y_side(1)
        multiply(3)
        self.step(6)
        sib_copies[2].wait_recv()
        for h, rows in enumerate(halves):
            y_copies[0][h].wait_recv()
            zout[rows] = (chip_sum(2, rows) + yin[0, rows].astype(F32)).astype(BF16)
            z_copies[h].start()
        self.step(7)
        if aside is not None:
            aside(whole)
        self.step(8)
        sib_copies[3].wait_recv()
        for copy in sent:
            copy.wait_send()
        for h, rows in enumerate(halves):
            y_copies[1][h].wait_recv()
            z_copies[h].wait_recv()
            if h == HALVES - 1:
                self.step(9)
            after(h, rows, chip_sum(3, rows) + yin[1, rows].astype(F32) + zin[rows].astype(F32))
        self.step(10)


def c_columns(joint, b, lane):
    if lane == 0:
        return joint[b, :, LANES : 2 * LANES]
    return swap_half(joint[b, :, 3 * LANES : 4 * LANES])


def both_lanes():
    return [(lane, slice(lane, lane + LANES)) for lane in (0, LANES)]


def forward_kernel(plan, *refs):
    refs = list(refs)
    layers, moving, buffer_names = plan["layers"], plan["moving"], plan["buffers"]

    def take(count):
        taken = refs[:count]
        del refs[:count]
        return taken

    (stream_in,) = take(1)
    if moving:
        small, in_proj, gate_in, up_in, out_in, down_in = take(6)
    else:
        gains, taps_ref, keep = take(3)
        weights = [dict(zip(WEIGHTS, take(4))) for _ in range(layers)]
    stream_out, middles, sources = take(1)[0], take(layers), take(layers - 1)
    saves = [dict(zip(SAVED, take(len(SAVED)))) for _ in range(layers)]
    if moving:
        weights = [dict(zip(WEIGHTS, take(4))) for _ in range(layers)]
        gains, taps_ref, keep = take(3)
    buffers = dict(zip(buffer_names, take(len(buffer_names))))
    if moving:
        (spread,) = take(1)
        shards, mine = ([dict(zip(WEIGHTS[::2], take(2))) for _ in range(layers)] for _ in range(2))
        rounds = [dict(zip(WEIGHTS[1::2], take(2))) for _ in range(layers)]
    place = Place(*take(3))
    run = Pass(place, buffers, FORWARD_PACE)
    tokens, features = run.tokens, run.features
    rows_of, blocks_of, pair = run.rows_of, run.blocks_of, run.pair
    joint, carried, mixed, gated = (buffers[name] for name in ("joint", "carried", "mixed", "gated"))
    gate_up, hidden = buffers["gate_up"], buffers["hidden"]
    in_w, out_w, both_w, down_w = (buffers["vmem_" + name] for name in WEIGHTS)
    main = gate_up.shape[2] // (2 * LANES) * LANES
    next_ref = buffers["next"]

    coming, scattered = {}, {}

    def moves(layer, names):
        for name in names:
            own = mine[layer][name] if name in mine[layer] else rounds[layer][name]
            coming[layer, name] = Gather(place, own, weights[layer][name])
            if name in mine[layer]:
                coming[layer, name].ready = functools.partial(landed, layer, name)
            run.begin([coming[layer, name]])

    def cut(layer, name):
        if name == "in_w":
            width = in_proj.shape[2] // 3
            groups = [in_proj.at[layer, :, i * width : (i + 1) * width] for i in range(3)]
        else:
            groups = [gate_in.at[layer], up_in.at[layer]]
        shards_from(groups, shards[layer][name])

    def scatter(layer, name):
        source = shards[layer][name]
        here = mine[layer][name].at[place.yl * 2 + place.core, place.zl]
        copies = [place.push(source.at[place.rank(*flips)], here, place.member(flips)) for flips in FLIPS]
        copies.append(place.copy(source.at[place.rank(0, 0, 0)], here))
        for copy in copies:
            copy.start()
        scattered[layer, name] = copies

    def landed(layer, name):
        copies = scattered.pop((layer, name))
        for copy in copies[:-1]:
            copy.wait_recv()
        copies[-1].wait()

    def parameters():
        owned = features // 32
        for layer in range(layers):
            for i in range(2):
                row = 5 * layer + i
                gains[2 * layer + i] = jnp.concatenate([spread[o, row : row + 1, :owned] for o in range(32)], axis=1)
            rows = pl.ds(5 * layer + 2, 3)
            parts = [
                spread[((place.yl * 2 + place.core) * 2 + zh) * 4 + place.zl * 2 + x, rows, :owned]
                for zh, x in itertools.product(range(2), repeat=2)
            ]
            taps_ref[layer] = jnp.zeros(taps_ref.shape[1:], F32)
            taps_ref[layer, :3, : 4 * owned] = jnp.concatenate(parts, axis=1)
        count = lax.broadcasted_iota(jnp.int32, (tokens, 1), 0)
        for block in range(8):
            zl, others = block // 4, block % 4
            places = (((place.zh * 2 + zl) * 2 + place.x) * tokens + count).astype(F32)
            starts = [spread[others * 8, 15:16, n : n + 1] for n in range(plan["documents"])]

            def segment(where):
                return sum(jnp.where(start <= where, 1.0, 0.0) for start in starts)

            own = segment(places)
            keep[0, block] = jnp.where(segment(places - 1.0) == own, 1.0, 0.0)
            keep[1, block] = jnp.where(segment(places - 2.0) == own, 1.0, 0.0)

    def load(layer, names):
        for name in names:
            if (layer, name) in coming:
                run.settle([coming.pop((layer, name))])
            source, target = weights[layer][name], buffers["vmem_" + name]
            if len(source.shape) == 2:
                run.load(name, source, target)
                continue
            copies = []
            rows = source.shape[-2]
            lead = source.shape[:-2]
            for n, index in enumerate(itertools.product(*(range(size) for size in lead))):
                copies.append(place.copy(source.at[index], target.at[pl.ds(n * rows, rows)]))
                copies[-1].start()
            filled = rows * len(copies)
            if filled < target.shape[0]:
                target[filled:] = jnp.zeros((target.shape[0] - filled, target.shape[1]), BF16)
            run.loading[name] = Several(copies)

    def rounded(values, gain):
        return (values * rms_scale(values) * gain).astype(BF16)

    def conv(layer, stream):
        def before_first():
            load(layer, ("in_w",))
            run.loaded("in_w")

        def first(whole, chip):
            at = pair(chip)

            def columns(j):
                joint[at, :, tile(j)] = blocks_of(dot(rows_of(whole[at]), in_w[:, tile(j)]))

            loop(2, columns)
            joint[at, :, 2 * TILE :] = blocks_of(dot(rows_of(whole[at]), in_w[:, 2 * TILE :]))
            here = pl.ds(HALO, tokens)
            carried[at, here, :LANES] = joint[at, :, :LANES] * joint[at, :, 2 * LANES : 3 * LANES]
            carried[at, here, LANES:] = joint[at, :, 3 * LANES : 4 * LANES] * joint[at, :, 4 * LANES :]

        def between(whole):
            halo = Halo(place, carried, pl.ds(tokens, HALO), buffers["tails"].at[layer], True)
            halo.start()
            run.saved()
            run.save(joint, saves[layer]["joint"])
            run.save(whole, saves[layer]["conv_whole"])
            halo.wait_recv()
            carried[:, :HALO] = buffers["tails"][layer]

            def block(b):
                keep_one, keep_two = keep[0, b], keep[1, b]
                for lane, lanes in both_lanes():
                    result = (
                        taps_ref[layer, 0:1, lanes] * carried[b, HALO - 2 : HALO - 2 + tokens, lanes] * keep_two
                        + taps_ref[layer, 1:2, lanes] * carried[b, HALO - 1 : HALO - 1 + tokens, lanes] * keep_one
                        + taps_ref[layer, 2:3, lanes] * carried[b, HALO : HALO + tokens, lanes]
                    )
                    mixed[b, :, lanes] = result
                    gated[b, :, lanes] = (c_columns(joint, b, lane) * result).astype(BF16)

            loop(8, block)
            halo.wait_send()
            for name in ("carried", "mixed", "gated"):
                run.save(buffers[name], saves[layer][name])

        def second(chip, j):
            return dot(rows_of(gated[pair(chip)]), out_w[:, tile(j)])

        def after(h, rows, total):
            middle = stream[rows] + total
            middles[layer][rows] = middle
            next_ref[rows] = rounded(middle, gains[2 * layer + 1])

        def before_second():
            load(layer, ("out_w",))
            if moving and layer + 1 < layers:
                scatter(layer + 1, "in_w")
            run.loaded("out_w")

        run.phase(next_ref, first, second, after, before_first, before_second, between)

    def ffn(layer):
        def before_first():
            load(layer, ("both_w",))
            run.loaded("both_w")

        def first(whole, chip):
            at = pair(chip)

            def columns(j):
                ups = pl.ds(pl.multiple_of(main + j * TILE, TILE), TILE)
                gate = dot(rows_of(whole[at]), both_w[:, tile(j)])
                up = dot(rows_of(whole[at]), both_w[:, ups])
                gate_up[at, :, tile(j)] = blocks_of(gate)
                gate_up[at, :, ups] = blocks_of(up)
                hidden[at, :, tile(j)] = blocks_of((gate * jax.nn.sigmoid(gate) * up).astype(BF16))

            loop(main // TILE, columns)
            both = dot(rows_of(whole[at]), both_w[:, 2 * main :])
            gate_up[at, :, 2 * main :] = blocks_of(both)
            lane = lax.broadcasted_iota(jnp.int32, both.shape, 1)
            tail = jnp.where(lane < LANES // 2, both * jax.nn.sigmoid(both) * swap_half(both), 0.0)
            hidden[at, :, main:] = blocks_of(tail.astype(BF16))

        def between(whole):
            run.saved()
            run.save(whole, saves[layer]["ffn_whole"])
            run.save(gate_up, saves[layer]["gate_up"])
            run.save(hidden, saves[layer]["hidden"])

        def second(chip, j):
            return dot(rows_of(hidden[pair(chip)]), down_w[:, tile(j)])

        def after(h, rows, total):
            result = middles[layer][rows] + total
            if layer + 1 < layers:
                sources[layer][rows] = result
                next_ref[rows] = rounded(result, gains[2 * layer + 2])
            else:
                stream_out[rows] = result

        def before_second():
            load(layer, ("down_w",))
            if moving and layer + 1 < layers:
                scatter(layer + 1, "both_w")
            run.loaded("down_w")

        run.phase(next_ref, first, second, after, before_first, before_second, between)

    if moving:
        cut(0, "in_w")
        rounds[0]["out_w"][...] = out_in[0].astype(BF16)
        run.enter([], True)
        kept = place.copy(small, spread.at[place.owner()])
        kept.start()
        spreads = [place.push(small, spread.at[place.owner()], device) for device, _ in every_other(place)]
        scatter(0, "in_w")
        for copy in spreads:
            copy.start()
        moves(0, ("out_w", "in_w", "both_w", "down_w"))
        run.launch(1)
        cut(0, "both_w")
        run.launch(8)
        rounds[0]["down_w"][...] = down_in[0].astype(BF16)
        for layer in range(1, layers):
            cut(layer, "in_w")
            cut(layer, "both_w")
            rounds[layer]["out_w"][...] = out_in[layer].astype(BF16)
            rounds[layer]["down_w"][...] = down_in[layer].astype(BF16)
            moves(layer, WEIGHTS)
        kept.wait()
        for copy in spreads:
            copy.wait_recv()
        scatter(0, "both_w")
        parameters()
        next_ref[...] = rounded(stream_in[...], gains[0])
    else:
        next_ref[...] = rounded(stream_in[...], gains[0])
        run.enter([], False)
    for layer in range(layers):
        conv(layer, sources[layer - 1] if layer else stream_in)
        ffn(layer)
    run.saved()
    for copy in place.sent:
        copy.wait_send()


class Several:
    def __init__(self, copies):
        self.copies = copies

    def wait(self):
        for copy in self.copies:
            copy.wait()


def whole_shape(mine):
    return (4, 2, 2, 2) + mine[2:] if len(mine) == 4 else (2, 2) + mine


def forward(stream, given, tall, moving, documents=0):
    tokens, features = stream.shape
    if moving:
        layers, owned = given[1].shape[:2]
        wide = (-(-3 * tall[0] // LANES) * LANES, 2 * tall[1])
    else:
        layers = given[1].shape[0]
        wide = (given[3].shape[1], given[5].shape[1])
    forms = forms_of(tokens, features, wide, tall, layers)
    inside = pl.BlockSpec(memory_space=pltpu.VMEM)
    anywhere = pl.BlockSpec(memory_space=pl.ANY)
    outs = [(forms["stream"], inside)] * (1 + layers + layers - 1)
    outs += [(forms[name], anywhere) for _ in range(layers) for name in SAVED]
    buffers = {name: forms[name] for name in ("joint", "carried", "mixed", "gated", "gate_up", "hidden", "next", "tails")}
    buffers |= {name: forms[name] for name in ("whole", "part", "sib", "yin", "yout", "zin", "zout")}
    buffers |= {"vmem_in_w": forms["in_w"], "vmem_both_w": forms["both_w"]}
    buffers |= {"vmem_out_w": ((forms["gated"][0][2], features), BF16), "vmem_down_w": forms["tall_w"]}
    scratch = [pltpu.VMEM(*form) for form in buffers.values()]
    if moving:
        columns = [(4, 2, owned, width) for width in wide]
        rows = [(owned, features), (tall[1] // 4, features)]
        wholes = [whole_shape(shape) for pair in zip(columns, rows) for shape in pair]
        outs += [((shape, BF16), anywhere) for _ in range(layers) for shape in wholes]
        outs += [(((2 * layers, 1, features), F32), inside), (((layers, HALO, forms["mixed"][0][2]), F32), inside)]
        outs.append((((2, 8, tokens, 1), F32), inside))
        scratch.append(pltpu.VMEM((32,) + given[0].shape, F32))
        scratch += [pltpu.VMEM((8, owned, width), BF16) for _ in range(layers) for width in wide]
        scratch += [pltpu.VMEM(shape, BF16) for _ in range(layers) for shape in columns]
        scratch += [pltpu.VMEM(shape, BF16) for _ in range(layers) for shape in rows]
    plan = {"layers": layers, "moving": moving, "buffers": tuple(buffers), "documents": documents}
    results = pl.pallas_call(
        functools.partial(forward_kernel, plan),
        out_shape=[jax.ShapeDtypeStruct(*form) for form, _ in outs],
        in_specs=[inside] * 7 if moving else [inside] * 4 + [anywhere] * (len(given) - 3),
        out_specs=[spec for _, spec in outs],
        scratch_shapes=scratch + [pltpu.SemaphoreType.DMA((SEMAPHORES,))] * 3,
        compiler_params=pltpu.CompilerParams(
            collective_id=COLLECTIVE_ID["forward"], has_side_effects=True, vmem_limit_bytes=62 << 20
        ),
        name="forward",
    )(stream, *given)
    stream_out, results = results[0], results[1:]
    middles, results = results[:layers], results[layers:]
    sources, results = results[: layers - 1], results[layers - 1 :]
    count = layers * len(SAVED)
    saved, results = results[:count], results[count:]
    if not moving:
        return stream_out, middles, sources, saved, given[3:], given[:3]
    return stream_out, middles, sources, saved, results[:-3], results[-3:]


def backward_kernel(plan, *refs):
    refs = list(refs)
    layers, moving, buffer_names = plan["layers"], plan["moving"], plan["buffers"]

    def take(count):
        taken = refs[:count]
        del refs[:count]
        return taken

    grad_out, gains, taps_ref, keep = take(4)
    middles, sources = take(layers), take(layers)
    weights = [dict(zip(WEIGHTS, take(4))) for _ in range(layers)]
    saves = [dict(zip(SAVED, take(len(SAVED)))) for _ in range(layers)]
    (grad_in,) = take(1)
    if moving:
        small_sum, grad_in_w, grad_out_w, gate_out, up_out, down_out = take(6)
    else:
        gain_out, taps_out = take(2)
        raw = [take(4) for _ in range(layers)]
    buffers = dict(zip(buffer_names, take(len(buffer_names))))
    if moving:
        landing = {name: take(5 if name in ("in_w", "both_w") else 4) for name in WEIGHTS}
        staging, slabs, slabs_in = take(2), *take(2)
        free = dict(zip(("both", "down", "conv"), take(3)))
    place = Place(*take(3))
    run = Pass(place, buffers, BACKWARD_PACE)
    tokens, features = run.tokens, run.features
    rows_of, blocks_of, all_rows, pair = run.rows_of, run.blocks_of, run.all_rows, run.pair
    wide = {"in_w": plan["wide"][0], "both_w": plan["wide"][1]}
    joint, gate_up = buffers["gate_up"].at[:, :, : wide["in_w"]], buffers["gate_up"]
    grad_joint, grad_gate_up = buffers["grad_rows"].at[:, :, : wide["in_w"]], buffers["grad_rows"]
    in_w, both_w = buffers["wide_w"].at[:, : wide["in_w"]], buffers["wide_w"]
    channels, units = buffers["mixed"].shape[2], buffers["hidden"].shape[2]
    out_w, down_w = buffers["tall_w"].at[:channels], buffers["tall_w"]
    gated, hidden = buffers["hidden"].at[:, :, :channels], buffers["hidden"]
    carried, mixed, edges, grad_gated = (buffers[name] for name in ("carried", "mixed", "edges", "grad_gated"))
    kept_whole, next_ref, grad_ref, held = (buffers[name] for name in ("conv_whole", "next", "stream", "held"))
    gain_grads, tap_grads = buffers["gain_grads"], buffers["tap_grads"]
    main = gate_up.shape[2] // (2 * LANES) * LANES

    def load_rows(name, source, target):
        if len(source.shape) == 2:
            run.load(name, source, target)
            return
        rows, lead = source.shape[-2], source.shape[:-2]
        copies = []
        for n, index in enumerate(itertools.product(*(range(size) for size in lead))):
            copies.append(place.copy(source.at[index], target.at[pl.ds(n * rows, rows)]))
            copies[-1].start()
        filled = rows * len(copies)
        if filled < target.shape[0]:
            target[filled:] = jnp.zeros((target.shape[0] - filled, target.shape[1]), BF16)
        run.loading[name] = Several(copies)

    def deliver_columns(outs, layer, views):
        def deliver(landed):
            run.saved()
            shards_to(landed, views)
            for source, out in outs:
                run.save(source, out.at[layer])

        return deliver

    def deliver_rows(out, layer):
        def deliver(final):
            run.save(final, out.at[layer])

        return deliver

    reduced = {"both": 0, "down": 0, "conv": 0}
    under_way = {"both": [], "down": [], "conv": []}

    def reduce(layer, kind, names):
        if not moving:
            for name in names:
                source = buffers["grad_" + name]
                target = raw[layer][WEIGHTS.index(name)]
                run.save(source.at[: target.shape[0]] if source.shape != target.shape else source, target)
            return
        if reduced[kind]:
            pl.semaphore_wait(free[kind], 9)
        reduced[kind] += 1
        run.saved()
        items = []
        for name in names:
            if name == "in_w":
                width = features
                views = [staging[0].at[:, i * width : (i + 1) * width] for i in range(3)]
                deliver = deliver_columns([(staging[0], grad_in_w)], layer, views)
            elif name == "both_w":
                deliver = deliver_columns([(staging[0], gate_out), (staging[1], up_out)], layer, list(staging))
            else:
                deliver = deliver_rows(grad_out_w if name == "out_w" else down_out, layer)
            total = buffers["grad_" + name]
            if name in ("out_w", "down_w"):
                total = total.at[: 4 * landing[name][3].shape[0]]
            items.append(Reduce(place, total, landing[name], deliver))
            items[-1].start()
        run.begin(items)
        under_way[kind] = items

    def settle(kind):
        items, under_way[kind] = under_way[kind], []
        run.settle(items)
        if items and reduced[kind] < layers:
            for device in [place.member(flips) for flips in FLIPS] + [place.beside("zh"), place.beside("x")]:
                pl.semaphore_signal(free[kind], inc=1, device_id=device, device_id_type=MESH)

    def step_back(h, rows, total, stream, gain, row):
        scale = rms_scale(stream)
        gain_grad = jnp.sum(total * stream * scale, axis=0, keepdims=True)
        gain_grads[row : row + 1] = gain_grad if h == 0 else gain_grads[row : row + 1] + gain_grad
        scaled = total * gain
        grad = (
            grad_ref[rows]
            + scale * scaled
            - stream * (scale * scale * scale) * jnp.mean(scaled * stream, axis=-1, keepdims=True)
        )
        grad_ref[rows] = grad
        next_ref[rows] = grad.astype(BF16)
        return grad

    def ffn_back(layer):
        def before_first():
            load_rows("down_w", weights[layer]["down_w"], down_w)
            run.load("gate_up", saves[layer]["gate_up"], gate_up)
            load_rows("both_w", weights[layer]["both_w"], both_w)
            run.load("hidden", saves[layer]["hidden"], hidden)
            run.load("whole", saves[layer]["ffn_whole"], kept_whole)
            run.load("held", middles[layer], held)
            run.loaded("down_w", "gate_up")

        def grads(grad_hidden, gate, up):
            sigmoid = jax.nn.sigmoid(gate)
            return grad_hidden * up * sigmoid * (1.0 + gate * (1.0 - sigmoid)), grad_hidden * gate * sigmoid

        def first(whole, chip):
            at = pair(chip)

            def columns(j):
                ups = pl.ds(pl.multiple_of(main + j * TILE, TILE), TILE)
                grad_hidden = dot_cols(rows_of(whole[at]), down_w[tile(j), :])
                gate, up = (rows_of(gate_up[at, :, lanes]) for lanes in (tile(j), ups))
                grad_gate, grad_up = grads(grad_hidden, gate, up)
                grad_gate_up[at, :, tile(j)] = blocks_of(grad_gate.astype(BF16))
                grad_gate_up[at, :, ups] = blocks_of(grad_up.astype(BF16))

            loop(main // TILE, columns)
            grad_hidden = dot_cols(rows_of(whole[at]), down_w[main:, :])
            both = rows_of(gate_up[at, :, 2 * main :])
            grad_gate, grad_up = grads(grad_hidden, both, swap_half(both))
            grad_gate_up[at, :, 2 * main :] = blocks_of((grad_gate + swap_half(grad_up)).astype(BF16))

        def second(chip, j):
            return dot_cols(rows_of(grad_gate_up[pair(chip)]), both_w[tile(j), :])

        def aside(whole):
            run.loaded("whole", "hidden")
            settle("both")
            settle("down")
            grad_both, grad_down = buffers["grad_both_w"], buffers["grad_down_w"]
            width = features // 4

            def both_rows(c):
                left = all_rows(kept_whole[:, :, tile(c, width)])
                result = dot_rows(left, all_rows(grad_gate_up[...])).astype(BF16)
                grad_both[c] = result.reshape(grad_both.shape[1:])

            def down_rows(j):
                left = all_rows(hidden[:, :, tile(j, LANES)])
                grad_down[tile(j, LANES), :] = dot_rows(left, all_rows(whole[...])).astype(BF16)

            loop(4, both_rows)
            reduce(layer, "both", ("both_w",))
            loop(units // LANES, down_rows)
            reduce(layer, "down", ("down_w",))

        def after(h, rows, total):
            step_back(h, rows, total, held[rows], gains[2 * layer + 1], 2 * layer + 1)

        run.phase(next_ref, first, second, after, before_first, lambda: run.loaded("both_w", "held"), None, aside)

    def conv_back(layer):
        taps = taps_ref.at[layer]

        def before_first():
            load_rows("out_w", weights[layer]["out_w"], out_w)
            for name, target in (("joint", joint), ("carried", carried), ("mixed", mixed)):
                run.load(name, saves[layer][name], target)
            load_rows("in_w", weights[layer]["in_w"], in_w)
            run.load("gated", saves[layer]["gated"], gated)
            run.load("whole", saves[layer]["conv_whole"], kept_whole)
            run.load("held", sources[layer], held)
            run.loaded("out_w")

        def first(whole, chip):
            at = pair(chip)
            grad_gated[at] = blocks_of(dot_cols(rows_of(whole[at]), out_w[...]))

        def between(whole):
            run.loaded("joint", "carried", "mixed")
            tap_grads[layer] = jnp.zeros(tap_grads.shape[1:], F32)

            def block(b):
                keep_one, keep_two = keep[0, b], keep[1, b]
                for lane, lanes in both_lanes():
                    grad_value = grad_gated[b, :, lanes]
                    grad_mixed = grad_value * c_columns(joint, b, lane)
                    first_tap, second_tap = grad_mixed * keep_two, grad_mixed * keep_one
                    edges[0, b, :tokens, lanes] = second_tap * taps[1:2, lanes]
                    edges[1, b, :tokens, lanes] = first_tap * taps[0:1, lanes]
                    mixed[b, :, lanes] = grad_value * mixed[b, :, lanes]
                    grad_gated[b, :, lanes] = grad_mixed * taps[2:3, lanes]
                    for row, grad, back_by in ((0, first_tap, 2), (1, second_tap, 1), (2, grad_mixed, 0)):
                        tap_in = carried[b, HALO - back_by : HALO - back_by + tokens, lanes]
                        tap_grads[layer, row : row + 1, lanes] += jnp.sum(grad * tap_in, axis=0, keepdims=True)

            loop(8, block)
            halo = Halo(place, edges, pl.ds(0, HALO), buffers["heads"].at[layer], False)
            halo.start()
            halo.wait_recv()
            edges[:, :, tokens:] = buffers["heads"][layer]

            def block_after(b):
                for lane, lanes in both_lanes():
                    grad_carried = (
                        grad_gated[b, :, lanes] + edges[0, b, 1 : 1 + tokens, lanes] + edges[1, b, 2 : 2 + tokens, lanes]
                    )
                    grad_c = mixed[b, :, lanes]
                    if lane == 0:
                        grad_joint[b, :, :LANES] = (grad_carried * joint[b, :, 2 * LANES : 3 * LANES]).astype(BF16)
                        grad_joint[b, :, LANES : 2 * LANES] = grad_c.astype(BF16)
                        grad_joint[b, :, 2 * LANES : 3 * LANES] = (grad_carried * joint[b, :, :LANES]).astype(BF16)
                    else:
                        grad_b = grad_carried * joint[b, :, 4 * LANES :]
                        grad_joint[b, :, 3 * LANES : 4 * LANES] = (grad_b + swap_half(grad_c)).astype(BF16)
                        grad_joint[b, :, 4 * LANES :] = (grad_carried * joint[b, :, 3 * LANES : 4 * LANES]).astype(BF16)

            loop(8, block_after)
            halo.wait_send()
            if layer == 0:
                gradients(whole)

        def second(chip, j):
            return dot_cols(rows_of(grad_joint[pair(chip)]), in_w[tile(j), :])

        def gradients(whole):
            run.loaded("whole", "gated")
            settle("conv")
            grad_in_rows, grad_out_rows = buffers["grad_in_w"], buffers["grad_out_w"]
            width = features // 4

            def in_rows(c):
                left = all_rows(kept_whole[:, :, tile(c, width)])
                result = dot_rows(left, all_rows(grad_joint[...])).astype(BF16)
                grad_in_rows[c] = result.reshape(grad_in_rows.shape[1:])

            def out_rows(j):
                left = all_rows(gated[:, :, tile(j, LANES)])
                grad_out_rows[tile(j, LANES), :] = dot_rows(left, all_rows(whole[...])).astype(BF16)

            loop(4, in_rows)
            loop(channels // LANES, out_rows)
            reduce(layer, "conv", ("in_w", "out_w"))

        def after(h, rows, total):
            grad = step_back(h, rows, total, held[rows], gains[2 * layer], 2 * layer)
            if layer == 0:
                grad_in[rows] = grad

        run.phase(
            next_ref, first, second, after, before_first, lambda: run.loaded("in_w", "held"), between, gradients if layer else None
        )

    grad_ref[...] = grad_out[...]
    next_ref[...] = grad_out[...].astype(BF16)
    run.enter([], moving)
    for layer in reversed(range(layers)):
        ffn_back(layer)
        conv_back(layer)
    if moving:
        run.launch(len(run.queue))
        owned = features // 32
        slabs[...] = jnp.zeros(slabs.shape, F32)
        for owner in range(32):
            slabs[owner, : 2 * layers, :owned] = gain_grads[:, owner * owned : (owner + 1) * owned]
        for layer in range(layers):
            row = 2 * layers + 3 * layer
            for zh, x in itertools.product(range(2), repeat=2):
                owner = ((place.yl * 2 + place.core) * 2 + zh) * 4 + place.zl * 2 + x
                low = (zh * 2 + x) * owned
                slabs[owner, row : row + 3, :owned] = tap_grads[layer, :3, low : low + owned]
        copies = []
        for i, (device, flips) in enumerate(every_other(place)):
            copies.append(place.push(slabs.at[place.owner(flips)], slabs_in.at[i], device))
            copies[-1].start()
        for kind in ("both", "down", "conv"):
            settle(kind)
        for copy in copies:
            copy.wait_recv()
        small_sum[...] = slabs[place.owner()] + jnp.sum(slabs_in[...], axis=0)
    else:
        gain_out[...] = gain_grads[...]
        taps_out[...] = tap_grads[...]
    run.saved()
    for copy in place.sent:
        copy.wait_send()


def backward(grad_out, gains, taps, keep, middles, sources, weights, saved, tall, moving):
    tokens, features = grad_out.shape
    layers = taps.shape[0]
    wide = (weights[0][0].shape[-1], weights[0][2].shape[-1])
    forms = forms_of(tokens, features, wide, tall, layers)
    inside = pl.BlockSpec(memory_space=pltpu.VMEM)
    anywhere = pl.BlockSpec(memory_space=pl.ANY)
    owned = features // 32
    outs = [(forms["stream"], inside)]
    if moving:
        outs.append((((16, LANES), F32), inside))
        shapes = ((owned, 3 * features), (owned, features), (owned, 4 * tall[1] * 2), (owned, 4 * tall[1] * 2), (tall[1] // 4, features))
        outs += [(((layers,) + shape, F32), anywhere) for shape in shapes]
    else:
        outs.append((((2 * layers, features), F32), inside))
        outs.append((((layers, HALO, forms["mixed"][0][2]), F32), inside))
        for _ in range(layers):
            for name in WEIGHTS:
                shape = forms["grad_" + name][0]
                outs.append((((tall[0] if name == "out_w" else tall[1], features) if len(shape) == 2 else shape, BF16), anywhere))
    names = ("conv_whole", "gate_up", "carried", "mixed", "hidden", "grad_rows", "grad_gated", "edges", "heads", "tall_w")
    names += ("next", "stream", "whole", "part", "sib", "yin", "yout", "zin", "zout")
    names += ("grad_in_w", "grad_both_w", "grad_out_w", "grad_down_w")
    buffers = {name: forms[name] for name in names}
    buffers["wide_w"], buffers["held"] = forms["both_w"], forms["stream"]
    buffers["gain_grads"] = ((2 * layers, features), F32)
    buffers["tap_grads"] = ((layers, HALO, forms["mixed"][0][2]), F32)
    scratch = [pltpu.VMEM(*form) for form in buffers.values()]
    if moving:
        for name in WEIGHTS:
            shape = forms["grad_" + name][0]
            if len(shape) == 2:
                shape = (tall[0] if name == "out_w" else tall[1], features)
            scratch += [pltpu.VMEM(*form) for form in landing_shapes(shape)]
        scratch += [pltpu.VMEM((owned, 3 * features), F32)] * 2
        scratch += [pltpu.VMEM((32, 16, LANES), F32), pltpu.VMEM((31, 16, LANES), F32)]
        scratch += [pltpu.SemaphoreType.REGULAR] * 3
    operands = list(middles) + list(sources) + [array for group in weights for array in group] + list(saved)
    plan = {"layers": layers, "moving": moving, "buffers": tuple(buffers), "wide": wide}
    return pl.pallas_call(
        functools.partial(backward_kernel, plan),
        out_shape=[jax.ShapeDtypeStruct(*form) for form, _ in outs],
        in_specs=[inside] * 4 + [anywhere] * len(operands),
        out_specs=[spec for _, spec in outs],
        scratch_shapes=scratch + [pltpu.SemaphoreType.DMA((SEMAPHORES,))] * 3,
        compiler_params=pltpu.CompilerParams(
            collective_id=COLLECTIVE_ID["backward"], has_side_effects=True, vmem_limit_bytes=63 << 20
        ),
        name="backward",
    )(grad_out, gains, taps, keep, *operands)


def sizes_of(axes):
    return tuple(lax.axis_size(axis) for axis in axes)


def split_owners(array, dim):
    owners = sizes_of(OWNERS)
    count = 1
    for size in owners:
        count *= size
    shape = array.shape
    return array.reshape(shape[:dim] + owners + (shape[dim] // count,) + shape[dim + 1 :])


def column_shards(weights):
    rows = weights[0].shape[0]
    mains, rests = [], []
    for weight in weights:
        parts = split_owners(weight, 1).transpose(5, 2, 3, 0, 1, 4, 6, 7).reshape(8, rows, -1)
        main = parts.shape[2] // LANES * LANES
        mains.append(parts[:, :, :main])
        rests.append(parts[:, :, main:])
    shards = jnp.concatenate(mains + rests, axis=2)
    return jnp.pad(shards, ((0, 0), (0, 0), (0, -shards.shape[2] % LANES)))


def column_whole(shards, groups, width):
    rows = shards.shape[1]
    yh, yl, core, zh, zl, x = sizes_of(OWNERS)
    wholes = []
    for group in range(groups):
        part = jnp.concatenate(
            [shards[..., a:b] for a, b in pieces_of(groups, width, group, 0, width)], axis=-1
        ).reshape(zl, yl, core, rows, yh, zh, x, -1)
        wholes.append(part.transpose(3, 4, 1, 2, 5, 0, 6, 7).reshape(rows, -1))
    return wholes


def gather_columns(shards):
    mine = lax.all_to_all(shards, TP, split_axis=0, concat_axis=0, tiled=True)
    whole = lax.all_gather(mine, DP, axis=0, tiled=False)
    yh, yl, core, zh, zl, x = sizes_of(OWNERS)
    rows, columns = shards.shape[1:]
    whole = whole.reshape(yh, zh, x, zl, yl, core, rows, columns)
    return whole.transpose(0, 4, 5, 1, 3, 2, 6, 7).reshape(-1, columns)


def scatter_columns(total):
    yh, yl, core, zh, zl, x = sizes_of(OWNERS)
    columns = total.shape[1]
    parts = split_owners(total, 0).transpose(0, 3, 5, 4, 1, 2, 6, 7)
    parts = parts.reshape(yh * zh * x, -1, columns)
    mine = lax.psum_scatter(parts, DP, scatter_dimension=0, tiled=False)
    mine = mine.reshape(8, -1, columns)
    return lax.all_to_all(mine, TP, split_axis=0, concat_axis=0, tiled=True)


def tap_masks(starts, token_count):
    zh, x, x_size = lax.axis_index("zh"), lax.axis_index("x"), lax.axis_size("x")
    blocks = (zh * 2 + jnp.arange(2, dtype=jnp.int32)) * x_size + x
    places = blocks[:, None] * token_count + jnp.arange(token_count, dtype=jnp.int32)

    def segment_of(where):
        return jnp.sum((starts[None, :, None, :] <= where[:, None, :, None]).astype(jnp.int32), axis=3)

    own_segment = segment_of(places)
    keep_one = (segment_of(places - 1) == own_segment).astype(F32)
    keep_two = (segment_of(places - 2) == own_segment).astype(F32)
    return keep_one.reshape(8, token_count, 1), keep_two.reshape(8, token_count, 1)


def local(stream_in, doc_starts, norm_mix, in_proj, conv_taps, out_proj, norm_ffn, w_gate, w_up, w_down, grad_out):
    _, token_count, features = stream_in.shape
    layers = norm_mix.shape[0]
    own_kernels = sizes_of(DP) == (1, 2, 2)
    stream = stream_in.reshape(-1, features)
    grad_stream = grad_out.reshape(-1, features)
    small = jnp.concatenate([norm_mix[:, None], norm_ffn[:, None], conv_taps.transpose(0, 2, 1)], axis=1)
    small = small.astype(BF16).astype(F32)
    owned = small.shape[2]
    tall = (features // 8, w_gate.shape[2] // 8)
    if own_kernels:
        packed = jnp.zeros((16, LANES), F32).at[: 5 * layers, :owned].set(small.reshape(-1, owned))
        packed = packed.at[15, : doc_starts.shape[1]].set(doc_starts[0].astype(F32))
        given = (packed, in_proj, w_gate, w_up, out_proj, w_down)
    else:
        starts = lax.all_gather(doc_starts, ("yl", "core"), axis=0, tiled=True)
        small = small.astype(BF16)
        gains = lax.all_gather(small[:, :2], OWNERS, axis=2, tiled=True).astype(F32).reshape(2 * layers, 1, features)
        taps = lax.all_gather(small[:, 2:], DP, axis=2, tiled=True).astype(F32)
        taps = jnp.pad(taps, ((0, 0), (0, HALO - 3), (0, -taps.shape[2] % LANES)))
        given = (gains, taps, jnp.stack(tap_masks(starts, token_count)))
        for layer in range(layers):
            in_w = gather_columns(column_shards(jnp.split(in_proj[layer].astype(BF16), 3, axis=1)))
            both_w = gather_columns(column_shards([w_gate[layer].astype(BF16), w_up[layer].astype(BF16)]))
            out_w = lax.all_gather(out_proj[layer].astype(BF16), DP, axis=0, tiled=True)
            down_w = lax.all_gather(w_down[layer].astype(BF16), DP, axis=0, tiled=True)
            given += (in_w, out_w, both_w, down_w)

    stream_out, middles, sources, saved, weights, params = forward(stream, given, tall, own_kernels, doc_starts.shape[1])
    weights = [tuple(weights[4 * layer : 4 * layer + 4]) for layer in range(layers)]
    grad_in, *results = backward(
        grad_stream, *params, middles, [stream] + list(sources), weights, saved, tall, own_kernels
    )
    if own_kernels:
        small_sums, grad_in_w, grad_out_w, grad_gate, grad_up, grad_down = results
        small_sums = small_sums[:, :owned]
        gain_grads = small_sums[: 2 * layers].reshape(layers, 2, owned)
        tap_grads = small_sums[2 * layers : 5 * layers].reshape(layers, 3, owned)
    else:
        gain_grads, tap_grads, *raw = results
        gain_grads = lax.psum_scatter(gain_grads, OWNERS, scatter_dimension=1, tiled=True).reshape(layers, 2, -1)
        tap_grads = lax.psum_scatter(tap_grads[:, :3, : tall[0]], DP, scatter_dimension=2, tiled=True)
        sums = []
        for layer in range(layers):
            grad_in_w, grad_out_w, grad_both, grad_down = raw[4 * layer : 4 * layer + 4]
            columns = [
                column_whole(scatter_columns(grad.reshape(features, -1)).astype(F32), groups, width)
                for grad, groups, width in ((grad_in_w, 3, tall[0]), (grad_both, 2, tall[1]))
            ]
            rows = [
                lax.psum_scatter(grad, DP, scatter_dimension=0, tiled=True).astype(F32) for grad in (grad_out_w, grad_down)
            ]
            sums.append((jnp.concatenate(columns[0], axis=1), rows[0], *columns[1], rows[1]))
        grad_in_w, grad_out_w, grad_gate, grad_up, grad_down = (jnp.stack(parts) for parts in zip(*sums))
    return (
        stream_out[None],
        grad_in[None],
        gain_grads[:, 0],
        grad_in_w,
        tap_grads.transpose(0, 2, 1),
        grad_out_w,
        gain_grads[:, 1],
        grad_gate,
        grad_up,
        grad_down,
    )


def solution(mesh):
    dp, seq = mesh.shape["dp"], mesh.shape["seq"]
    side = dp // 2
    split = Mesh(mesh.devices.reshape(side // 2, 2, 2, seq // side // 2, 2, side), OWNERS)
    token = P(ROW_AXES, SEQ_AXES, None)
    vector = P(None, OWNERS)
    matrix = P(None, OWNERS, None)
    return jax.shard_map(
        local,
        mesh=split,
        in_specs=(token, P(ROW_AXES, None), vector, matrix, matrix, matrix, vector, matrix, matrix, matrix, token),
        out_specs=(token, token, vector, matrix, matrix, matrix, vector, matrix, matrix, matrix),
        check_vma=False,
    )
```
